32 devices in a mesh: pipe: 2 (over x), tensor: 4 (over y, core), dp: 4 (over z).
Axes of the slice: x: 2, y: 2, z: 4, core: 2. Of those that a mesh axis runs over, the one named last changes fastest.
Arguments:
- tokens: bfloat16 [8, 1024, 768], P('dp', 'tensor'), may hold values from -6 to 6
- segment_ids: int32 [8, 1024], P('dp'), may hold values from 0 to 3, never falling along the last dimension, each value on 1 to 512 neighbouring positions
- pad_mask: int32 [8, 1024], P('dp'), may hold values from 0 to 1, as said below
- block_perm: int32 [2, 12, 2], P('pipe', 'tensor'), may hold values from 0 to 1, each once within a row
- qkv_weight: bfloat16 [2, 3, 768, 768], P('pipe', None, None, 'tensor'), may hold values from -0.21875 to 0.21875
- qkv_bias: bfloat16 [2, 2, 768], P('pipe', None, 'tensor'), may hold values from -2 to 2
- out_weight: bfloat16 [2, 768, 768], P('pipe', 'tensor'), may hold values from -1.75 to 1.75
- up_weight: bfloat16 [2, 768, 3072], P('pipe', None, 'tensor'), may hold values from -0.21875 to 0.21875
- up_bias: bfloat16 [2, 3072], P('pipe', 'tensor'), may hold values from -3 to 3
- down_weight: bfloat16 [2, 3072, 768], P('pipe', 'tensor'), may hold values from -0.109375 to 0.109375
- norm_gain: float32 [2, 2, 768], P('pipe'), may hold values from 0.5 to 1.5
- shift_bias: float32 [2, 4, 768], P('pipe'), may hold values from -3 to 3
- cotangent: bfloat16 [8, 1024, 768], P('dp', 'tensor'), may hold values from -6 to 6
Outputs:
- layer_out: bfloat16 [2, 8, 1024, 768], P('pipe', 'dp', 'tensor')
- input_grad: bfloat16 [2, 8, 1024, 768], P('pipe', 'dp', 'tensor')
- grad_qkv_weight: float32 [2, 3, 768, 768], P('pipe', None, None, 'tensor')
- grad_qkv_bias: float32 [2, 2, 768], P('pipe', None, 'tensor')
- grad_out_weight: float32 [2, 768, 768], P('pipe', 'tensor')
- grad_up_weight: float32 [2, 768, 3072], P('pipe', None, 'tensor')
- grad_up_bias: float32 [2, 3072], P('pipe', 'tensor')
- grad_down_weight: float32 [2, 3072, 768], P('pipe', 'tensor')
- grad_norm_gain: float32 [2, 2, 768], P('pipe')
- grad_shift_bias: float32 [2, 4, 768], P('pipe')
The draws below stay inside these ranges and needn't reach their ends.
Inputs may be any that keep to these rules, and one draw needn't show every extreme that they name: In each sequence the ones of pad_mask form a prefix.
All inputs are finite; a program needn't handle non-finite values.
Results may differ from the reference program's by a relative error of at most 0.018.
Values may be sent and summed in bfloat16 or wider, within the bound.
No kernel may reach another device: no remote copies, remote signals or barrier semaphores. Data moves between devices by JAX's collectives and lax.ppermute only.
A program may use at most 192 MiB of HBM per device.

```python
import math
import jax
import jax.numpy as jnp
import numpy as np
from jax import lax

D = 768
HEADS = 12
FF = 3072
NB = 2
LEN = 1024
SEQS = 8


def draw_pad_mask(key, part):
    key = jax.random.fold_in(key, 7)
    kept_len = LEN - jax.random.randint(key, (SEQS, 1), 0, LEN // 4 + 1)
    return (jnp.arange(LEN, dtype=jnp.int32)[None, :] < kept_len).astype(jnp.int32)


def level_of(rng, dims, split, smallest, top_value):
    def one(position, shards_of):
        heights = jax.random.uniform(jax.random.fold_in(jax.random.fold_in(rng, 6), position), (shards_of,), jnp.float32, smallest / len(split), top_value / len(split))
        return jnp.repeat(jnp.exp(heights), dims[position] // shards_of).reshape((-1,) + (1,) * (len(dims) - position - 1))

    factor_of = one(*split[0])
    for cut in split[1:]:
        factor_of = factor_of * one(*cut)
    return factor_of


def split_up(count, total, limit, skew):
    portions = [(1 << 20) // math.isqrt(rank ** skew) + 1 for rank in range(2, count + 1)]
    rest, given = total - limit - (count - 1), [1] * (count - 1)
    while rest > 0:
        free = [i for i in range(count - 1) if given[i] < limit]
        mass, budget = sum([portions[i] for i in free]), rest
        for i in free:
            more = min(limit - given[i], max(1, budget * portions[i] // mass), rest)
            given[i] = given[i] + more
            rest = rest - more
    return np.array([limit] + given)


def uneven(own_key, number_of, total, most, skew):
    if number_of == 2:
        one = jax.random.randint(own_key, (), max(1, total - most), min(most, total - 1) + 1)
        return jnp.stack([one, total - one])
    sizes = jnp.asarray(split_up(number_of, total, most, skew), jnp.int32)
    couples = (number_of - 1) // 2
    giver, receiver = sizes[1:1 + 2 * couples:2], sizes[2:2 + 2 * couples:2]
    room = jnp.minimum(giver - 1, most - receiver)
    shifted = jax.random.randint(jax.random.fold_in(own_key, 1), (couples,), 0, 1 << 20) % (room + 1)
    sizes = sizes.at[1:1 + 2 * couples:2].set(giver - shifted).at[2:2 + 2 * couples:2].set(receiver + shifted)
    return sizes[jax.random.permutation(jax.random.fold_in(own_key, 2), number_of)]


def noise(own_key, dims, spread, most, split=(), kind=jnp.bfloat16):
    loudness = level_of(own_key, dims, split, -0.22, 0.18) if split else 1.0
    drawn = jax.random.normal(own_key, dims, jnp.float32) * spread * loudness
    return jnp.minimum(jnp.maximum(drawn, -most), most).astype(kind)


def setup_inputs(seed: int = 0) -> dict:
    splits = jax.random.split(jax.random.key(seed), 14)
    tokens = noise(splits[0], (SEQS, LEN, D), 1.0, 6.0, ((0, 4), (1, 4)))
    segment_ids = jax.vmap(lambda own: jnp.searchsorted(jnp.cumsum(uneven(own, 4, LEN, LEN // 2, 0)), jnp.arange(LEN), side="right"))(jax.random.split(splits[1], SEQS)).reshape((SEQS, LEN)).astype(jnp.int32)
    pad_mask = draw_pad_mask(jax.random.fold_in(splits[13], 71), 0)
    block_perm = jax.vmap(lambda own: jax.random.permutation(own, NB))(jax.random.split(splits[3], 2 * HEADS)).reshape((2, HEADS, NB)).astype(jnp.int32)
    qkv_weight = noise(splits[4], (2, 3, D, D), D ** -0.5, 0.21875, ((0, 2), (3, 4)))
    qkv_bias = noise(splits[5], (2, 2, D), 0.3, 2.0, ((0, 2), (2, 4)))
    out_weight = noise(splits[6], (2, D, D), (D // 64) ** -0.5, 1.75, ((0, 2), (1, 4)))
    up_weight = noise(splits[7], (2, D, FF), D ** -0.5, 0.21875, ((0, 2), (2, 4)))
    up_bias = noise(splits[8], (2, FF), 0.5, 3.0, ((0, 2), (1, 4)))
    down_weight = noise(splits[9], (2, FF, D), FF ** -0.5, 0.109375, ((0, 2), (1, 4)))
    norm_gain = jnp.clip(1.0 + 0.1 * jax.random.normal(splits[10], (2, 2, D), jnp.float32), 0.5, 1.5)
    shift_bias = noise(splits[11], (2, 4, D), 0.5, 3.0, ((0, 2),), jnp.float32)
    cotangent = noise(splits[12], (SEQS, LEN, D), 1.0, 6.0, ((0, 4), (1, 4)))
    return {"tokens": tokens, "segment_ids": segment_ids, "pad_mask": pad_mask, "block_perm": block_perm, "qkv_weight": qkv_weight, "qkv_bias": qkv_bias, "out_weight": out_weight, "up_weight": up_weight, "up_bias": up_bias, "down_weight": down_weight, "norm_gain": norm_gain, "shift_bias": shift_bias, "cotangent": cotangent}


NORM_EPSILON_TERM = 1e-06
MASKED = -1e+30

@jax.custom_vjp
def low(v):
    return lax.optimization_barrier(v.astype(jnp.bfloat16)).astype(jnp.float32)

@jax.custom_vjp
def low_back(v):
    return v

def low_keep(v):
    return (low(v), None)

def low_pass(kept, grad):
    return (grad,)

def back_keep(v):
    return (v, None)

def back_low(kept, grad):
    return (low(grad),)
low.defvjp(low_keep, low_pass)
low_back.defvjp(back_keep, back_low)

def matmul(left, right):
    return jnp.dot(left, right, precision=lax.Precision.HIGHEST)

def norm_rows(resid, gain, shift):
    centred = resid - lax.optimization_barrier(jnp.mean(resid, axis=-1, keepdims=True))
    return centred * lax.rsqrt(lax.optimization_barrier(jnp.mean(centred * centred, axis=-1, keepdims=True)) + NORM_EPSILON_TERM) * gain + shift

def layer(x_in, w_qkv, b_qkv, w_out, w_up, b_up, w_down, gains, shifts, block_order, seg_row, pad_row):
    rows_in = low_back(x_in)
    query = low(low_back(matmul(rows_in, w_qkv[0]) + b_qkv[0]))
    keys = low(low_back(matmul(rows_in, w_qkv[1])))
    values = low(low_back(matmul(rows_in, w_qkv[2]) + b_qkv[1]))
    length, width = rows_in.shape
    blocks = block_order.shape[1]
    head_count = block_order.shape[0]
    head_size = width // head_count
    block_len = length // blocks
    chosen_blocks_list = block_order[:, :, None] == jnp.arange(blocks, dtype=jnp.int32)[None, None, :]
    chosen_f = chosen_blocks_list.astype(jnp.float32)
    seg_blocks = seg_row.reshape(blocks, block_len)
    pad_blocks = pad_row.reshape(blocks, block_len)
    seg_keys = lax.optimization_barrier(jnp.sum(jnp.where(chosen_blocks_list[..., None], seg_blocks[None, None], 0), axis=2))
    pad_keys = lax.optimization_barrier(jnp.sum(jnp.where(chosen_blocks_list[..., None], pad_blocks[None, None], 0), axis=2))
    allowed = (seg_blocks[None, :, :, None] == seg_keys[:, :, None, :]) & (pad_keys[:, :, None, :] == 1)
    query4 = query.reshape(blocks, block_len, head_count, head_size)
    keys4 = keys.reshape(blocks, block_len, head_count, head_size)
    values4 = values.reshape(blocks, block_len, head_count, head_size)
    keys_sel = jnp.einsum('hij,jbhe->hibe', chosen_f, keys4, precision=lax.Precision.HIGHEST)
    values_sel = jnp.einsum('hij,jbhe->hibe', chosen_f, values4, precision=lax.Precision.HIGHEST)
    raw = jnp.einsum('iahe,hibe->hiab', query4, keys_sel, precision=lax.Precision.HIGHEST) * head_size ** (-0.5)
    scores = jnp.where(allowed, low_back(raw), MASKED)
    ceiling = jnp.maximum(lax.optimization_barrier(jnp.max(scores, axis=-1, keepdims=True)), 0.0)
    weights = jnp.where(allowed, jnp.exp(scores - ceiling), 0.0)
    total = jnp.exp(-ceiling) + lax.optimization_barrier(jnp.sum(weights, axis=-1, keepdims=True))
    probs = low(weights / total)
    mixed = jnp.einsum('hiab,hibe->iahe', probs, values_sel, precision=lax.Precision.HIGHEST)
    attn = low(low_back(mixed.reshape(length, width)))
    resid1 = rows_in + low_back(matmul(attn, w_out)) + shifts[0]
    hidden = norm_rows(resid1, gains[0], shifts[1])
    pre = low_back(matmul(low(hidden), w_up) + b_up)
    act = low(jax.nn.gelu(pre, approximate=False))
    resid2 = hidden + low_back(matmul(act, w_down)) + shifts[2]
    return norm_rows(resid2, gains[1], shifts[3])

def reference(tokens, segment_ids, pad_mask, block_perm, qkv_weight, qkv_bias, out_weight, up_weight, up_bias, down_weight, norm_gain, shift_bias, cotangent):
    params = tuple((item.astype(jnp.float32) for item in (qkv_weight, qkv_bias, out_weight, up_weight, up_bias, down_weight, norm_gain, shift_bias)))

    def one_sequence(totals, inputs):
        rows, seg_row, pad_row, cotangent_rows = inputs

        def both_layers(rows_in, offset, *weights):
            first = low(layer(rows_in, *[item[0] for item in weights], block_perm[0], seg_row, pad_row))
            second = layer(first + offset, *[item[1] for item in weights], block_perm[1], seg_row, pad_row)
            return (second, first)
        start = rows.astype(jnp.float32)
        second, backward, first = jax.vjp(both_layers, start, jnp.zeros_like(start), *params, has_aux=True)
        grads = backward(cotangent_rows.astype(jnp.float32))
        totals = tuple((total + grad for total, grad in zip(totals, grads[2:])))
        return (totals, (first.astype(jnp.bfloat16), second.astype(jnp.bfloat16), grads[0].astype(jnp.bfloat16), grads[1].astype(jnp.bfloat16)))
    zeros = tuple((jnp.zeros_like(item) for item in params))
    totals, outputs = lax.scan(one_sequence, zeros, (tokens, segment_ids, pad_mask, cotangent))
    first, second, grad_first, grad_second = outputs
    layer_out = jnp.stack([first, second])
    input_grad = jnp.stack([grad_first, grad_second])
    return (layer_out, input_grad, totals[0], totals[1], totals[2], totals[3], totals[4], totals[5], totals[6], totals[7])
```

```python
import jax
import jax.numpy as jnp
from jax import lax
from jax.sharding import PartitionSpec as P

HEAD_DIM = 64
NORM_EPSILON_TERM = 1e-06
MASKED = -1e30
BF16 = jnp.bfloat16
F32 = jnp.float32


def swap(value, axis, bit):
    count = lax.axis_size(axis)
    return lax.ppermute(value, axis, [(source, source ^ bit) for source in range(count)])


def core_swap(value):
    return swap(value, "tensor", 1)


def chip_swap(value):
    return swap(value, "tensor", 2)


def gather_rows(rows):
    rows = lax.optimization_barrier(rows)
    far = chip_swap(rows)
    near = core_swap(rows)
    far_near = core_swap(far)
    return jnp.concatenate([rows, near, far, far_near], axis=0)


def scatter_rows(partial):
    quarter = partial.shape[0] // 4
    blocks = [partial[r * quarter : (r + 1) * quarter] for r in range(4)]
    near_far = core_swap(blocks[3].astype(BF16))
    near = core_swap(blocks[1].astype(BF16))
    far_sum = blocks[2] + near_far.astype(F32)
    far = chip_swap(far_sum.astype(BF16))
    return blocks[0] + near.astype(F32) + far.astype(F32)


def norm_forward(resid, gain, shift):
    centred = resid - jnp.mean(resid, axis=-1, keepdims=True)
    inverse = lax.rsqrt(jnp.mean(centred * centred, axis=-1, keepdims=True) + NORM_EPSILON_TERM)
    normed = centred * inverse
    return (normed * gain + shift, normed, inverse)


def norm_backward(upstream, normed, inverse, gain):
    scaled = upstream * gain
    inner = (
        scaled
        - jnp.mean(scaled, axis=-1, keepdims=True)
        - normed * jnp.mean(scaled * normed, axis=-1, keepdims=True)
    )
    return (inverse * inner, jnp.sum(upstream * normed, axis=0), jnp.sum(upstream, axis=0))


def gelu_exact(values):
    return jax.nn.gelu(values, approximate=False)


def pick(blocks_swapped, tensor):
    return jnp.where(blocks_swapped[:, None, None, None], tensor[:, ::-1], tensor)


def split_heads(matrix):
    rows, width = matrix.shape
    heads = width // HEAD_DIM
    return matrix.reshape(2, rows // 2, heads, HEAD_DIM).transpose(2, 0, 1, 3)


def join_heads(tensor):
    heads, blocks, rows, _ = tensor.shape
    return tensor.transpose(1, 2, 0, 3).reshape(blocks * rows, heads * HEAD_DIM)


def dot(left, right):
    return jnp.dot(left, right, preferred_element_type=F32)


def dot_tn(left, right):
    return lax.dot_general(left, right, (((0,), (0,)), ((), ())), preferred_element_type=F32)


def dot_nt(left, right):
    return lax.dot_general(left, right, (((1,), (1,)), ((), ())), preferred_element_type=F32)


def scores_of(query, keys, allowed):
    raw = jnp.einsum("hiae,hibe->hiab", query, keys, preferred_element_type=F32)
    return jnp.where(allowed, raw * HEAD_DIM ** (-0.5), MASKED)


def attention_forward(query, keys, values, turned, allowed):
    q4, k4, v4 = split_heads(query), pick(turned, split_heads(keys)), pick(turned, split_heads(values))
    scores = scores_of(q4, k4, allowed)
    ceiling = jnp.maximum(jnp.max(scores, axis=-1, keepdims=True), 0.0)
    weights = jnp.where(allowed, jnp.exp(scores - ceiling), 0.0)
    total = jnp.exp(-ceiling) + jnp.sum(weights, axis=-1, keepdims=True)
    probs = (weights / total).astype(BF16)
    mixed = jnp.einsum("hiab,hibe->hiae", probs, v4, preferred_element_type=F32)
    return join_heads(mixed).astype(BF16), ceiling + jnp.log(total)


def attention_backward(query, keys, values, turned, allowed, log_total, grad):
    q4, k4, v4 = split_heads(query), pick(turned, split_heads(keys)), pick(turned, split_heads(values))
    g4 = split_heads(grad)
    scores = scores_of(q4, k4, allowed)
    probs = jnp.where(allowed, jnp.exp(scores - log_total), 0.0)
    grad_probs = jnp.einsum("hiae,hibe->hiab", g4, v4, preferred_element_type=F32)
    centre = jnp.sum(probs * grad_probs, axis=-1, keepdims=True)
    grad_scores = (probs * (grad_probs - centre)).astype(BF16)
    grad_values = jnp.einsum("hiab,hiae->hibe", probs.astype(BF16), g4, preferred_element_type=F32)
    scale = HEAD_DIM ** (-0.5)
    grad_query = scale * jnp.einsum(
        "hiab,hibe->hiae", grad_scores, k4, preferred_element_type=F32
    )
    grad_keys = scale * jnp.einsum("hiab,hiae->hibe", grad_scores, q4, preferred_element_type=F32)
    return (
        join_heads(grad_query.astype(BF16)),
        join_heads(pick(turned, grad_keys.astype(BF16))),
        join_heads(pick(turned, grad_values.astype(BF16))),
    )


def layer_forward(rows_in, weights, turned, allowed):
    w_qkv, b_qkv, w_out, w_up, b_up, w_down, gains, shifts = weights
    x_full = gather_rows(rows_in)
    query = (dot(x_full, w_qkv[0]) + b_qkv[0]).astype(BF16)
    keys = dot(x_full, w_qkv[1]).astype(BF16)
    values = (dot(x_full, w_qkv[2]) + b_qkv[1]).astype(BF16)
    attn, log_total = attention_forward(query, keys, values, turned, allowed)
    projected = scatter_rows(dot(attn, w_out))
    resid1 = rows_in.astype(F32) + projected + shifts[0]
    hidden, normed1, inverse1 = norm_forward(resid1, gains[0], shifts[1])
    ffn_in = gather_rows(hidden.astype(BF16))
    pre = dot(ffn_in, w_up) + b_up
    act = gelu_exact(pre).astype(BF16)
    branch = scatter_rows(dot(act, w_down))
    resid2 = hidden + branch + shifts[2]
    output, normed2, inverse2 = norm_forward(resid2, gains[1], shifts[3])
    kept = (x_full, query, keys, values, log_total, attn, normed1, inverse1, ffn_in, pre, act)
    return output.astype(BF16), kept + (normed2, inverse2)


def layer_backward(grad_out, kept, weights, turned, allowed):
    w_qkv, b_qkv, w_out, w_up, b_up, w_down, gains, shifts = weights
    x_full, query, keys, values, log_total, attn, normed1, inverse1, ffn_in, pre, act = kept[:11]
    normed2, inverse2 = kept[11:]
    grad_resid2, grad_gain2, grad_shift2 = norm_backward(grad_out, normed2, inverse2, gains[1])
    branch_rows = gather_rows(grad_resid2.astype(BF16))
    grad_act = dot_nt(branch_rows, w_down)
    grad_pre = jax.vjp(gelu_exact, pre)[1](grad_act)[0].astype(BF16)
    grad_hidden = scatter_rows(dot_nt(grad_pre, w_up))
    grad_down = dot_tn(act, branch_rows)
    grad_up = dot_tn(ffn_in, grad_pre)
    grad_upbias = jnp.sum(grad_pre.astype(F32), axis=0)
    grad_resid1, grad_gain1, grad_shift1 = norm_backward(
        grad_hidden + grad_resid2, normed1, inverse1, gains[0]
    )
    grad_mixed = gather_rows(grad_resid1.astype(BF16))
    grad_outw = dot_tn(attn, grad_mixed)
    grad_attn = dot_nt(grad_mixed, w_out).astype(BF16)
    grads = attention_backward(query, keys, values, turned, allowed, log_total, grad_attn)
    grad_rows = scatter_rows(
        dot_nt(grads[0], w_qkv[0]) + dot_nt(grads[1], w_qkv[1]) + dot_nt(grads[2], w_qkv[2])
    )
    grad_in = (grad_rows + grad_resid1).astype(BF16)
    grad_qkvw = jnp.stack([dot_tn(x_full, grad) for grad in grads])
    grad_qkvb = jnp.stack([jnp.sum(grads[k].astype(F32), axis=0) for k in (0, 2)])
    small = jnp.stack(
        [
            grad_gain1,
            grad_gain2,
            jnp.sum(grad_resid1, axis=0),
            grad_shift1,
            jnp.sum(grad_resid2, axis=0),
            grad_shift2,
        ]
    )
    return grad_in, (grad_qkvw, grad_outw, grad_up, grad_down), (grad_qkvb, grad_upbias), small


def sum_small(value, axes):
    for axis in axes:
        count = lax.axis_size(axis)
        if count & (count - 1):
            value = lax.psum(value, axis)
            continue
        bit = 1
        while bit < count:
            value = value + swap(value, axis, bit)
            bit *= 2
    return value


def body(
    tokens,
    segment_ids,
    pad_mask,
    block_perm,
    qkv_weight,
    qkv_bias,
    out_weight,
    up_weight,
    up_bias,
    down_weight,
    norm_gain,
    shift_bias,
    cotangent,
):
    section = lax.axis_index("pipe")
    place = lax.axis_index("tensor")
    first_section = section == 0
    own_weights = (
        qkv_weight[0],
        qkv_bias[0].astype(F32),
        out_weight[0],
        up_weight[0],
        up_bias[0].astype(F32),
        down_weight[0],
        norm_gain[0],
        shift_bias[0],
    )
    other_weights = tuple(swap(item, "pipe", 1) for item in own_weights)
    own_turned = block_perm[0][:, 0] == 1
    other_turned = swap(block_perm[0][:, 0].astype(F32), "pipe", 1) == 1

    def select(own, other):
        return (jnp.where(first_section, own, other), jnp.where(first_section, other, own))

    chosen = [select(own, other) for own, other in zip(own_weights, other_weights)]
    layers = [tuple(item[layer] for item in chosen) for layer in range(2)]
    turned = select(own_turned, other_turned)

    def relative(row):
        quarters = row.reshape(4, -1)
        return jnp.concatenate(
            [lax.dynamic_index_in_dim(quarters, place ^ r, 0, keepdims=False) for r in range(4)]
        ).reshape(2, -1)

    segments = relative(lax.dynamic_index_in_dim(segment_ids, section, 0, keepdims=False))
    real = relative(lax.dynamic_index_in_dim(pad_mask, section, 0, keepdims=False)) == 1

    def allowed_for(flags):
        key_segments = jnp.where(flags[:, None, None], segments[None, ::-1], segments[None])
        key_real = jnp.where(flags[:, None, None], real[None, ::-1], real[None])
        return (segments[None, :, :, None] == key_segments[:, :, None, :]) & key_real[:, :, None, :]

    allowed = [allowed_for(flags) for flags in turned]
    rows = lax.dynamic_index_in_dim(tokens, section, 0, keepdims=False)
    out_first, kept_first = layer_forward(rows, layers[0], turned[0], allowed[0])
    out_second, kept_second = layer_forward(out_first, layers[1], turned[1], allowed[1])

    def place_outputs(first, second):
        own = jnp.where(first_section, first, second)
        received = swap(jnp.where(first_section, second, first), "pipe", 1)
        return jnp.stack(
            [jnp.where(first_section, own, received), jnp.where(first_section, received, own)]
        )[None]

    layer_out = place_outputs(out_first, out_second)
    grad_out = lax.dynamic_index_in_dim(cotangent, section, 0, keepdims=False).astype(F32)
    grad_second, big_second, bias_second, small_second = layer_backward(
        grad_out, kept_second, layers[1], turned[1], allowed[1]
    )
    grad_first, big_first, bias_first, small_first = layer_backward(
        grad_second.astype(F32), kept_first, layers[0], turned[0], allowed[0]
    )
    input_grad = place_outputs(grad_first, grad_second)

    def over_parts(grad, source):
        low = grad.astype(BF16)
        received = lax.ppermute(low, "pipe", [(source, 1 - source)])
        return lax.psum((grad + received.astype(F32)).astype(BF16), "dp")

    second_sums = [over_parts(grad, 0) for grad in big_second]
    first_sums = [over_parts(grad, 1) for grad in big_first]
    qkvw, outw, upw, downw = [
        jnp.where(first_section, first, second).astype(F32)[None]
        for first, second in zip(first_sums, second_sums)
    ]

    def small_sums(biases, small):
        small = sum_small(small, ("tensor",))
        flat = jnp.concatenate([small.reshape(-1), biases[0].reshape(-1), biases[1].reshape(-1)])
        return sum_small(flat.reshape(-1, 128), ("pipe", "dp")).reshape(-1)

    flat = jnp.where(
        first_section, small_sums(bias_first, small_first), small_sums(bias_second, small_second)
    )
    width = tokens.shape[2]
    gains = flat[: 2 * width].reshape(1, 2, width)
    shifts = flat[2 * width : 6 * width].reshape(1, 4, width)
    local = qkv_bias.shape[2]
    qkvb = flat[6 * width : 6 * width + 2 * local].reshape(1, 2, local)
    upb = flat[6 * width + 2 * local :].reshape(1, -1)
    return (layer_out, input_grad, qkvw, qkvb, outw, upw, upb, downw, gains, shifts)


def solution(mesh):
    return jax.shard_map(
        body,
        mesh=mesh,
        in_specs=(
            P("dp", "tensor", None),
            P("dp", None),
            P("dp", None),
            P("pipe", "tensor", None),
            P("pipe", None, None, "tensor"),
            P("pipe", None, "tensor"),
            P("pipe", "tensor", None),
            P("pipe", None, "tensor"),
            P("pipe", "tensor"),
            P("pipe", "tensor", None),
            P("pipe", None, None),
            P("pipe", None, None),
            P("dp", "tensor", None),
        ),
        out_specs=(
            P("pipe", "dp", "tensor", None),
            P("pipe", "dp", "tensor", None),
            P("pipe", None, None, "tensor"),
            P("pipe", None, "tensor"),
            P("pipe", "tensor", None),
            P("pipe", None, "tensor"),
            P("pipe", "tensor"),
            P("pipe", "tensor", None),
            P("pipe", None, None),
            P("pipe", None, None),
        ),
        check_vma=False,
    )
```

```python
from functools import partial

import jax
import jax.numpy as jnp
from jax import lax
from jax.experimental import pallas as pl
from jax.experimental.pallas import tpu as pltpu
from jax.sharding import PartitionSpec as P

BF16 = jnp.bfloat16
F32 = jnp.float32
HEAD_DIM = 64
PAIR = 2 * HEAD_DIM
LOG2E = 1.4426950408889634
MASKED = -1e30
VMEM_LIMIT = 16 * 1024 * 1024
NORM_EPSILON_TERM = 1e-06

FLAGS = 5

SPACES = {"v": pltpu.VMEM, "s": pltpu.SMEM, "h": pl.ANY}
PLACES = {"v": pltpu.VMEM, "s": pl.ANY, "h": pltpu.HBM}


def shape(dims, dtype=BF16):
    return jax.ShapeDtypeStruct(dims, dtype)


def call(kernel, outs, args, flops=0, scratch=(), copies=0):
    scratch = list(scratch)
    if copies:
        scratch.append(pltpu.SemaphoreType.DMA((copies,)))
    return pl.pallas_call(
        kernel,
        out_shape=[PLACES[space](item.shape, item.dtype) for space, item in outs],
        in_specs=[pl.BlockSpec(memory_space=SPACES[space]) for space, _ in args],
        out_specs=[pl.BlockSpec(memory_space=SPACES[space]) for space, _ in outs],
        scratch_shapes=scratch,
        compiler_params=pltpu.CompilerParams(vmem_limit_bytes=VMEM_LIMIT),
        cost_estimate=pl.CostEstimate(flops=flops, bytes_accessed=0, transcendentals=0),
    )(*[pltpu.with_memory_space_constraint(item, PLACES[space]) for space, item in args])


class Copies:
    def __init__(self, sems):
        self.sems, self.pending = sems, []

    def start(self, source, target):
        copy = pltpu.make_async_copy(source, target, self.sems.at[len(self.pending)])
        copy.start()
        self.pending.append(copy)

    def start_one(self, cases, target):
        sem = self.sems.at[len(self.pending)]
        made = []
        for condition, source in cases:
            made.append(pltpu.make_async_copy(source, target, sem))
            pl.when(condition)(made[-1].start)
        self.pending.append(made[0])

    def done(self):
        for copy in self.pending:
            copy.wait()


def dot(left, right):
    return jnp.dot(left, right, preferred_element_type=F32)


def dot_tn(left, right):
    return lax.dot_general(left, right, (((0,), (0,)), ((), ())), preferred_element_type=F32)


def dot_nt(left, right):
    return lax.dot_general(left, right, (((1,), (1,)), ((), ())), preferred_element_type=F32)


def pack_kernel(gains_in, shifts_in, up_in, qkv_in, perm_ref, out_ref, gains, shifts, up, qkv_b, sems):
    copies = Copies(sems)
    for source, target in ((gains_in, gains), (shifts_in, shifts), (up_in, up), (qkv_in, qkv_b)):
        copies.start(source, target)
    out_ref[...] = jnp.zeros_like(out_ref)
    lane = lax.broadcasted_iota(jnp.int32, (1, out_ref.shape[1]), 1)
    flags = jnp.zeros((1, out_ref.shape[1]), F32)
    for head in range(perm_ref.shape[1]):
        flags = jnp.where(lane == head, perm_ref[0, head, 0].astype(F32), flags)
    out_ref[9:10] = flags
    copies.done()
    out_ref[0:2] = gains[0]
    out_ref[2:6] = shifts[0]
    out_ref[6:7] = up[...].astype(F32)
    out_ref[7:9, 0 : qkv_b.shape[2]] = qkv_b[0].astype(F32)


GAIN1, GAIN2, BIAS_OUT, SHIFT1, BIAS2, SHIFT2, BIAS_UP, BIAS_Q, TURNED = 0, 1, 2, 3, 4, 5, 6, 8, 10


def params_kernel(where_ref, own_ref, other_ref, pair_ref, other_pair_ref, first_out, second_out, flags_copy, flags, sems):
    section, core = where_ref[0], where_ref[1]
    width = own_ref.shape[1]
    local = width // 4
    heads = local // HEAD_DIM
    lane = lax.broadcasted_iota(jnp.int32, (1, width), 1)
    flags[...] = jnp.zeros_like(flags)
    for layer, out_ref in enumerate((first_out, second_out)):
        here = section == layer
        mine = jnp.where(here, own_ref[...], other_ref[...])
        pair = jnp.where(here, pair_ref[...], other_pair_ref[...])
        first = jnp.where(core == 0, mine, pair)
        second = jnp.where(core == 0, pair, mine)
        out_ref[...] = mine
        out_ref[BIAS_UP + 1 : BIAS_UP + 2] = pair[BIAS_UP : BIAS_UP + 1]
        biases = jnp.where(lane < local, first, pltpu.roll(second, local, 1))
        out_ref[BIAS_Q : BIAS_Q + 2] = biases[7:9]
        turned = jnp.where(lane < heads, first, pltpu.roll(second, heads, 1))[9:10]
        lanes = jnp.zeros((1, width), F32)
        for head in range(2 * heads):
            chosen = (lane // HEAD_DIM) % (2 * heads) == head
            lanes = jnp.where(chosen, turned[:, head : head + 1], lanes)
        out_ref[TURNED : TURNED + 1] = lanes
        flags[layer : layer + 1] = turned[:, 0:PAIR]
    copies = Copies(sems)
    copies.start(flags, flags_copy)
    copies.done()


def marks_kernel(where_ref, segments_ref, real_ref, out_ref):
    quarter = out_ref.shape[1] // 2
    out_ref[...] = jnp.zeros_like(out_ref)
    for r in range(4):
        cols = pl.ds(pl.multiple_of((where_ref[4] ^ r) * quarter, PAIR), quarter)
        at = slice((r % 2) * quarter, (r % 2 + 1) * quarter)
        segment = jnp.where(where_ref[0] == 0, segments_ref[0:1, cols], segments_ref[1:2, cols])
        real = jnp.where(where_ref[0] == 0, real_ref[0:1, cols], real_ref[1:2, cols])
        out_ref[1 + r // 2 : 2 + r // 2, at] = jnp.where(real == 1, segment, -1)
        if r % 2 == 0:
            out_ref[0:1, (r // 2) * quarter : (r // 2 + 1) * quarter] = segment


def halve_kernel(where_ref, *refs):
    count = len(refs) // 2
    copies = Copies(refs[-1])
    for source, half in zip(refs[:count], refs[count:-1]):
        columns = half.shape[2]
        copies.start_one(
            [
                (where_ref[2] == side, source.at[:, :, pl.ds(side * columns, columns)])
                for side in range(2)
            ],
            half,
        )
    copies.done()


def halves_of(where, *wholes):
    return call(
        halve_kernel,
        [("v", shape(whole.shape[:2] + (whole.shape[2] // 2,))) for whole in wholes],
        [("s", where)] + [("h", whole) for whole in wholes],
        copies=len(wholes),
    )


def weight_copies(copies, where_ref, layer, k, own, other, target):
    here = where_ref[0] == layer
    if len(other) == 1:
        copies.start_one(
            [(here, own.at[k]), (jnp.logical_not(here), other[0].at[k])], target(slice(None))
        )
        return
    columns = other[0].shape[-1]
    for side in range(2):
        cols = pl.ds(side * columns, columns)
        direct = where_ref[2] == side
        copies.start_one(
            [
                (here, own.at[k, :, cols]),
                (jnp.logical_not(here) & direct, other[0].at[k]),
                (jnp.logical_not(here) & jnp.logical_not(direct), other[1].at[k]),
            ],
            target(cols),
        )


def load_kernel(layer, items, plain, where_ref, *refs):
    sems = refs[-1]
    copies = Copies(sems)
    count = sum(2 * (1 + parts) for _, parts in items)
    sources, plain_in, outs = refs[:count], refs[count : count + plain], refs[count + plain : -1]
    for (by_core, parts), out_ref in zip(items, outs):
        for pair in range(2):
            own, *other = sources[: 1 + parts]
            sources = sources[1 + parts :]
            if by_core:
                rows = out_ref.shape[1] // 2
                slot = (where_ref[1] + pair) % 2
                at = pl.ds(pl.multiple_of(slot * rows, rows), rows)
                for k in range(out_ref.shape[0]):
                    weight_copies(
                        copies, where_ref, layer, k, own, other, lambda cols, k=k: out_ref.at[k, at, cols]
                    )
            else:
                weight_copies(
                    copies, where_ref, layer, 0, own, other, lambda cols: out_ref.at[pair, :, cols]
                )
    for source, target in zip(plain_in, outs[len(items) :]):
        copies.start(source, target)
    copies.done()


def load(layer, where, items, arrays=()):
    outs, sources, kinds, count = [], [], [], len(arrays)
    for by_core, own, other, pair_own, pair_other in items:
        k, rows, columns = own.shape
        outs.append(shape((k, 2 * rows, columns)) if by_core else shape((2, rows, columns)))
        sources += [own, *other, pair_own, *pair_other]
        kinds.append((by_core, len(other)))
        count += 2 * k * len(other)
    outs += [shape(item.shape, item.dtype) for item in arrays]
    return call(
        partial(load_kernel, layer, kinds, len(arrays)),
        [("v", item) for item in outs],
        [("s", where)] + [("h", item) for item in (*sources, *arrays)],
        copies=count,
    )


def qkv_kernel(x_ref, w_ref, b_ref, q_ref, kv_ref, x_copy, q_copy, sems):
    copies = Copies(sems)
    copies.start(x_ref, x_copy)
    x = x_ref[...]
    width = q_ref.shape[1]
    q_ref[...] = (dot_nt(x, w_ref[0]) + b_ref[BIAS_Q : BIAS_Q + 1, :width]).astype(BF16)
    copies.start(q_ref, q_copy)
    kv_ref[:, :width] = dot_nt(x, w_ref[1]).astype(BF16)
    kv_ref[:, width:] = (dot_nt(x, w_ref[2]) + b_ref[BIAS_Q + 1 : BIAS_Q + 2, :width]).astype(BF16)
    copies.done()


def qkv(x, w, b):
    rows, width = x.shape[0], w.shape[1]
    return call(
        qkv_kernel,
        [
            ("v", shape((rows, width))),
            ("v", shape((rows, 2 * width))),
            ("h", shape(x.shape)),
            ("h", shape((rows, width))),
        ],
        [("v", x), ("v", w), ("v", b)],
        6 * rows * x.shape[1] * width,
        copies=2,
    )


def lanes_of(rows):
    return lax.broadcasted_iota(jnp.int32, (rows, PAIR), 1)


def fill_bias(bias, side, marks_ref):
    rows = bias.shape[1]
    wanted = jnp.transpose(marks_ref[:, side * rows : (side + 1) * rows])[:, 0:1]
    for j in range(2):
        bias[j] = jnp.where(wanted == marks_ref[1 + j : 2 + j, :], 0.0, MASKED).astype(F32)


def block_of(where_ref, layer, head, turned):
    return where_ref[FLAGS + 6 * layer + head] ^ turned


def attn_rows(layer, where_ref, turned, q_ref, kv_ref, marks_ref, o_ref, lse_ref, bias):
    rows, width = q_ref.shape
    fill_bias(bias, turned, marks_ref)
    lanes = lanes_of(rows)
    low = lanes < HEAD_DIM
    scale = HEAD_DIM**-0.5 * LOG2E
    logs = jnp.zeros((rows, PAIR), F32)
    for tile in range(width // PAIR):
        cols = slice(tile * PAIR, (tile + 1) * PAIR)
        vcols = slice(width + cols.start, width + cols.stop)
        q = q_ref[:, cols]
        mixed = []
        for side in range(2):
            head = 2 * tile + side
            block = block_of(where_ref, layer, head, turned)
            q_head = jnp.where(low if side == 0 else ~low, q, jnp.zeros_like(q))
            s = dot_nt(q_head, kv_ref[block, :, cols]) * scale + bias[block]
            top = jnp.maximum(jnp.max(s, axis=1, keepdims=True), 0.0)
            e = jnp.exp2(s - top)
            total = jnp.exp2(-top) + jnp.sum(e, axis=1, keepdims=True)
            p = (e * (1.0 / total)).astype(BF16)
            mixed.append(dot(p, kv_ref[block, :, vcols]))
            logs = jnp.where(lanes == head, top + jnp.log2(total), logs)
        o_ref[:, cols] = jnp.where(low, mixed[0], mixed[1]).astype(BF16)
    lse_ref[...] = logs


def attn_far_kernel(
    layer, where_ref, q_ref, kv0_ref, kv1_ref, kv2_ref, kv3_ref, marks_ref, w_ref,
    out_ref, kv_ref, kv_copy, o_copy, lse_copy, bias, o_ref, lse_ref, sems,
):
    copies = Copies(sems)
    half = kv0_ref.shape[0]
    for block, pair in enumerate(((kv0_ref, kv1_ref), (kv2_ref, kv3_ref))):
        kv_ref[block, :half] = pair[0][...]
        kv_ref[block, half:] = pair[1][...]
    copies.start(kv_ref, kv_copy)
    attn_rows(layer, where_ref, 1, q_ref, kv_ref, marks_ref, o_ref, lse_ref, bias)
    copies.start(o_ref, o_copy)
    copies.start(lse_ref, lse_copy)
    out_ref[...] = dot(o_ref[...], w_ref[0]).astype(out_ref.dtype)
    copies.done()


def attn_own_kernel(
    layer, where_ref, q_ref, kv_ref, marks_ref, w_ref, out_ref, o_copy, lse_copy, bias, o_ref, lse_ref, sems
):
    copies = Copies(sems)
    attn_rows(layer, where_ref, 0, q_ref, kv_ref, marks_ref, o_ref, lse_ref, bias)
    copies.start(o_ref, o_copy)
    copies.start(lse_ref, lse_copy)
    out_ref[...] = dot(o_ref[...], w_ref[0]).astype(out_ref.dtype)
    copies.done()


def attn(layer, where, q, kv, marks, w):
    rows, width = q.shape
    far = len(kv) > 1
    outs = [("v", shape((rows, w.shape[2]), BF16 if far else F32))]
    if far:
        joined = shape((2, 2 * rows, kv[0].shape[1]))
        outs += [("v", joined), ("h", joined)]
    outs += [("h", shape((rows, width))), ("h", shape((rows, PAIR), F32))]
    args = [("s", where)] + [("v", item) for item in (q, *kv, marks, w)]
    return call(
        partial(attn_far_kernel if far else attn_own_kernel, layer),
        outs,
        args,
        8 * rows * rows * width + 2 * rows * width * w.shape[2],
        scratch=[
            pltpu.VMEM((2, rows, 2 * rows), F32),
            pltpu.VMEM((rows, width), BF16),
            pltpu.VMEM((rows, PAIR), F32),
        ],
        copies=3 if far else 2,
    )


def normed_rows(resid):
    centred = resid - jnp.mean(resid, axis=1, keepdims=True)
    inverse = lax.rsqrt(jnp.mean(centred * centred, axis=1, keepdims=True) + NORM_EPSILON_TERM)
    return centred * inverse, inverse


def norm1_kernel(x_ref, own_ref, far_ref, norms_ref, low_ref, full_ref, resid_copy, low_copy, resid, sems):
    copies = Copies(sems)
    projected = own_ref[...] + far_ref[...].astype(F32)
    total = x_ref[...].astype(F32) + projected + norms_ref[BIAS_OUT : BIAS_OUT + 1, :]
    resid[...] = total
    copies.start(resid, resid_copy)
    hidden = normed_rows(total)[0] * norms_ref[GAIN1 : GAIN1 + 1, :] + norms_ref[SHIFT1 : SHIFT1 + 1, :]
    full_ref[...] = hidden
    low_ref[...] = hidden.astype(BF16)
    copies.start(low_ref, low_copy)
    copies.done()


def norm1(x, own, far, norms):
    return call(
        norm1_kernel,
        [("v", shape(x.shape)), ("v", shape(x.shape, F32)), ("h", shape(x.shape, F32)), ("h", shape(x.shape))],
        [("v", x), ("v", own), ("v", far), ("v", norms)],
        scratch=[pltpu.VMEM(x.shape, F32)],
        copies=2,
    )


def norm2_kernel(h_ref, own_ref, far_ref, norms_ref, low_ref, resid_copy, low_copy, resid, sems):
    copies = Copies(sems)
    branch = own_ref[...] + far_ref[...].astype(F32)
    total = h_ref[...] + branch + norms_ref[BIAS2 : BIAS2 + 1, :]
    resid[...] = total
    copies.start(resid, resid_copy)
    out = normed_rows(total)[0] * norms_ref[GAIN2 : GAIN2 + 1, :] + norms_ref[SHIFT2 : SHIFT2 + 1, :]
    low_ref[...] = out.astype(BF16)
    copies.start(low_ref, low_copy)
    copies.done()


def norm2(h, own, far, norms):
    return call(
        norm2_kernel,
        [("v", shape(h.shape)), ("h", shape(h.shape, F32)), ("h", shape(h.shape))],
        [("v", h), ("v", own), ("v", far), ("v", norms)],
        scratch=[pltpu.VMEM(h.shape, F32)],
        copies=2,
    )


TAIL = tuple(
    0.5 * c
    for c in (
        0.05029408002973294, -0.1830316054165625, 0.16930258232763196, -0.005798692821681883,
        0.14152663657068731, 0.16851528425000623, 0.20784663429852349, 0.22566934002005623,
        0.22567586682378352,
    )
)


def gelu_and_slope(u):
    bell = jnp.exp2(u * u * (-0.5 * LOG2E))
    t = 1.0 / (1.0 + jnp.abs(u) * (0.4 * 0.5**0.5))
    poly = TAIL[0]
    for c in TAIL[1:]:
        poly = poly * t + c
    tail = poly * t * bell
    below = jnp.where(u < 0.0, tail, 1.0 - tail)
    return u * below, below + u * bell * 0.3989422804014327


def ffn_kernel(far, h_ref, up_ref, down_ref, b_ref, out_ref, act_copy, slope_copy, *rest):
    act_ref, slope_ref, sems = rest[-3:]
    copies = Copies(sems)
    if far:
        copies.start(h_ref, rest[0])
    h = h_ref[...]
    units = up_ref.shape[2]
    total = None
    for half in range(2):
        cols = slice(half * units, (half + 1) * units)
        act, slope = gelu_and_slope(dot(h, up_ref[half]) + b_ref[BIAS_UP + half : BIAS_UP + half + 1, :])
        act = act.astype(BF16)
        act_ref[:, cols] = act
        slope_ref[:, cols] = slope.astype(BF16)
        copies.start(act_ref.at[:, cols], act_copy.at[:, cols])
        copies.start(slope_ref.at[:, cols], slope_copy.at[:, cols])
        part = dot(act, down_ref[half])
        total = part if total is None else total + part
    out_ref[...] = total.astype(out_ref.dtype)
    copies.done()


def ffn(h, up, down, b, far):
    rows, width = h.shape
    units = 2 * up.shape[2]
    outs = [
        ("v", shape((rows, width), BF16 if far else F32)),
        ("h", shape((rows, units))),
        ("h", shape((rows, units))),
    ]
    if far:
        outs.append(("h", shape(h.shape)))
    return call(
        partial(ffn_kernel, far),
        outs,
        [("v", h), ("v", up), ("v", down), ("v", b)],
        4 * rows * width * units,
        scratch=[pltpu.VMEM((rows, units), BF16)] * 2,
        copies=5,
    )


def norm_back(upstream, resid, gain, low_ref, full_ref, sums_ref):
    normed, inverse = normed_rows(resid)
    scaled = upstream * gain
    inner = (
        scaled
        - jnp.mean(scaled, axis=1, keepdims=True)
        - normed * jnp.mean(scaled * normed, axis=1, keepdims=True)
    )
    grad = inverse * inner
    full_ref[...] = grad
    low_ref[...] = grad.astype(BF16)
    sums_ref[...] = jnp.zeros_like(sums_ref)
    sums_ref[0:1] = jnp.sum(upstream * normed, axis=0, keepdims=True)
    sums_ref[1:2] = jnp.sum(upstream, axis=0, keepdims=True)
    sums_ref[2:3] = jnp.sum(grad, axis=0, keepdims=True)


def norm2_back_kernel(inner, *refs):
    if inner:
        own_ref, far_ref, resid1_ref, resid_in, norms_ref, low_ref, full_ref, sums_ref, grad_ref, resid, sems = refs
    else:
        up_ref, resid_in, norms_ref, low_ref, full_ref, sums_ref, resid, sems = refs
    copies = Copies(sems)
    copies.start(resid_in, resid)
    if inner:
        grad_in = (own_ref[...] + far_ref[...].astype(F32) + resid1_ref[...]).astype(BF16)
        grad_ref[...] = grad_in
    else:
        grad_in = up_ref[...]
    copies.done()
    gain = norms_ref[GAIN2 : GAIN2 + 1, :]
    norm_back(grad_in.astype(F32), resid[...], gain, low_ref, full_ref, sums_ref)


def norm2_back(upstream, resid, norms):
    dims = upstream[0].shape
    inner = len(upstream) > 1
    outs = [("v", shape(dims)), ("v", shape(dims, F32)), ("v", shape((8, dims[1]), F32))]
    if inner:
        outs.append(("v", shape(dims)))
    return call(
        partial(norm2_back_kernel, inner),
        outs,
        [("v", item) for item in upstream] + [("h", resid), ("v", norms)],
        scratch=[pltpu.VMEM(dims, F32)],
        copies=1,
    )


def norm1_back_kernel(own_ref, far_ref, skip_ref, resid_in, norms_ref, low_ref, full_ref, sums_ref, resid, sems):
    copies = Copies(sems)
    copies.start(resid_in, resid)
    upstream = own_ref[...] + far_ref[...].astype(F32) + skip_ref[...]
    copies.done()
    gain = norms_ref[GAIN1 : GAIN1 + 1, :]
    norm_back(upstream, resid[...], gain, low_ref, full_ref, sums_ref)


def norm1_back(own, far, skip, resid, norms):
    dims = own.shape
    return call(
        norm1_back_kernel,
        [("v", shape(dims)), ("v", shape(dims, F32)), ("v", shape((8, dims[1]), F32))],
        [("v", own), ("v", far), ("v", skip), ("h", resid), ("v", norms)],
        scratch=[pltpu.VMEM(dims, F32)],
        copies=1,
    )


def ffn_back_kernel(df_ref, slope_ref, up_ref, down_ref, dh_ref, du_ref, db_ref):
    df = df_ref[...]
    units = up_ref.shape[2]
    total = None
    for half in range(2):
        cols = slice(half * units, (half + 1) * units)
        du = (dot_nt(df, down_ref[half]) * slope_ref[:, cols].astype(F32)).astype(BF16)
        du_ref[:, cols] = du
        db_ref[half : half + 1, :] = jnp.sum(du.astype(F32), axis=0, keepdims=True)
        part = dot_nt(du, up_ref[half])
        total = part if total is None else total + part
    dh_ref[...] = total.astype(dh_ref.dtype)


def ffn_back(df, slope, up, down, far):
    rows, width = df.shape
    units = 2 * up.shape[2]
    return call(
        ffn_back_kernel,
        [
            ("v", shape((rows, width), BF16 if far else F32)),
            ("v", shape((rows, units))),
            ("v", shape((2, units // 2), F32)),
        ],
        [("v", df), ("v", slope), ("v", up), ("v", down)],
        4 * rows * width * units,
    )


def ffn_grads_of(half, h, act, df, du):
    units = act[0].shape[1] // 2
    cols = slice(half * units, (half + 1) * units)
    up = dot_tn(h[0][...], du[0][:, cols]) + dot_tn(h[1][...], du[1][:, cols])
    down = dot_tn(act[0][:, cols], df[0][...]) + dot_tn(act[1][:, cols], df[1][...])
    return up, down


def ffn_pair_kernel(h0, h1, a0, a1, df0, df1, du0, du1, out_ref):
    up, down = ffn_grads_of(1, (h0, h1), (a0, a1), (df0, df1), (du0, du1))
    out_ref[0] = up.astype(BF16)
    out_ref[1] = down.astype(BF16)


def ffn_own_kernel(where_ref, h0, h1, a0, a1, df0, df1, du0, du1, got_ref, *outs):
    up, down = ffn_grads_of(0, (h0, h1), (a0, a1), (df0, df1), (du0, du1))
    up += got_ref[0].astype(F32)
    down += got_ref[1].astype(F32)
    first = where_ref[0] == 0
    half = outs[0].shape[0]
    for part in range(2):
        rows = slice(part * half, (part + 1) * half)
        outs[2 * part][...] = jnp.where(first, down[rows], up[rows]).astype(BF16)
        outs[2 * part + 1][...] = jnp.where(first, up[rows], down[rows])


def ffn_pair(args):
    rows, width = args[0].shape
    units = args[2].shape[1] // 2
    return call(
        ffn_pair_kernel,
        [("v", shape((2, width, units)))],
        [("v", item) for item in args],
        8 * rows * width * units,
    )[0]


def ffn_own(where, args, got):
    rows, width = args[0].shape
    units = args[2].shape[1] // 2
    return call(
        ffn_own_kernel,
        [("v", shape((width // 2, units))), ("v", shape((width // 2, units), F32))] * 2,
        [("s", where)] + [("v", item) for item in (*args, got)],
        8 * rows * width * units,
    )


def attn_back_kernel(
    layer, turned, where_ref, dz_ref, q_ref, kv_ref, marks_ref, lse_ref, w_ref,
    dq_ref, dkv_ref, dkv_pair_ref, bias, do_ref,
):
    rows, width = q_ref.shape
    fill_bias(bias, turned, marks_ref)
    low = lanes_of(rows) < HEAD_DIM
    scale = HEAD_DIM**-0.5
    do_ref[...] = dot_nt(dz_ref[...], w_ref[0]).astype(BF16)
    for tile in range(width // PAIR):
        cols = slice(tile * PAIR, (tile + 1) * PAIR)
        vcols = slice(width + cols.start, width + cols.stop)
        q, do = q_ref[:, cols], do_ref[:, cols]
        dq, dk, dv = [], 0.0, 0.0
        for side in range(2):
            head = 2 * tile + side
            block = block_of(where_ref, layer, head, turned)
            part = low if side == 0 else ~low
            q_head = jnp.where(part, q, jnp.zeros_like(q))
            do_head = jnp.where(part, do, jnp.zeros_like(do))
            k = kv_ref[block, :, cols]
            s = dot_nt(q_head, k) * (scale * LOG2E) + bias[block]
            p = jnp.exp2(s - lse_ref[:, head : head + 1])
            dp = dot_nt(do_head, kv_ref[block, :, vcols])
            centre = jnp.sum(p * dp, axis=1, keepdims=True)
            ds = (p * (dp - centre)).astype(BF16)
            dq.append(dot(ds, k))
            dv += dot_tn(p.astype(BF16), do_head)
            dk += dot_tn(ds, q_head)
        dq_ref[:, cols] = (jnp.where(low, dq[0], dq[1]) * scale).astype(BF16)
        dkv_ref[:, cols] = dk[:rows] * scale
        dkv_ref[:, vcols] = dv[:rows]
        dkv_pair_ref[:, cols] = (dk[rows:] * scale).astype(BF16)
        dkv_pair_ref[:, vcols] = dv[rows:].astype(BF16)


def attn_back(layer, turned, where, dz, q, kv, marks, lse, w):
    rows, width = q.shape
    return call(
        partial(attn_back_kernel, layer, turned),
        [("v", shape((rows, width))), ("v", shape((rows, 2 * width), F32)), ("v", shape((rows, 2 * width)))],
        [("s", where)] + [("v", item) for item in (dz, q, kv, marks, lse, w)],
        20 * rows * rows * width,
        scratch=[pltpu.VMEM((2, rows, 2 * rows), F32), pltpu.VMEM((rows, width), BF16)],
    )


def row_grads_kernel(
    small_ref, dq0_ref, dq1_ref, kv0_ref, kv1_ref, pair0_ref, pair1_ref, w_ref, dx_ref, d0_ref, d1_ref
):
    width = dq0_ref.shape[1]
    turned = small_ref[TURNED : TURNED + 1, :] == 1.0
    near = kv0_ref[...] + pair0_ref[...].astype(F32)
    far = kv1_ref[...] + pair1_ref[...].astype(F32)
    d0_ref[:, :width] = dq0_ref[...]
    d1_ref[:, :width] = dq1_ref[...]
    d0_ref[:, width:] = jnp.where(turned, far, near).astype(BF16)
    d1_ref[:, width:] = jnp.where(turned, near, far).astype(BF16)
    total = None
    for k in range(3):
        part = dot(d1_ref[:, k * width : (k + 1) * width], w_ref[k])
        total = part if total is None else total + part
    dx_ref[...] = total.astype(BF16)


def row_grads(small, dq, kv, pair, w):
    rows, width = dq[0].shape
    return call(
        row_grads_kernel,
        [("v", shape((rows, w.shape[2])))] + [("v", shape((rows, 3 * width)))] * 2,
        [("v", item) for item in (small, *dq, *kv, *pair, w)],
        6 * rows * width * w.shape[2],
    )


def attn_grads_kernel(
    where_ref, d0_ref, d1_ref, x0_ref, x1_ref, o0_ref, o1_ref, dz0_ref, dz1_ref, w_ref,
    dx_ref, own_ref, pair_ref, db_ref,
):
    width = o0_ref.shape[1]
    first_core = where_ref[1] == 0
    share = width // 2
    db_ref[...] = jnp.zeros_like(db_ref)
    for k in range(4):
        cols = slice(k * width, (k + 1) * width)
        if k < 3:
            left, right = (d0_ref[:, cols], d1_ref[:, cols]), (x0_ref[...], x1_ref[...])
        else:
            left, right = (o0_ref[...], o1_ref[...]), (dz0_ref[...], dz1_ref[...])
        if k in (0, 2):
            sums = jnp.sum(left[0].astype(F32), axis=0, keepdims=True)
            sums += jnp.sum(left[1].astype(F32), axis=0, keepdims=True)
            db_ref[0:1, k // 2 * width : (k // 2 + 1) * width] = sums
        both = dot_tn(left[0], right[0]) + dot_tn(left[1], right[1])
        rows = slice(k * share, (k + 1) * share)
        own_ref[rows] = jnp.where(first_core, both[:share], both[share:])
        pair_ref[rows] = jnp.where(first_core, both[share:], both[:share]).astype(BF16)
    total = None
    for k in range(3):
        part = dot(d0_ref[:, k * width : (k + 1) * width], w_ref[k])
        total = part if total is None else total + part
    dx_ref[...] = total


def attn_grads(where, d, x, o, dz, w):
    rows, width = o[0].shape
    columns = x[0].shape[1]
    return call(
        attn_grads_kernel,
        [
            ("v", shape((rows, columns), F32)),
            ("v", shape((2 * width, columns), F32)),
            ("v", shape((2 * width, columns))),
            ("v", shape((8, 2 * width), F32)),
        ],
        [("s", where)] + [("v", item) for item in (*d, *x, *o, *dz, w)],
        22 * rows * width * columns,
    )


def split_kernel(where_ref, own_ref, got_ref, sent_ref, kept_ref):
    half = kept_ref.shape[0]
    first = where_ref[0] == 0
    top = own_ref[:half] + got_ref[:half].astype(F32)
    bottom = own_ref[half:] + got_ref[half:].astype(F32)
    kept_ref[...] = jnp.where(first, top, bottom)
    sent_ref[...] = jnp.where(first, bottom, top).astype(BF16)


def split(where, own, got):
    rows, columns = own.shape
    return call(
        split_kernel,
        [("v", shape((rows // 2, columns))), ("v", shape((rows // 2, columns), F32))],
        [("s", where), ("v", own), ("v", got)],
    )


def add_kernel(where_ref, kept_ref, got_ref, out_ref):
    out_ref[...] = (kept_ref[...] + got_ref[...].astype(F32)).astype(BF16)


def halve_sum_kernel(bit, parts, where_ref, *refs):
    kept, got, (sent_ref, own_ref) = refs[:parts], refs[parts : 2 * parts], refs[2 * parts :]
    mine = (where_ref[3] >> bit) & 1
    if parts == 2:
        for half in range(2):
            total = kept[half][...] + got[half][...].astype(F32)

            @pl.when(mine == half)
            def _():
                own_ref[...] = total

            @pl.when(mine != half)
            def _():
                sent_ref[...] = total.astype(BF16)

        return
    rows = own_ref.shape[0]
    at = pl.ds(pl.multiple_of(mine * rows, 16), rows)
    own_ref[...] = kept[0][at] + got[0][at].astype(F32)
    at = pl.ds(pl.multiple_of((1 - mine) * rows, 16), rows)
    sent_ref[...] = (kept[0][at] + got[0][at].astype(F32)).astype(BF16)


def join_kernel(bit, where_ref, own_ref, got_ref, out_ref):
    rows = own_ref.shape[0]
    mine = (where_ref[3] >> bit) & 1
    out_ref[pl.ds(pl.multiple_of(mine * rows, 16), rows)] = own_ref[...]
    out_ref[pl.ds(pl.multiple_of((1 - mine) * rows, 16), rows)] = got_ref[...]


def results_kernel(kind, where_ref, *refs):
    *pieces, first_ref, second_ref, buffer, sems = refs
    copies = Copies(sems)
    count = len(pieces) - 2
    rows = pieces[0].shape[0]
    first = where_ref[0] == 0
    for at in range(count):
        side, part = divmod(at, count // 2)
        other = pieces[count + side][part * rows : (part + 1) * rows]
        values = jnp.where(first, pieces[at][...], other).astype(F32)
        buffer[at * rows : (at + 1) * rows] = values
        if kind == "ffn":
            target = (first_ref, second_ref)[side].at[pl.ds(part * rows, rows)]
            copies.start(buffer.at[pl.ds(at * rows, rows)], target)
            continue
        local = rows // 2
        for k in (2 * at, 2 * at + 1):
            target = first_ref.at[k] if k < 3 else second_ref
            copies.start(buffer.at[pl.ds(k * local, local)], target)
    copies.done()


def results(kind, where, first, second):
    rows, columns = first[0].shape
    if kind == "attn":
        outs = [shape((3, rows // 2, columns), F32), shape((rows // 2, columns), F32)]
    else:
        outs = [shape((rows * len(first) // 2, columns), F32)] * 2
    return call(
        partial(results_kernel, kind),
        [("h", item) for item in outs],
        [("s", where)] + [("v", item) for item in (*first, *second)],
        scratch=[pltpu.VMEM((rows * len(first), columns), F32)],
        copies=4,
    )


def place_kernel(where_ref, first_ref, second_ref, first_got, second_got, out_ref, buffer, sems):
    copies = Copies(sems)
    first = where_ref[0] == 0
    buffer[0] = jnp.where(first, first_ref[...], second_got[...])
    buffer[1] = jnp.where(first, first_got[...], second_ref[...])
    copies.start(buffer, out_ref.at[0])
    copies.done()


def grad_in_kernel(where_ref, own_ref, far_ref, skip_ref, out_ref):
    out_ref[...] = (own_ref[...] + far_ref[...].astype(F32) + skip_ref[...]).astype(BF16)


def pack_sums_kernel(where_ref, *refs):
    own_ref, pair_ref = refs[-2:]
    for layer in range(2):
        norm1_ref, norm2_ref, up0_ref, up1_ref, qkv_ref = refs[5 * layer : 5 * layer + 5]
        at = 8 * layer
        for row, source in (
            (GAIN1, norm1_ref[0:1]),
            (GAIN2, norm2_ref[0:1]),
            (BIAS_OUT, norm1_ref[2:3]),
            (SHIFT1, norm1_ref[1:2]),
            (BIAS2, norm2_ref[2:3]),
            (SHIFT2, norm2_ref[1:2]),
            (7, qkv_ref[0:1]),
        ):
            own_ref[at + row : at + row + 1] = source
            pair_ref[at + row : at + row + 1] = source
        own_ref[at + 6 : at + 7] = up0_ref[0:1] + up1_ref[0:1]
        pair_ref[at + 6 : at + 7] = up0_ref[1:2] + up1_ref[1:2]


def small_add_kernel(where_ref, own_ref, got_ref, total_ref, shared_ref):
    total = own_ref[...] + got_ref[...]
    total_ref[...] = total
    row = lax.broadcasted_iota(jnp.int32, total.shape, 0)
    shared_ref[...] = jnp.where(row % 8 < BIAS_UP, total, 0.0)


def small_results_kernel(where_ref, own_ref, got_ref, *refs):
    outs, (gains, shifts, up, qkv_b), sems = refs[:4], refs[4:8], refs[8]
    total = own_ref[...] + got_ref[...]
    total = jnp.where(where_ref[0] == 0, total[:8], total[8:])
    gains[0] = total[0:2]
    shifts[0] = total[2:6]
    up[...] = total[6:7]
    local = qkv_b.shape[2]
    for k in range(2):
        both = total[7:8, 2 * k * local : 2 * (k + 1) * local]
        qkv_b[0, k : k + 1] = jnp.where(where_ref[1] == 0, both[:, :local], both[:, local:])
    copies = Copies(sems)
    for source, target in zip((gains, shifts, up, qkv_b), outs):
        copies.start(source, target)
    copies.done()


def swap(value, axis, bit):
    count = lax.axis_size(axis)
    return lax.ppermute(value, axis, [(source, source ^ bit) for source in range(count)])


def core_swap(value):
    return swap(value, "tensor", 1)


def chip_swap(value):
    return swap(value, "tensor", 2)


def tie(value, *after):
    return lax.optimization_barrier((value, *after))[0]


class Sum:
    def __init__(self, owner, *pieces):
        self.owner = owner
        self.kept = [kept for _, kept in pieces]
        self.got = [swap(sent, "pipe", 1) for sent, _ in pieces]
        count = lax.axis_size("dp")
        self.bits = count.bit_length() - 1
        self.halving = count == 1 << self.bits and self.kept[0].shape[0] % (16 * count) == 0

    def add(self, where):
        totals = [
            call(add_kernel, [("v", shape(kept.shape))], [("s", where), ("v", kept), ("v", got)])[0]
            for kept, got in zip(self.kept, self.got)
        ]
        self.total = totals[0] if len(totals) == 1 else jnp.concatenate(totals)
        return self.total

    def halve(self, bit, where):
        parts = len(self.kept)
        rows, columns = self.kept[0].shape
        dims = (rows * parts // 2, columns)
        sent, kept = call(
            partial(halve_sum_kernel, bit, parts),
            [("v", shape(dims)), ("v", shape(dims, F32))],
            [("s", where)] + [("v", item) for item in (*self.kept, *self.got)],
        )
        self.kept, self.got = [kept], [swap(sent, "dp", 1 << bit)]
        return sent

    def join(self, bit, where):
        rows, columns = self.total.shape
        got = swap(self.total, "dp", 1 << bit)
        (self.total,) = call(
            partial(join_kernel, bit),
            [("v", shape((2 * rows, columns)))],
            [("s", where), ("v", self.total), ("v", got)],
        )
        return self.total

    def steps(self):
        if not self.halving:

            def whole(where):
                self.add(where)
                self.total = lax.psum(self.total, "dp")
                return self.total

            return [whole]
        bits = range(self.bits)
        return (
            [partial(self.halve, bit) for bit in bits]
            + [self.add]
            + [partial(self.join, bit) for bit in reversed(bits)]
        )

    def finish(self, *after):
        self.other = lax.ppermute(
            tie(self.total, *after) if after else self.total, "pipe", [(1 - self.owner, self.owner)]
        )


def layer_forward(layer, own_in, far_in, w_qkv, small, marks, where, hooks):
    own_q, own_kv, own_x_kept, own_q_kept = qkv(own_in, w_qkv, small)
    own_pair = core_swap(own_kv)
    far_q, far_kv, far_x_kept, far_q_kept = qkv(far_in, w_qkv, small)
    far_pair = core_swap(far_kv)
    w_out = hooks["out"](far_q)
    far_out, kv, kv_kept, far_o, far_lse = attn(
        layer, where, far_q, (own_kv, own_pair, far_kv, far_pair), marks, w_out
    )
    far_out = chip_swap(far_out)
    own_out, own_o, own_lse = attn(layer, where, own_q, (kv,), marks, w_out)
    w_up, w_down = hooks["ffn"](own_out)
    own_out = tie(own_out, w_up)
    own_h, hidden, resid1, own_h_kept = norm1(own_in, own_out, far_out, small)
    far_h = chip_swap(own_h)
    own_branch, own_act, own_slope = ffn(own_h, w_up, w_down, small, False)
    far_h = tie(far_h, own_branch)
    far_branch, far_act, far_slope, far_h_kept = ffn(far_h, w_up, w_down, small, True)
    own_branch = tie(own_branch, *hooks["next"](far_branch))
    output, resid2, output_kept = norm2(hidden, own_branch, chip_swap(far_branch), small)
    kept = dict(
        x=(own_x_kept, far_x_kept),
        q=(own_q_kept, far_q_kept),
        kv=kv_kept,
        lse=(own_lse, far_lse),
        o=(own_o, far_o),
        resid=(resid1, resid2),
        h=(own_h_kept, far_h_kept),
        act=(own_act, far_act),
        slope=(own_slope, far_slope),
    )
    return output, output_kept, kept


def layer_backward(layer, upstream, kept, small, marks, where, loads, hooks):
    own_df, skip2, norm2_sums, *grad_in = norm2_back(upstream, kept["resid"][1], small)
    far_df = chip_swap(own_df)
    w_up, w_down, own_slope, far_slope = loads["ffn"](kept["slope"], own_df)
    own_dh, own_du, own_db = ffn_back(own_df, own_slope, w_up, w_down, False)
    far_df = tie(far_df, own_dh, *hooks["df"](own_dh))
    far_dh, far_du, far_db = ffn_back(far_df, far_slope, w_up, w_down, True)
    own_act, far_act, own_h, far_h = loads["rows"]((*kept["act"], *kept["h"]), far_dh)
    grads = (own_h, far_h, own_act, far_act, own_df, far_df, own_du, far_du)
    pair = ffn_pair(grads)
    own_dh = tie(own_dh, *hooks["dh"](pair))
    parts = ffn_own(where, grads, core_swap(pair))
    own_dh = tie(own_dh, parts[0])
    own_dz, skip1, norm1_sums = norm1_back(own_dh, chip_swap(far_dh), skip2, kept["resid"][0], small)
    far_dz = chip_swap(own_dz)
    w_out, kv, own_q, far_q, own_lse, far_lse = loads["out"](
        (kept["kv"], *kept["q"], *kept["lse"]), own_dz
    )
    own_dq, own_dkv, own_send = attn_back(layer, 0, where, own_dz, own_q, kv, marks, own_lse, w_out)
    own_pair = core_swap(own_send)
    w_qkv, own_x, far_x, own_o, far_o = loads["qkv"]((*kept["x"], *kept["o"]), own_send)
    far_dz = tie(far_dz, w_qkv, *hooks["dz"](own_send, parts))
    far_dq, far_dkv, far_send = attn_back(layer, 1, where, far_dz, far_q, kv, marks, far_lse, w_out)
    far_pair = core_swap(far_send)
    far_dx, own_d, far_d = row_grads(
        small, (own_dq, far_dq), (own_dkv, far_dkv), (own_pair, far_pair), w_qkv
    )
    far_dx = chip_swap(far_dx)
    own_dx, attn_own, attn_pair, qkv_sums = attn_grads(
        where, (own_d, far_d), (own_x, far_x), (own_o, far_o), (own_dz, far_dz), w_qkv
    )
    sums = (norm1_sums, norm2_sums, own_db, far_db, qkv_sums)
    return (own_dx, far_dx, skip1), grad_in, sums, (attn_own, core_swap(attn_pair)), parts


def body(
    tokens,
    segment_ids,
    pad_mask,
    block_perm,
    qkv_weight,
    qkv_bias,
    out_weight,
    up_weight,
    up_bias,
    down_weight,
    norm_gain,
    shift_bias,
    cotangent,
):
    section = lax.axis_index("pipe")
    place = lax.axis_index("tensor")
    replica = lax.axis_index("dp")
    paired = lax.axis_size("dp") % 2 == 0
    width = tokens.shape[2]
    local = qkv_bias.shape[2]
    here = jnp.stack([section, place % 2, replica % 2, replica, place]).astype(jnp.int32)
    qkv_rows = jnp.transpose(qkv_weight[0], (0, 2, 1))

    def other_half(half, whole):
        if paired:
            return swap(half, "dp", 1)
        even = replica % 2 == 0
        rest = jnp.where(even, whole[..., width // 2 :], whole[..., : width // 2])
        return swap(rest, "pipe", 1)

    qkv_half, out_half = halves_of(here, qkv_rows, out_weight)
    qkv_x = swap(qkv_half, "pipe", 1)
    rows = lax.optimization_barrier(lax.dynamic_index_in_dim(tokens, section, 0, keepdims=False))
    far_rows = chip_swap(rows)
    (own_small,) = call(
        pack_kernel,
        [("v", shape((16, width), F32))],
        [("h", norm_gain), ("h", shift_bias), ("h", up_bias), ("h", qkv_bias), ("s", block_perm)],
        scratch=[
            pltpu.VMEM(item.shape, item.dtype) for item in (norm_gain, shift_bias, up_bias, qkv_bias)
        ],
        copies=4,
    )
    other_small = swap(own_small, "pipe", 1)
    out_x = swap(tie(out_half, qkv_x), "pipe", 1)
    up_half, down_half = halves_of(tie(here, own_small), up_weight, down_weight)
    up_x = swap(tie(up_half, out_x, other_small), "pipe", 1)
    *smalls, flags = call(
        params_kernel,
        [("v", shape((16, width), F32))] * 2 + [("h", shape((8, PAIR), F32))],
        [("s", here)]
        + [
            ("v", item)
            for item in (own_small, other_small, core_swap(own_small), core_swap(other_small))
        ],
        scratch=[pltpu.VMEM((8, PAIR), F32)],
        copies=1,
    )
    heads = 2 * block_perm.shape[1]
    where = jnp.concatenate([here, flags[:2, :heads].reshape(-1).astype(jnp.int32)])
    (marks,) = call(
        marks_kernel,
        [("v", shape((8, segment_ids.shape[1] // 2), jnp.int32))],
        [("s", here), ("v", segment_ids), ("v", pad_mask)],
    )

    def item(by_core, own, other):
        return by_core, own, other, core_swap(own), tuple(core_swap(part) for part in other)

    items = dict(
        qkv=item(True, qkv_rows, (qkv_x, other_half(qkv_x, qkv_rows))),
        out=item(True, out_weight, (out_x, other_half(out_x, out_weight))),
    )
    ready = tie(where, far_rows, marks, *smalls)
    (first_qkv,) = load(0, ready, [items["qkv"]])

    fetched = {}

    def first_ffn(after):
        down_x = fetched["down"]
        items["up"] = item(False, up_weight, (up_x, fetched["up"]))
        items["down"] = item(False, down_weight, (down_x, other_half(down_x, down_weight)))
        return load_ffn(0, (), after)

    def first_out(after):
        fetched["down"] = swap(tie(down_half, up_x), "pipe", 1)
        fetched["up"] = other_half(up_x, up_weight)
        return load(0, tie(where, after, up_x), [items["out"]])[0]

    def load_ffn(layer, arrays, after):
        return load(layer, tie(where, after), [items["up"], items["down"]], arrays)

    def load_one(layer, name, arrays, after):
        return load(layer, tie(where, after), [items[name]], arrays)

    def load_rows(arrays, after):
        return load(0, tie(where, after), [], arrays)

    second = []

    def load_second(after):
        second.extend(load(1, tie(where, after), [items["qkv"], items["out"]]))
        return second

    out_first, first_kept, kept_first = layer_forward(
        0,
        rows,
        far_rows,
        first_qkv,
        smalls[0],
        marks,
        where,
        {"out": first_out, "ffn": first_ffn, "next": load_second},
    )
    def second_ffn(after):
        fetched["first"] = lax.ppermute(first_kept, "pipe", [(1, 0)])
        return load_ffn(1, (), tie(after, fetched["first"]))

    out_second, second_kept, kept_second = layer_forward(
        1,
        out_first,
        chip_swap(out_first),
        second[0],
        smalls[1],
        marks,
        where,
        {
            "out": lambda after: second[1],
            "ffn": second_ffn,
            "next": lambda after: (),
        },
    )

    def loads(layer):
        return {
            "out": partial(load_one, layer, "out"),
            "qkv": partial(load_one, layer, "qkv"),
            "ffn": partial(load_ffn, layer),
            "rows": load_rows,
        }

    def place_outputs(first, second, first_got, second_got, after):
        return call(
            place_kernel,
            [("h", shape((1, 2) + first.shape))],
            [("s", after)] + [("v", value) for value in (first, second, first_got, second_got)],
            scratch=[pltpu.VMEM((2,) + first.shape, BF16)],
            copies=1,
        )[0]

    sums, steps = {}, {}

    def begin(name, owner, *pieces):
        sums[name] = Sum(owner, *pieces)
        steps[name] = sums[name].steps()

    def run(name, after):
        return steps[name].pop(0)(tie(where, after)) if steps[name] else after

    upstream = lax.dynamic_index_in_dim(cotangent, section, 0, keepdims=False)
    outputs = []

    def later_df(after):
        second_got = lax.ppermute(second_kept, "pipe", [(0, 1)])
        outputs.append(
            place_outputs(first_kept, second_kept, fetched["first"], second_got, tie(where, after))
        )
        return (outputs[0],)

    def later_dz(after, parts):
        begin("ab1", 1, parts[0:2], parts[2:4])
        return (sums["ab1"].got[0],)

    grads, _, small_second, attn_second, _ = layer_backward(
        1,
        (upstream,),
        kept_second,
        smalls[1],
        marks,
        where,
        loads(1),
        {"df": later_df, "dh": lambda after: (), "dz": later_dz},
    )
    sent, kept = split(where, *attn_second)
    begin("c1", 1, (sent, kept))
    grads = (tie(grads[0], run("ab1", sent)),) + grads[1:]

    def first_df(after):
        one = run("ab1", after)
        return (run("c1", one),)

    def first_dh(after):
        one = run("ab1", after)
        return (run("c1", one),)

    def first_dz(after, parts):
        begin("a0", 0, parts[0:2])
        begin("b0", 0, parts[2:4])
        one = run("ab1", after)
        one = run("c1", one)
        return (run("a0", one),)

    grads, (grad_second,), small_first, attn_first, _ = layer_backward(
        0,
        grads,
        kept_first,
        smalls[0],
        marks,
        where,
        loads(0),
        {"df": first_df, "dh": first_dh, "dz": first_dz},
    )
    order = [attn_first[0]]

    def now():
        return tie(where, order[-1])

    def step(*names):
        for name in names:
            order.append(run(name, order[-1]))

    def small_add(total, got):
        total, shared = call(
            small_add_kernel,
            [("v", shape((16, width), F32))] * 2,
            [("s", now()), ("v", total), ("v", got)],
        )
        order.append(total)
        return total, shared

    sent, kept = split(now(), *attn_first)
    order.append(sent)
    begin("c0", 0, (sent, kept))
    total, pair_sums = call(
        pack_sums_kernel,
        [("v", shape((16, width), F32))] * 2,
        [("s", now())] + [("v", value) for value in (*small_first, *small_second)],
    )
    order.append(total)
    got = core_swap(pair_sums)
    step("a0", "c1", "b0")
    total, shared = small_add(total, got)
    got = chip_swap(shared)
    step("ab1")
    sums["ab1"].finish()
    (grad_first,) = call(
        grad_in_kernel, [("v", shape(rows.shape))], [("s", now())] + [("v", value) for value in grads]
    )
    order.append(grad_first)
    first_got = lax.ppermute(grad_first, "pipe", [(1, 0)])
    second_got = lax.ppermute(grad_second, "pipe", [(0, 1)])
    total, _ = small_add(total, got)
    hops = [("pipe", 1)]
    count = lax.axis_size("dp")
    if count & (count - 1):
        total = lax.psum(total, "dp")
    else:
        hops += [("dp", 1 << bit) for bit in range(count.bit_length() - 1)]
    got = swap(total, *hops[0])
    step("a0", "b0")
    for hop in hops[1:]:
        total, _ = small_add(total, got)
        got = swap(total, *hop)
        step("c0", "a0", "b0")
    while steps["c1"]:
        step("c1")
    sums["c1"].finish()
    for name in ("a0", "b0"):
        while steps[name]:
            step(name, "c0")
        sums[name].finish()
    while steps["c0"]:
        step("c0")
    sums["c0"].finish()
    outs = [shape(item.shape, F32) for item in (norm_gain, shift_bias, up_bias, qkv_bias)]
    gains, shifts, upb, qkvb = call(
        small_results_kernel,
        [("h", item) for item in outs],
        [("s", now()), ("v", total), ("v", got)],
        scratch=[pltpu.VMEM(item.shape, F32) for item in outs],
        copies=4,
    )
    layer_out = outputs[0]
    input_grad = place_outputs(grad_first, grad_second, first_got, second_got, tie(where, gains))

    def pieces(second, *names):
        first = [sums[name].total for name in names] + [sums[name].other for name in names]
        return first, [sums[second].other, sums[second].total]

    upw, downw = results("ffn", tie(where, input_grad), *pieces("ab1", "a0", "b0"))
    qkvw, outw = results("attn", tie(where, upw), *pieces("c1", "c0"))
    qkvw = jnp.transpose(qkvw, (0, 2, 1))
    return (
        layer_out,
        input_grad,
        qkvw[None],
        qkvb,
        outw[None],
        upw[None],
        upb,
        downw[None],
        gains,
        shifts,
    )


def solution(mesh):
    return jax.shard_map(
        body,
        mesh=mesh,
        in_specs=(
            P("dp", "tensor", None),
            P("dp", None),
            P("dp", None),
            P("pipe", "tensor", None),
            P("pipe", None, None, "tensor"),
            P("pipe", None, "tensor"),
            P("pipe", "tensor", None),
            P("pipe", None, "tensor"),
            P("pipe", "tensor"),
            P("pipe", "tensor", None),
            P("pipe", None, None),
            P("pipe", None, None),
            P("dp", "tensor", None),
        ),
        out_specs=(
            P("pipe", "dp", "tensor", None),
            P("pipe", "dp", "tensor", None),
            P("pipe", None, None, "tensor"),
            P("pipe", None, "tensor"),
            P("pipe", "tensor", None),
            P("pipe", None, "tensor"),
            P("pipe", "tensor"),
            P("pipe", "tensor", None),
            P("pipe", None, None),
            P("pipe", None, None),
        ),
        check_vma=False,
    )
```

```python
from functools import partial

import jax
import jax.numpy as jnp
from jax import lax
from jax.experimental import pallas as pl
from jax.experimental.pallas import tpu as pltpu
from jax.sharding import PartitionSpec as P

BF16 = jnp.bfloat16
F32 = jnp.float32
HEAD_DIM = 64
PAIR = 2 * HEAD_DIM
LOG2E = 1.4426950408889634
MASKED = -1e30
VMEM_LIMIT = 16 * 1024 * 1024
COST = 2e10
NORM_EPSILON_TERM = 1e-06

FLAGS = 5

SPACES = {"v": pltpu.VMEM, "s": pltpu.SMEM, "h": pl.ANY}
PLACES = {"v": pltpu.VMEM, "s": pl.ANY, "h": pltpu.HBM}


def shape(dims, dtype=BF16):
    return jax.ShapeDtypeStruct(dims, dtype)


def call(kernel, outs, args, us=0.1, scratch=(), copies=0):
    flops = int(us * COST)
    scratch = list(scratch)
    if copies:
        scratch.append(pltpu.SemaphoreType.DMA((copies,)))
    return pl.pallas_call(
        kernel,
        name=(kernel.func if isinstance(kernel, partial) else kernel).__name__,
        out_shape=[PLACES[space](item.shape, item.dtype) for space, item in outs],
        in_specs=[pl.BlockSpec(memory_space=SPACES[space]) for space, _ in args],
        out_specs=[pl.BlockSpec(memory_space=SPACES[space]) for space, _ in outs],
        scratch_shapes=scratch,
        compiler_params=pltpu.CompilerParams(vmem_limit_bytes=VMEM_LIMIT),
        cost_estimate=pl.CostEstimate(flops=flops, bytes_accessed=0, transcendentals=0),
    )(*[pltpu.with_memory_space_constraint(item, PLACES[space]) for space, item in args])


class Copies:
    def __init__(self, sems):
        self.sems, self.pending = sems, []

    def start(self, source, target):
        copy = pltpu.make_async_copy(source, target, self.sems.at[len(self.pending)])
        copy.start()
        self.pending.append(copy)

    def start_one(self, cases, target):
        sem = self.sems.at[len(self.pending)]
        made = []
        for condition, source in cases:
            made.append(pltpu.make_async_copy(source, target, sem))
            pl.when(condition)(made[-1].start)
        self.pending.append(made[0])

    def done(self):
        for copy in self.pending:
            copy.wait()


def loop(count, step):
    lax.fori_loop(0, count, lambda i, _: step(i), None)


def part_of(i, size):
    return pl.ds(pl.multiple_of(i * size, size), size)


def dot(left, right):
    return jnp.dot(left, right, preferred_element_type=F32)


def dot_tn(left, right):
    return lax.dot_general(left, right, (((0,), (0,)), ((), ())), preferred_element_type=F32)


def dot_nt(left, right):
    return lax.dot_general(left, right, (((1,), (1,)), ((), ())), preferred_element_type=F32)


def pack_kernel(gains_in, shifts_in, up_in, qkv_in, perm_ref, out_ref, gains, shifts, up, qkv_b, sems):
    copies = Copies(sems)
    for source, target in ((gains_in, gains), (shifts_in, shifts), (up_in, up), (qkv_in, qkv_b)):
        copies.start(source, target)
    out_ref[...] = jnp.zeros_like(out_ref)
    lane = lax.broadcasted_iota(jnp.int32, (1, out_ref.shape[1]), 1)
    flags = jnp.zeros((1, out_ref.shape[1]), F32)
    for head in range(perm_ref.shape[1]):
        flags = jnp.where(lane == head, perm_ref[0, head, 0].astype(F32), flags)
    out_ref[9:10] = flags
    copies.done()
    out_ref[0:2] = gains[0]
    out_ref[2:6] = shifts[0]
    out_ref[6:7] = up[...].astype(F32)
    out_ref[7:9, 0 : qkv_b.shape[2]] = qkv_b[0].astype(F32)


GAIN1, GAIN2, BIAS_OUT, SHIFT1, BIAS2, SHIFT2, BIAS_UP, BIAS_Q, TURNED = 0, 1, 2, 3, 4, 5, 6, 8, 10


def params_kernel(where_ref, own_ref, other_ref, pair_ref, other_pair_ref, first_out, second_out, flags_copy, flags, sems):
    section, core = where_ref[0], where_ref[1]
    width = own_ref.shape[1]
    local = width // 4
    heads = local // HEAD_DIM
    lane = lax.broadcasted_iota(jnp.int32, (1, width), 1)
    flags[...] = jnp.zeros_like(flags)
    for layer, out_ref in enumerate((first_out, second_out)):
        here = section == layer
        mine = jnp.where(here, own_ref[...], other_ref[...])
        pair = jnp.where(here, pair_ref[...], other_pair_ref[...])
        first = jnp.where(core == 0, mine, pair)
        second = jnp.where(core == 0, pair, mine)
        out_ref[...] = mine
        out_ref[BIAS_UP + 1 : BIAS_UP + 2] = pair[BIAS_UP : BIAS_UP + 1]
        biases = jnp.where(lane < local, first, pltpu.roll(second, local, 1))
        out_ref[BIAS_Q : BIAS_Q + 2] = biases[7:9]
        turned = jnp.where(lane < heads, first, pltpu.roll(second, heads, 1))[9:10]
        lanes = jnp.zeros((1, width), F32)
        for head in range(2 * heads):
            chosen = (lane // HEAD_DIM) % (2 * heads) == head
            lanes = jnp.where(chosen, turned[:, head : head + 1], lanes)
        out_ref[TURNED : TURNED + 1] = lanes
        flags[layer : layer + 1] = turned[:, 0:PAIR]
    copies = Copies(sems)
    copies.start(flags, flags_copy)
    copies.done()


def marks_kernel(where_ref, segments_ref, real_ref, out_ref):
    quarter = out_ref.shape[1] // 2
    out_ref[...] = jnp.zeros_like(out_ref)
    for r in range(4):
        cols = pl.ds(pl.multiple_of((where_ref[4] ^ r) * quarter, PAIR), quarter)
        at = slice((r % 2) * quarter, (r % 2 + 1) * quarter)
        segment = jnp.where(where_ref[0] == 0, segments_ref[0:1, cols], segments_ref[1:2, cols])
        real = jnp.where(where_ref[0] == 0, real_ref[0:1, cols], real_ref[1:2, cols])
        out_ref[1 + r // 2 : 2 + r // 2, at] = jnp.where(real == 1, segment, -1)
        if r % 2 == 0:
            out_ref[0:1, (r // 2) * quarter : (r // 2 + 1) * quarter] = segment


def halve_kernel(where_ref, *refs):
    count = len(refs) // 2
    copies = Copies(refs[-1])
    for source, half in zip(refs[:count], refs[count:-1]):
        columns = half.shape[2]
        copies.start_one(
            [
                (where_ref[2] == side, source.at[:, :, pl.ds(side * columns, columns)])
                for side in range(2)
            ],
            half,
        )
    copies.done()


def halves_of(where, *wholes):
    return call(
        halve_kernel,
        [("v", shape(whole.shape[:2] + (whole.shape[2] // 2,))) for whole in wholes],
        [("s", where)] + [("h", whole) for whole in wholes],
        copies=len(wholes),
    )


def weight_copies(copies, where_ref, layer, k, own, other, target):
    here = where_ref[0] == layer
    if len(other) == 1:
        copies.start_one(
            [(here, own.at[k]), (jnp.logical_not(here), other[0].at[k])], target(slice(None))
        )
        return
    columns = other[0].shape[-1]
    for side in range(2):
        cols = pl.ds(side * columns, columns)
        direct = where_ref[2] == side
        copies.start_one(
            [
                (here, own.at[k, :, cols]),
                (jnp.logical_not(here) & direct, other[0].at[k]),
                (jnp.logical_not(here) & jnp.logical_not(direct), other[1].at[k]),
            ],
            target(cols),
        )


def load_kernel(layer, items, plain, where_ref, *refs):
    sems = refs[-1]
    copies = Copies(sems)
    count = sum(2 * (1 + parts) for _, parts in items)
    sources, plain_in, outs = refs[:count], refs[count : count + plain], refs[count + plain : -1]
    for (by_core, parts), out_ref in zip(items, outs):
        for pair in range(2):
            own, *other = sources[: 1 + parts]
            sources = sources[1 + parts :]
            if by_core:
                rows = out_ref.shape[1] // 2
                slot = (where_ref[1] + pair) % 2
                at = pl.ds(pl.multiple_of(slot * rows, rows), rows)
                for k in range(out_ref.shape[0]):
                    weight_copies(
                        copies, where_ref, layer, k, own, other, lambda cols, k=k: out_ref.at[k, at, cols]
                    )
            else:
                weight_copies(
                    copies, where_ref, layer, 0, own, other, lambda cols: out_ref.at[pair, :, cols]
                )
    for source, target in zip(plain_in, outs[len(items) :]):
        copies.start(source, target)
    copies.done()


def load(layer, where, items, arrays=()):
    outs, sources, kinds, count = [], [], [], len(arrays)
    for by_core, own, other, pair_own, pair_other in items:
        k, rows, columns = own.shape
        outs.append(shape((k, 2 * rows, columns)) if by_core else shape((2, rows, columns)))
        sources += [own, *other, pair_own, *pair_other]
        kinds.append((by_core, len(other)))
        count += 2 * k * len(other)
    outs += [shape(item.shape, item.dtype) for item in arrays]
    return call(
        partial(load_kernel, layer, kinds, len(arrays)),
        [("v", item) for item in outs],
        [("s", where)] + [("h", item) for item in (*sources, *arrays)],
        us=2.4,
        copies=count,
    )


def qkv_kernel(x_ref, w_ref, b_ref, q_ref, kv_ref, x_copy, q_copy, sems):
    copies = Copies(sems)
    copies.start(x_ref, x_copy)
    x = x_ref[...]
    width = q_ref.shape[1]
    q_ref[...] = (dot_nt(x, w_ref[0]) + b_ref[BIAS_Q : BIAS_Q + 1, :width]).astype(BF16)
    copies.start(q_ref, q_copy)
    kv_ref[:, :width] = dot_nt(x, w_ref[1]).astype(BF16)
    kv_ref[:, width:] = (dot_nt(x, w_ref[2]) + b_ref[BIAS_Q + 1 : BIAS_Q + 2, :width]).astype(BF16)
    copies.done()


def qkv(x, w, b):
    rows, width = x.shape[0], w.shape[1]
    return call(
        qkv_kernel,
        [
            ("v", shape((rows, width))),
            ("v", shape((rows, 2 * width))),
            ("h", shape(x.shape)),
            ("h", shape((rows, width))),
        ],
        [("v", x), ("v", w), ("v", b)],
        1.1,
        copies=2,
    )


def lanes_of(rows):
    return lax.broadcasted_iota(jnp.int32, (rows, PAIR), 1)


def fill_bias(bias, side, marks_ref):
    rows = bias.shape[1]
    wanted = jnp.transpose(marks_ref[:, side * rows : (side + 1) * rows])[:, 0:1]
    for j in range(2):
        bias[j] = jnp.where(wanted == marks_ref[1 + j : 2 + j, :], 0.0, MASKED).astype(F32)


def block_of(where_ref, layer, head, turned):
    return where_ref[FLAGS + 6 * layer + head] ^ turned


def attn_rows(layer, where_ref, turned, q_ref, kv_ref, marks_ref, o_ref, lse_ref, bias):
    rows, width = q_ref.shape
    fill_bias(bias, turned, marks_ref)
    lanes = lanes_of(rows)
    low = lanes < HEAD_DIM
    scale = HEAD_DIM**-0.5 * LOG2E
    lse_ref[...] = jnp.zeros_like(lse_ref)

    def step(tile):
        cols, vcols = part_of(tile, PAIR), part_of(tile + width // PAIR, PAIR)
        q = q_ref[:, cols]
        mixed = []
        for side in range(2):
            head = 2 * tile + side
            block = block_of(where_ref, layer, head, turned)
            q_head = jnp.where(low if side == 0 else ~low, q, jnp.zeros_like(q))
            s = dot_nt(q_head, kv_ref[block, :, cols]) * scale + bias[block]
            top = jnp.maximum(jnp.max(s, axis=1, keepdims=True), 0.0)
            e = jnp.exp2(s - top)
            total = jnp.exp2(-top) + jnp.sum(e, axis=1, keepdims=True)
            p = (e * (1.0 / total)).astype(BF16)
            mixed.append(dot(p, kv_ref[block, :, vcols]))
            lse_ref[...] = jnp.where(lanes == head, top + jnp.log2(total), lse_ref[...])
        o_ref[:, cols] = jnp.where(low, mixed[0], mixed[1]).astype(BF16)

    loop(width // PAIR, step)


def attn_far_kernel(
    layer, where_ref, q_ref, kv0_ref, kv1_ref, kv2_ref, kv3_ref, marks_ref, w_ref,
    out_ref, kv_ref, kv_copy, o_copy, lse_copy, bias, o_ref, lse_ref, sems,
):
    copies = Copies(sems)
    half = kv0_ref.shape[0]
    for block, pair in enumerate(((kv0_ref, kv1_ref), (kv2_ref, kv3_ref))):
        kv_ref[block, :half] = pair[0][...]
        kv_ref[block, half:] = pair[1][...]
    copies.start(kv_ref, kv_copy)
    attn_rows(layer, where_ref, 1, q_ref, kv_ref, marks_ref, o_ref, lse_ref, bias)
    copies.start(o_ref, o_copy)
    copies.start(lse_ref, lse_copy)
    out_ref[...] = dot(o_ref[...], w_ref[0]).astype(out_ref.dtype)
    copies.done()


def attn_own_kernel(
    layer, where_ref, q_ref, kv_ref, marks_ref, w_ref, out_ref, o_copy, lse_copy, bias, o_ref, lse_ref, sems
):
    copies = Copies(sems)
    attn_rows(layer, where_ref, 0, q_ref, kv_ref, marks_ref, o_ref, lse_ref, bias)
    copies.start(o_ref, o_copy)
    copies.start(lse_ref, lse_copy)
    out_ref[...] = dot(o_ref[...], w_ref[0]).astype(out_ref.dtype)
    copies.done()


def attn(layer, where, q, kv, marks, w):
    rows, width = q.shape
    far = len(kv) > 1
    outs = [("v", shape((rows, w.shape[2]), BF16 if far else F32))]
    if far:
        joined = shape((2, 2 * rows, kv[0].shape[1]))
        outs += [("v", joined), ("h", joined)]
    outs += [("h", shape((rows, width))), ("h", shape((rows, PAIR), F32))]
    args = [("s", where)] + [("v", item) for item in (q, *kv, marks, w)]
    return call(
        partial(attn_far_kernel if far else attn_own_kernel, layer),
        outs,
        args,
        4.6,
        scratch=[
            pltpu.VMEM((2, rows, 2 * rows), F32),
            pltpu.VMEM((rows, width), BF16),
            pltpu.VMEM((rows, PAIR), F32),
        ],
        copies=3 if far else 2,
    )


def normed_rows(resid):
    centred = resid - jnp.mean(resid, axis=1, keepdims=True)
    inverse = lax.rsqrt(jnp.mean(centred * centred, axis=1, keepdims=True) + NORM_EPSILON_TERM)
    return centred * inverse, inverse


def norm1_kernel(x_ref, own_ref, far_ref, norms_ref, low_ref, full_ref, resid_copy, low_copy, resid, sems):
    copies = Copies(sems)
    projected = own_ref[...] + far_ref[...].astype(F32)
    total = x_ref[...].astype(F32) + projected + norms_ref[BIAS_OUT : BIAS_OUT + 1, :]
    resid[...] = total
    copies.start(resid, resid_copy)
    hidden = normed_rows(total)[0] * norms_ref[GAIN1 : GAIN1 + 1, :] + norms_ref[SHIFT1 : SHIFT1 + 1, :]
    full_ref[...] = hidden
    low_ref[...] = hidden.astype(BF16)
    copies.start(low_ref, low_copy)
    copies.done()


def norm1(x, own, far, norms):
    return call(
        norm1_kernel,
        [("v", shape(x.shape)), ("v", shape(x.shape, F32)), ("h", shape(x.shape, F32)), ("h", shape(x.shape))],
        [("v", x), ("v", own), ("v", far), ("v", norms)],
        scratch=[pltpu.VMEM(x.shape, F32)],
        us=1.2,
        copies=2,
    )


def norm2_kernel(h_ref, own_ref, far_ref, norms_ref, low_ref, resid_copy, low_copy, resid, sems):
    copies = Copies(sems)
    branch = own_ref[...] + far_ref[...].astype(F32)
    total = h_ref[...] + branch + norms_ref[BIAS2 : BIAS2 + 1, :]
    resid[...] = total
    copies.start(resid, resid_copy)
    out = normed_rows(total)[0] * norms_ref[GAIN2 : GAIN2 + 1, :] + norms_ref[SHIFT2 : SHIFT2 + 1, :]
    low_ref[...] = out.astype(BF16)
    copies.start(low_ref, low_copy)
    copies.done()


def norm2(h, own, far, norms):
    return call(
        norm2_kernel,
        [("v", shape(h.shape)), ("h", shape(h.shape, F32)), ("h", shape(h.shape))],
        [("v", h), ("v", own), ("v", far), ("v", norms)],
        scratch=[pltpu.VMEM(h.shape, F32)],
        us=1.2,
        copies=2,
    )


TAIL = tuple(
    0.5 * c
    for c in (
        0.05029408002973294, -0.1830316054165625, 0.16930258232763196, -0.005798692821681883,
        0.14152663657068731, 0.16851528425000623, 0.20784663429852349, 0.22566934002005623,
        0.22567586682378352,
    )
)


def gelu_and_slope(u):
    bell = jnp.exp2(u * u * (-0.5 * LOG2E))
    t = 1.0 / (1.0 + jnp.abs(u) * (0.4 * 0.5**0.5))
    poly = TAIL[0]
    for c in TAIL[1:]:
        poly = poly * t + c
    tail = poly * t * bell
    below = jnp.where(u < 0.0, tail, 1.0 - tail)
    return u * below, below + u * bell * 0.3989422804014327


UNITS = 768


def ffn_kernel(far, h_ref, up_ref, down_ref, b_ref, out_ref, act_copy, slope_copy, *rest):
    act_ref, slope_ref, total_ref, sems = rest[-4:]
    steps = up_ref.shape[2] // UNITS
    if far:
        rows_copy = pltpu.make_async_copy(h_ref, rest[0], sems.at[4 * steps])
        rows_copy.start()
    total_ref[...] = jnp.zeros_like(total_ref)

    def copies_of(i):
        half, cols = i // steps, part_of(i % steps, UNITS)
        return [
            pltpu.make_async_copy(kept.at[half, :, cols], copy.at[half, :, cols], sems.at[2 * i + k])
            for k, (kept, copy) in enumerate(((act_ref, act_copy), (slope_ref, slope_copy)))
        ]

    def step(i):
        half, cols = i // steps, part_of(i % steps, UNITS)
        pre = dot(h_ref[...], up_ref[half, :, cols]) + b_ref[pl.ds(BIAS_UP + half, 1), cols]
        act, slope = gelu_and_slope(pre)
        act = act.astype(BF16)
        act_ref[half, :, cols] = act
        slope_ref[half, :, cols] = slope.astype(BF16)
        for copy in copies_of(i):
            copy.start()
        total_ref[...] += dot(act, down_ref[half, cols, :])

    loop(2 * steps, step)
    out_ref[...] = total_ref[...].astype(out_ref.dtype)

    def finish(i):
        for copy in copies_of(i):
            copy.wait()

    loop(2 * steps, finish)
    if far:
        rows_copy.wait()


def ffn(h, up, down, b, far):
    rows, width = h.shape
    units = up.shape[2]
    outs = [
        ("v", shape((rows, width), BF16 if far else F32)),
        ("h", shape((2, rows, units))),
        ("h", shape((2, rows, units))),
    ]
    if far:
        outs.append(("h", shape(h.shape)))
    return call(
        partial(ffn_kernel, far),
        outs,
        [("v", h), ("v", up), ("v", down), ("v", b)],
        3.5,
        scratch=[pltpu.VMEM((2, rows, units), BF16)] * 2 + [pltpu.VMEM((rows, width), F32)],
        copies=4 * (units // UNITS) + 1,
    )


def norm_back(upstream, resid, gain, low_ref, full_ref, sums_ref):
    normed, inverse = normed_rows(resid)
    scaled = upstream * gain
    inner = (
        scaled
        - jnp.mean(scaled, axis=1, keepdims=True)
        - normed * jnp.mean(scaled * normed, axis=1, keepdims=True)
    )
    grad = inverse * inner
    full_ref[...] = grad
    low_ref[...] = grad.astype(BF16)
    sums_ref[...] = jnp.zeros_like(sums_ref)
    sums_ref[0:1] = jnp.sum(upstream * normed, axis=0, keepdims=True)
    sums_ref[1:2] = jnp.sum(upstream, axis=0, keepdims=True)
    sums_ref[2:3] = jnp.sum(grad, axis=0, keepdims=True)


def norm2_back_kernel(inner, *refs):
    if inner:
        own_ref, far_ref, resid1_ref, resid_in, norms_ref, low_ref, full_ref, sums_ref, grad_ref, resid, sems = refs
    else:
        up_ref, resid_in, norms_ref, low_ref, full_ref, sums_ref, resid, sems = refs
    copies = Copies(sems)
    copies.start(resid_in, resid)
    if inner:
        grad_in = (own_ref[...] + far_ref[...].astype(F32) + resid1_ref[...]).astype(BF16)
        grad_ref[...] = grad_in
    else:
        grad_in = up_ref[...]
    copies.done()
    gain = norms_ref[GAIN2 : GAIN2 + 1, :]
    norm_back(grad_in.astype(F32), resid[...], gain, low_ref, full_ref, sums_ref)


def norm2_back(upstream, resid, norms):
    dims = upstream[0].shape
    inner = len(upstream) > 1
    outs = [("v", shape(dims)), ("v", shape(dims, F32)), ("v", shape((8, dims[1]), F32))]
    if inner:
        outs.append(("v", shape(dims)))
    return call(
        partial(norm2_back_kernel, inner),
        outs,
        [("v", item) for item in upstream] + [("h", resid), ("v", norms)],
        scratch=[pltpu.VMEM(dims, F32)],
        us=1.7,
        copies=1,
    )


def norm1_back_kernel(own_ref, far_ref, skip_ref, resid_in, norms_ref, low_ref, full_ref, sums_ref, resid, sems):
    copies = Copies(sems)
    copies.start(resid_in, resid)
    upstream = own_ref[...] + far_ref[...].astype(F32) + skip_ref[...]
    copies.done()
    gain = norms_ref[GAIN1 : GAIN1 + 1, :]
    norm_back(upstream, resid[...], gain, low_ref, full_ref, sums_ref)


def norm1_back(own, far, skip, resid, norms):
    dims = own.shape
    return call(
        norm1_back_kernel,
        [("v", shape(dims)), ("v", shape(dims, F32)), ("v", shape((8, dims[1]), F32))],
        [("v", own), ("v", far), ("v", skip), ("h", resid), ("v", norms)],
        scratch=[pltpu.VMEM(dims, F32)],
        us=1.7,
        copies=1,
    )


def ffn_back_kernel(df_ref, slope_ref, up_ref, down_ref, dh_ref, du_ref, db_ref, total_ref):
    units = up_ref.shape[2]
    steps = units // UNITS
    total_ref[...] = jnp.zeros_like(total_ref)

    def step(i):
        half, cols = i // steps, part_of(i % steps, UNITS)
        du = dot_nt(df_ref[...], down_ref[half, cols, :]) * slope_ref[half, :, cols].astype(F32)
        du = du.astype(BF16)
        du_ref[:, part_of(i, UNITS)] = du
        db_ref[pl.ds(half, 1), cols] = jnp.sum(du.astype(F32), axis=0, keepdims=True)
        total_ref[...] += dot_nt(du, up_ref[half, :, cols])

    loop(2 * steps, step)
    dh_ref[...] = total_ref[...].astype(dh_ref.dtype)


def ffn_back(df, slope, up, down, far):
    rows, width = df.shape
    units = 2 * up.shape[2]
    return call(
        ffn_back_kernel,
        [
            ("v", shape((rows, width), BF16 if far else F32)),
            ("v", shape((rows, units))),
            ("v", shape((2, units // 2), F32)),
        ],
        [("v", df), ("v", slope), ("v", up), ("v", down)],
        1.8,
        scratch=[pltpu.VMEM((rows, width), F32)],
    )


def ffn_grads_of(half, h, act, df, du):
    units = act[0].shape[2]
    cols = slice(half * units, (half + 1) * units)
    up = dot_tn(h[0][...], du[0][:, cols]) + dot_tn(h[1][...], du[1][:, cols])
    down = dot_tn(act[0][half], df[0][...]) + dot_tn(act[1][half], df[1][...])
    return up, down


def ffn_pair_kernel(h0, h1, a0, a1, df0, df1, du0, du1, up_ref, down_ref):
    up, down = ffn_grads_of(1, (h0, h1), (a0, a1), (df0, df1), (du0, du1))
    up_ref[...] = up.astype(BF16)
    down_ref[...] = down.astype(BF16)


def ffn_own_kernel(where_ref, h0, h1, a0, a1, df0, df1, du0, du1, up_got, down_got, *outs):
    up, down = ffn_grads_of(0, (h0, h1), (a0, a1), (df0, df1), (du0, du1))
    up += up_got[...].astype(F32)
    down += down_got[...].astype(F32)
    first = where_ref[0] == 0
    half = outs[0].shape[0]
    for part in range(2):
        rows = slice(part * half, (part + 1) * half)
        outs[2 * part][...] = jnp.where(first, down[rows], up[rows]).astype(BF16)
        outs[2 * part + 1][...] = jnp.where(first, up[rows], down[rows])


def ffn_pair(args):
    rows, width = args[0].shape
    units = args[2].shape[2]
    return call(
        ffn_pair_kernel,
        [("v", shape((width, units)))] * 2,
        [("v", item) for item in args],
        1.4,
    )


def ffn_own(where, args, got):
    rows, width = args[0].shape
    units = args[2].shape[2]
    return call(
        ffn_own_kernel,
        [("v", shape((width // 2, units))), ("v", shape((width // 2, units), F32))] * 2,
        [("s", where)] + [("v", item) for item in (*args, *got)],
        2.2,
    )


def attn_back_kernel(
    layer, turned, where_ref, dz_ref, q_ref, kv_ref, marks_ref, lse_ref, w_ref,
    dq_ref, dkv_ref, dkv_pair_ref, bias, do_ref,
):
    rows, width = q_ref.shape
    fill_bias(bias, turned, marks_ref)
    low = lanes_of(rows) < HEAD_DIM
    scale = HEAD_DIM**-0.5
    do_ref[...] = dot_nt(dz_ref[...], w_ref[0]).astype(BF16)
    lanes = lanes_of(rows)
    tiles = width // PAIR

    def step(tile):
        cols, vcols = part_of(tile, PAIR), part_of(tile + tiles, PAIR)
        q, do = q_ref[:, cols], do_ref[:, cols]
        dq, dk, dv = [], 0.0, 0.0
        for side in range(2):
            head = 2 * tile + side
            block = block_of(where_ref, layer, head, turned)
            part = low if side == 0 else ~low
            q_head = jnp.where(part, q, jnp.zeros_like(q))
            do_head = jnp.where(part, do, jnp.zeros_like(do))
            k = kv_ref[block, :, cols]
            s = dot_nt(q_head, k) * (scale * LOG2E) + bias[block]
            log_total = jnp.sum(jnp.where(lanes == head, lse_ref[...], 0.0), axis=1, keepdims=True)
            p = jnp.exp2(s - log_total)
            dp = dot_nt(do_head, kv_ref[block, :, vcols])
            centre = jnp.sum(p * dp, axis=1, keepdims=True)
            ds = (p * (dp - centre)).astype(BF16)
            dq.append(dot(ds, k))
            dv += dot_tn(p.astype(BF16), do_head)
            dk += dot_tn(ds, q_head)
        dq_ref[:, cols] = (jnp.where(low, dq[0], dq[1]) * scale).astype(BF16)
        dkv_ref[:, cols] = dk[:rows] * scale
        dkv_ref[:, vcols] = dv[:rows]
        dkv_pair_ref[:, cols] = (dk[rows:] * scale).astype(BF16)
        dkv_pair_ref[:, vcols] = dv[rows:].astype(BF16)

    loop(tiles, step)


def attn_back(layer, turned, where, dz, q, kv, marks, lse, w):
    rows, width = q.shape
    return call(
        partial(attn_back_kernel, layer, turned),
        [("v", shape((rows, width))), ("v", shape((rows, 2 * width), F32)), ("v", shape((rows, 2 * width)))],
        [("s", where)] + [("v", item) for item in (dz, q, kv, marks, lse, w)],
        4.4,
        scratch=[pltpu.VMEM((2, rows, 2 * rows), F32), pltpu.VMEM((rows, width), BF16)],
    )


def row_grads_kernel(
    small_ref, dq0_ref, dq1_ref, kv0_ref, kv1_ref, pair0_ref, pair1_ref, w_ref, dx_ref, d0_ref, d1_ref
):
    width = dq0_ref.shape[1]
    turned = small_ref[TURNED : TURNED + 1, :] == 1.0
    near = kv0_ref[...] + pair0_ref[...].astype(F32)
    far = kv1_ref[...] + pair1_ref[...].astype(F32)
    d0_ref[:, :width] = dq0_ref[...]
    d1_ref[:, :width] = dq1_ref[...]
    d0_ref[:, width:] = jnp.where(turned, far, near).astype(BF16)
    d1_ref[:, width:] = jnp.where(turned, near, far).astype(BF16)
    total = None
    for k in range(3):
        part = dot(d1_ref[:, k * width : (k + 1) * width], w_ref[k])
        total = part if total is None else total + part
    dx_ref[...] = total.astype(BF16)


def row_grads(small, dq, kv, pair, w):
    rows, width = dq[0].shape
    return call(
        row_grads_kernel,
        [("v", shape((rows, w.shape[2])))] + [("v", shape((rows, 3 * width)))] * 2,
        [("v", item) for item in (small, *dq, *kv, *pair, w)],
        0.9,
    )


def attn_grads_kernel(
    where_ref, d0_ref, d1_ref, x0_ref, x1_ref, o0_ref, o1_ref, dz0_ref, dz1_ref, w_ref,
    dx_ref, own_ref, pair_ref, db_ref,
):
    width = o0_ref.shape[1]
    first_core = where_ref[1] == 0
    share = width // 2
    db_ref[...] = jnp.zeros_like(db_ref)
    for k in range(4):
        cols = slice(k * width, (k + 1) * width)
        if k < 3:
            left, right = (d0_ref[:, cols], d1_ref[:, cols]), (x0_ref[...], x1_ref[...])
        else:
            left, right = (o0_ref[...], o1_ref[...]), (dz0_ref[...], dz1_ref[...])
        if k in (0, 2):
            sums = jnp.sum(left[0].astype(F32), axis=0, keepdims=True)
            sums += jnp.sum(left[1].astype(F32), axis=0, keepdims=True)
            db_ref[0:1, k // 2 * width : (k // 2 + 1) * width] = sums
        both = dot_tn(left[0], right[0]) + dot_tn(left[1], right[1])
        rows = slice(k * share, (k + 1) * share)
        own_ref[rows] = jnp.where(first_core, both[:share], both[share:])
        pair_ref[rows] = jnp.where(first_core, both[share:], both[:share]).astype(BF16)
    total = None
    for k in range(3):
        part = dot(d0_ref[:, k * width : (k + 1) * width], w_ref[k])
        total = part if total is None else total + part
    dx_ref[...] = total


def attn_grads(where, d, x, o, dz, w):
    rows, width = o[0].shape
    columns = x[0].shape[1]
    return call(
        attn_grads_kernel,
        [
            ("v", shape((rows, columns), F32)),
            ("v", shape((2 * width, columns), F32)),
            ("v", shape((2 * width, columns))),
            ("v", shape((8, 2 * width), F32)),
        ],
        [("s", where)] + [("v", item) for item in (*d, *x, *o, *dz, w)],
        2.7,
    )


def split_kernel(where_ref, own_ref, got_ref, sent_ref, kept_ref):
    half = kept_ref.shape[0]
    first = where_ref[0] == 0
    top = own_ref[:half] + got_ref[:half].astype(F32)
    bottom = own_ref[half:] + got_ref[half:].astype(F32)
    kept_ref[...] = jnp.where(first, top, bottom)
    sent_ref[...] = jnp.where(first, bottom, top).astype(BF16)


def split(where, own, got):
    rows, columns = own.shape
    return call(
        split_kernel,
        [("v", shape((rows // 2, columns))), ("v", shape((rows // 2, columns), F32))],
        [("s", where), ("v", own), ("v", got)],
    )


def add_kernel(where_ref, *refs):
    parts, out_ref = len(refs) // 2, refs[-1]
    rows = refs[0].shape[0]
    for part in range(parts):
        total = refs[part][...] + refs[parts + part][...].astype(F32)
        out_ref[part * rows : (part + 1) * rows] = total.astype(BF16)


def halve_sum_kernel(bit, parts, where_ref, *refs):
    kept, got, (sent_ref, own_ref) = refs[:parts], refs[parts : 2 * parts], refs[2 * parts :]
    mine = (where_ref[3] >> bit) & 1
    if parts == 2:
        for half in range(2):
            total = kept[half][...] + got[half][...].astype(F32)

            @pl.when(mine == half)
            def _():
                own_ref[...] = total

            @pl.when(mine != half)
            def _():
                sent_ref[...] = total.astype(BF16)

        return
    rows = own_ref.shape[0]
    at = pl.ds(pl.multiple_of(mine * rows, 16), rows)
    own_ref[...] = kept[0][at] + got[0][at].astype(F32)
    at = pl.ds(pl.multiple_of((1 - mine) * rows, 16), rows)
    sent_ref[...] = (kept[0][at] + got[0][at].astype(F32)).astype(BF16)


def join_kernel(bit, where_ref, own_ref, got_ref, out_ref):
    rows = own_ref.shape[0]
    mine = (where_ref[3] >> bit) & 1
    out_ref[pl.ds(pl.multiple_of(mine * rows, 16), rows)] = own_ref[...]
    out_ref[pl.ds(pl.multiple_of((1 - mine) * rows, 16), rows)] = got_ref[...]


def results_kernel(kind, where_ref, *refs):
    *pieces, first_ref, second_ref, buffer, sems = refs
    copies = Copies(sems)
    first = where_ref[0] == 0
    rows = buffer.shape[1]
    half = rows // 2
    count = len(pieces) - 2
    for side in range(2):
        for part in range(2):
            at = slice(part * half, (part + 1) * half)
            ours = pieces[2 * side + part][...] if count == 4 else pieces[side][at]
            values = jnp.where(first, ours, pieces[count + side][at]).astype(F32)
            buffer[side, at] = values
            if kind == "ffn":
                target = (first_ref, second_ref)[side].at[pl.ds(part * half, half)]
            else:
                k = 2 * side + part
                target = first_ref.at[k] if k < 3 else second_ref
            copies.start(buffer.at[side, pl.ds(part * half, half)], target)
    copies.done()


def results(kind, where, first, second):
    rows, columns = second[0].shape
    if kind == "attn":
        outs = [shape((3, rows // 2, columns), F32), shape((rows // 2, columns), F32)]
    else:
        outs = [shape((rows, columns), F32)] * 2
    return call(
        partial(results_kernel, kind),
        [("h", item) for item in outs],
        [("s", where)] + [("v", item) for item in (*first, *second)],
        scratch=[pltpu.VMEM((2, rows, columns), F32)],
        us=2.5,
        copies=4,
    )


def place_kernel(where_ref, first_ref, second_ref, first_got, second_got, out_ref, buffer, sems):
    copies = Copies(sems)
    first = where_ref[0] == 0
    buffer[0] = jnp.where(first, first_ref[...], second_got[...])
    buffer[1] = jnp.where(first, first_got[...], second_ref[...])
    copies.start(buffer, out_ref.at[0])
    copies.done()


def grad_in_kernel(where_ref, own_ref, far_ref, skip_ref, out_ref):
    out_ref[...] = (own_ref[...] + far_ref[...].astype(F32) + skip_ref[...]).astype(BF16)


def pack_sums_kernel(where_ref, *refs):
    own_ref, pair_ref = refs[-2:]
    for layer in range(2):
        norm1_ref, norm2_ref, up0_ref, up1_ref, qkv_ref = refs[5 * layer : 5 * layer + 5]
        at = 8 * layer
        for row, source in (
            (GAIN1, norm1_ref[0:1]),
            (GAIN2, norm2_ref[0:1]),
            (BIAS_OUT, norm1_ref[2:3]),
            (SHIFT1, norm1_ref[1:2]),
            (BIAS2, norm2_ref[2:3]),
            (SHIFT2, norm2_ref[1:2]),
            (7, qkv_ref[0:1]),
        ):
            own_ref[at + row : at + row + 1] = source
            pair_ref[at + row : at + row + 1] = source
        own_ref[at + 6 : at + 7] = up0_ref[0:1] + up1_ref[0:1]
        pair_ref[at + 6 : at + 7] = up0_ref[1:2] + up1_ref[1:2]


def small_add_kernel(where_ref, own_ref, got_ref, total_ref, shared_ref):
    total = own_ref[...] + got_ref[...]
    total_ref[...] = total
    row = lax.broadcasted_iota(jnp.int32, total.shape, 0)
    shared_ref[...] = jnp.where(row % 8 < BIAS_UP, total, 0.0)


def small_results_kernel(where_ref, own_ref, got_ref, *refs):
    outs, (gains, shifts, up, qkv_b), sems = refs[:4], refs[4:8], refs[8]
    total = own_ref[...] + got_ref[...]
    total = jnp.where(where_ref[0] == 0, total[:8], total[8:])
    gains[0] = total[0:2]
    shifts[0] = total[2:6]
    up[...] = total[6:7]
    local = qkv_b.shape[2]
    for k in range(2):
        both = total[7:8, 2 * k * local : 2 * (k + 1) * local]
        qkv_b[0, k : k + 1] = jnp.where(where_ref[1] == 0, both[:, :local], both[:, local:])
    copies = Copies(sems)
    for source, target in zip((gains, shifts, up, qkv_b), outs):
        copies.start(source, target)
    copies.done()


def swap(value, axis, bit):
    count = lax.axis_size(axis)
    return lax.ppermute(value, axis, [(source, source ^ bit) for source in range(count)])


def core_swap(value):
    return swap(value, "tensor", 1)


def chip_swap(value):
    return swap(value, "tensor", 2)


def tie(value, *after):
    return lax.optimization_barrier((value, *after))[0]


class Sum:
    def __init__(self, owner, *pieces):
        self.owner = owner
        self.kept = [kept for _, kept in pieces]
        self.got = [swap(sent, "pipe", 1) for sent, _ in pieces]
        count = lax.axis_size("dp")
        self.bits = count.bit_length() - 1
        self.halving = count == 1 << self.bits and self.kept[0].shape[0] % (16 * count) == 0

    def add(self, where):
        rows, columns = self.kept[0].shape
        (self.total,) = call(
            add_kernel,
            [("v", shape((rows * len(self.kept), columns)))],
            [("s", where)] + [("v", item) for item in (*self.kept, *self.got)],
        )
        return self.total

    def whole(self, where, *after):
        total = self.add(where)
        self.total = lax.psum(tie(total, *after), "dp")
        return total

    def halve(self, bit, where):
        parts = len(self.kept)
        rows, columns = self.kept[0].shape
        dims = (rows * parts // 2, columns)
        sent, kept = call(
            partial(halve_sum_kernel, bit, parts),
            [("v", shape(dims)), ("v", shape(dims, F32))],
            [("s", where)] + [("v", item) for item in (*self.kept, *self.got)],
        )
        self.kept, self.got = [kept], [swap(sent, "dp", 1 << bit)]
        return sent

    def join(self, bit, where):
        rows, columns = self.total.shape
        got = swap(self.total, "dp", 1 << bit)
        (self.total,) = call(
            partial(join_kernel, bit),
            [("v", shape((2 * rows, columns)))],
            [("s", where), ("v", self.total), ("v", got)],
        )
        return self.total

    def steps(self):
        if not self.halving:
            return [self.whole]
        bits = range(self.bits)
        return (
            [partial(self.halve, bit) for bit in bits]
            + [self.add]
            + [partial(self.join, bit) for bit in reversed(bits)]
        )

    def finish(self):
        self.other = lax.ppermute(self.total, "pipe", [(1 - self.owner, self.owner)])


def layer_forward(layer, own_in, far_in, w_qkv, small, marks, where, hooks):
    own_q, own_kv, own_x_kept, own_q_kept = qkv(own_in, w_qkv, small)
    own_pair = core_swap(own_kv)
    far_q, far_kv, far_x_kept, far_q_kept = qkv(far_in, w_qkv, small)
    far_pair = core_swap(far_kv)
    w_out = hooks["out"](far_q)
    far_out, kv, kv_kept, far_o, far_lse = attn(
        layer, where, far_q, (own_kv, own_pair, far_kv, far_pair), marks, w_out
    )
    far_out = chip_swap(far_out)
    own_out, own_o, own_lse = attn(layer, where, own_q, (kv,), marks, w_out)
    own_h, hidden, resid1, own_h_kept = norm1(own_in, own_out, far_out, small)
    far_h = chip_swap(own_h)
    w_up, w_down = hooks["ffn"](own_out, own_h)
    own_branch, own_act, own_slope = ffn(own_h, w_up, w_down, small, False)
    far_h = tie(far_h, own_branch)
    far_branch, far_act, far_slope, far_h_kept = ffn(far_h, w_up, w_down, small, True)
    own_branch = tie(own_branch, *hooks["next"](far_branch))
    output, resid2, output_kept = norm2(hidden, own_branch, chip_swap(far_branch), small)
    kept = dict(
        x=(own_x_kept, far_x_kept),
        q=(own_q_kept, far_q_kept),
        kv=kv_kept,
        lse=(own_lse, far_lse),
        o=(own_o, far_o),
        resid=(resid1, resid2),
        h=(own_h_kept, far_h_kept),
        act=(own_act, far_act),
        slope=(own_slope, far_slope),
    )
    return output, output_kept, kept


def layer_backward(layer, upstream, kept, small, marks, where, loads, hooks):
    own_df, skip2, norm2_sums, *grad_in = norm2_back(upstream, kept["resid"][1], small)
    far_df = chip_swap(own_df)
    w_up, w_down, own_slope, far_slope = loads["ffn"](kept["slope"], tie(where, own_df))
    own_dh, own_du, own_db = ffn_back(own_df, own_slope, w_up, w_down, False)
    far_df = tie(far_df, own_dh, *hooks["df"](own_dh))
    far_dh, far_du, far_db = ffn_back(far_df, far_slope, w_up, w_down, True)
    own_act, far_act, own_h, far_h = loads["rows"](
        (*kept["act"], *kept["h"]), tie(where, far_dh, *hooks["dh"](far_dh))
    )
    grads = (own_h, far_h, own_act, far_act, own_df, far_df, own_du, far_du)
    pair = ffn_pair(grads)
    got = [core_swap(item) for item in pair]
    own_dh = tie(own_dh, pair[0])
    own_dz, skip1, norm1_sums = norm1_back(own_dh, chip_swap(far_dh), skip2, kept["resid"][0], small)
    far_dz = chip_swap(own_dz)
    w_out, kv, own_q, far_q, own_lse, far_lse = loads["out"](
        (kept["kv"], *kept["q"], *kept["lse"]), tie(where, own_dz)
    )
    parts = ffn_own(tie(where, w_out), grads, got)
    own_dq, own_dkv, own_send = attn_back(
        layer, 0, tie(where, parts[0], *hooks["dz"](parts)), own_dz, own_q, kv, marks, own_lse, w_out
    )
    own_pair = core_swap(own_send)
    far_dz = tie(far_dz, own_send)
    far_dq, far_dkv, far_send = attn_back(layer, 1, where, far_dz, far_q, kv, marks, far_lse, w_out)
    far_pair = core_swap(tie(far_send, *hooks["send"](far_send)))
    w_qkv, own_x, far_x, own_o, far_o = loads["qkv"]((*kept["x"], *kept["o"]), tie(where, far_send))
    far_dx, own_d, far_d = row_grads(
        small, (own_dq, far_dq), (own_dkv, far_dkv), (own_pair, far_pair), w_qkv
    )
    own_dx, attn_own, attn_pair, qkv_sums = attn_grads(
        tie(where, far_dx, *hooks["dx"](far_dx)),
        (own_d, far_d),
        (own_x, far_x),
        (own_o, far_o),
        (own_dz, far_dz),
        w_qkv,
    )
    far_dx = chip_swap(far_dx)
    sums = (norm1_sums, norm2_sums, own_db, far_db, qkv_sums)
    return (own_dx, far_dx, skip1), grad_in, sums, (attn_own, core_swap(attn_pair))


def body(
    tokens,
    segment_ids,
    pad_mask,
    block_perm,
    qkv_weight,
    qkv_bias,
    out_weight,
    up_weight,
    up_bias,
    down_weight,
    norm_gain,
    shift_bias,
    cotangent,
):
    section = lax.axis_index("pipe")
    place = lax.axis_index("tensor")
    replica = lax.axis_index("dp")
    paired = lax.axis_size("dp") % 2 == 0
    width = tokens.shape[2]
    local = qkv_bias.shape[2]
    here = jnp.stack([section, place % 2, replica % 2, replica, place]).astype(jnp.int32)
    qkv_rows = jnp.transpose(qkv_weight[0], (0, 2, 1))

    def other_half(half, whole):
        if paired:
            return swap(half, "dp", 1)
        even = replica % 2 == 0
        rest = jnp.where(even, whole[..., width // 2 :], whole[..., : width // 2])
        return swap(rest, "pipe", 1)

    (qkv_half,) = halves_of(here, qkv_rows)
    qkv_x = swap(qkv_half, "pipe", 1)
    rows = lax.optimization_barrier(lax.dynamic_index_in_dim(tokens, section, 0, keepdims=False))
    far_rows = chip_swap(rows)
    (own_small,) = call(
        pack_kernel,
        [("v", shape((16, width), F32))],
        [("h", norm_gain), ("h", shift_bias), ("h", up_bias), ("h", qkv_bias), ("s", block_perm)],
        scratch=[
            pltpu.VMEM(item.shape, item.dtype) for item in (norm_gain, shift_bias, up_bias, qkv_bias)
        ],
        copies=4,
    )
    other_small = swap(own_small, "pipe", 1)
    up_half, down_half = halves_of(tie(here, own_small, qkv_half), up_weight, down_weight)
    up_x = swap(up_half, "pipe", 1)
    out_x = swap(tie(out_weight, qkv_x), "pipe", 1)
    (marks,) = call(
        marks_kernel,
        [("v", shape((8, segment_ids.shape[1] // 2), jnp.int32))],
        [("s", tie(here, up_half)), ("v", segment_ids), ("v", pad_mask)],
    )
    *smalls, flags = call(
        params_kernel,
        [("v", shape((16, width), F32))] * 2 + [("h", shape((8, PAIR), F32))],
        [("s", here)]
        + [
            ("v", item)
            for item in (own_small, other_small, core_swap(own_small), core_swap(other_small))
        ],
        scratch=[pltpu.VMEM((8, PAIR), F32)],
        copies=1,
    )
    heads = 2 * block_perm.shape[1]
    where = jnp.concatenate([here, flags[:2, :heads].reshape(-1).astype(jnp.int32)])
    def item(by_core, own, other, after=(), later=()):
        pair_own = core_swap(tie(own, *after) if after else own)
        pair_other = tuple(core_swap(tie(part, *later) if later else part) for part in other)
        return by_core, own, other, pair_own, pair_other

    other_qkv = other_half(tie(qkv_x, own_small, up_half), qkv_rows)
    items = dict(qkv=item(True, qkv_rows, (qkv_x, other_qkv)))
    (first_qkv,) = load(0, tie(where, marks, *smalls, far_rows, up_x), [items["qkv"]])

    def first_out(after):
        fetched["down"] = swap(tie(down_half, up_x), "pipe", 1)
        fetched["up"] = other_half(tie(up_x, after), up_weight)
        items["out"] = item(True, out_weight, (out_x,), (first_qkv,))
        return load(0, tie(where, after), [items["out"]])[0]

    fetched = {}

    def first_ffn(early, after):
        down_x = fetched["down"]
        other_down = other_half(tie(down_x, early), down_weight)
        items["up"] = item(False, up_weight, (up_x, fetched["up"]), (early,), (early,))
        items["down"] = item(False, down_weight, (down_x, other_down), (early,), (after,))
        return load_ffn(0, (), tie(where, after))

    def load_ffn(layer, arrays, after):
        return load(layer, after, [items["up"], items["down"]], arrays)

    def load_one(layer, name, arrays, after):
        return load(layer, after, [items[name]], arrays)

    def load_rows(arrays, after):
        return load(0, after, [], arrays)

    second = []

    def load_second(after):
        second.extend(load(1, tie(where, after), [items["qkv"], items["out"]]))
        return second

    out_first, first_kept, kept_first = layer_forward(
        0,
        rows,
        far_rows,
        first_qkv,
        smalls[0],
        marks,
        where,
        {"out": first_out, "ffn": first_ffn, "next": load_second},
    )
    def second_ffn(early, after):
        fetched["first"] = lax.ppermute(first_kept, "pipe", [(1, 0)])
        return load_ffn(1, (), tie(where, after, fetched["first"]))

    out_second, second_kept, kept_second = layer_forward(
        1,
        out_first,
        chip_swap(out_first),
        second[0],
        smalls[1],
        marks,
        where,
        {
            "out": lambda after: second[1],
            "ffn": second_ffn,
            "next": lambda after: (),
        },
    )

    def loads(layer):
        return {
            "out": partial(load_one, layer, "out"),
            "qkv": partial(load_one, layer, "qkv"),
            "ffn": partial(load_ffn, layer),
            "rows": load_rows,
        }

    def place_outputs(first, second, first_got, second_got, after):
        return call(
            place_kernel,
            [("h", shape((1, 2) + first.shape))],
            [("s", after)] + [("v", value) for value in (first, second, first_got, second_got)],
            us=1.5,
            scratch=[pltpu.VMEM((2,) + first.shape, BF16)],
            copies=1,
        )[0]

    sums, steps = {}, {}

    def begin(name, owner, *pieces):
        sums[name] = Sum(owner, *pieces)
        steps[name] = sums[name].steps()

    def run(after, *names):
        for name in names:
            if steps[name]:
                after = steps[name].pop(0)(tie(where, after))
        return after

    upstream = lax.dynamic_index_in_dim(cotangent, section, 0, keepdims=False)
    outputs = []

    def nothing(*_):
        return ()

    def later_df(after):
        second_got = lax.ppermute(second_kept, "pipe", [(0, 1)])
        outputs.append(
            place_outputs(first_kept, second_kept, fetched["first"], second_got, tie(where, after))
        )
        return outputs

    def later_dz(parts):
        begin("ab1", 1, parts[0:2], parts[2:4])
        return ()

    grads, _, small_second, attn_second = layer_backward(
        1,
        (upstream,),
        kept_second,
        smalls[1],
        marks,
        where,
        loads(1),
        {
            "df": later_df,
            "dh": nothing,
            "dz": later_dz,
            "send": lambda after: sums["ab1"].got[:1],
            "dx": nothing,
        },
    )
    grads = (tie(grads[0], run(grads[0], "ab1")),) + grads[1:]

    def first_df(after):
        sent, kept = split(tie(where, after), *attn_second)
        begin("c1", 1, (sent, kept))
        return (sent,)

    def first_dh(after):
        return (run(after, "ab1"),)

    def first_dz(parts):
        begin("a0", 0, parts[0:2])
        begin("b0", 0, parts[2:4])
        return (run(parts[0], "ab1", "c1"),)

    def first_send(after):
        return (run(after, "ab1", "c1", "a0"),)

    grads, (grad_second,), small_first, attn_first = layer_backward(
        0,
        grads,
        kept_first,
        smalls[0],
        marks,
        where,
        loads(0),
        {"df": first_df, "dh": first_dh, "dz": first_dz, "send": first_send, "dx": nothing},
    )
    last = [attn_first[0]]

    def now():
        return tie(where, *last)

    def then(*values):
        last[:] = values

    def step(*names):
        then(run(last[-1], *names))

    def small_add(total, got):
        total, shared = call(
            small_add_kernel,
            [("v", shape((16, width), F32))] * 2,
            [("s", now()), ("v", total), ("v", got)],
        )
        then(total)
        return total, shared

    total, pair_sums = call(
        pack_sums_kernel,
        [("v", shape((16, width), F32))] * 2,
        [("s", now())] + [("v", value) for value in (*small_first, *small_second)],
    )
    then(total)
    got = core_swap(pair_sums)
    sent, kept = split(now(), *attn_first)
    then(sent)
    begin("c0", 0, (sent, kept))
    step("a0", "b0", "c1", "ab1")
    sums["ab1"].finish()
    step("a0", "b0", "c0")
    total, shared = small_add(total, got)
    got = chip_swap(shared)
    (grad_first,) = call(
        grad_in_kernel, [("v", shape(rows.shape))], [("s", now())] + [("v", value) for value in grads]
    )
    then(grad_first)
    first_got = lax.ppermute(grad_first, "pipe", [(1, 0)])
    second_got = lax.ppermute(grad_second, "pipe", [(0, 1)])
    step("a0", "c0", "b0", "c1")
    while steps["a0"]:
        step("a0")
    sums["a0"].finish()
    step("c0")
    total, _ = small_add(total, got)
    hops = [("pipe", 1)]
    count = lax.axis_size("dp")
    if count & (count - 1):
        total = lax.psum(total, "dp")
    else:
        hops += [("dp", 1 << bit) for bit in range(count.bit_length() - 1)]
    got = swap(total, *hops[0])
    while steps["c1"]:
        step("c1")
    sums["c1"].finish()
    step("b0")
    input_grad = place_outputs(grad_first, grad_second, first_got, second_got, now())
    then(input_grad)
    step("c0")
    for hop in hops[1:]:
        total, _ = small_add(total, got)
        got = swap(total, *hop)
    while steps["b0"]:
        step("b0")
    sums["b0"].finish()
    while steps["c0"]:
        step("c0")
    sums["c0"].finish()
    outs = [shape(item.shape, F32) for item in (norm_gain, shift_bias, up_bias, qkv_bias)]
    gains, shifts, upb, qkvb = call(
        small_results_kernel,
        [("h", item) for item in outs],
        [("s", now()), ("v", total), ("v", got)],
        scratch=[pltpu.VMEM(item.shape, F32) for item in outs],
        copies=4,
    )
    layer_out = outputs[0]

    def pieces(second, *names):
        first = [sums[name].total for name in names] + [sums[name].other for name in names]
        return first, [sums[second].other, sums[second].total]

    upw, downw = results("ffn", tie(where, gains), *pieces("ab1", "a0", "b0"))
    qkvw, outw = results("attn", tie(where, upw), *pieces("c1", "c0"))
    qkvw = jnp.transpose(qkvw, (0, 2, 1))
    return (
        layer_out,
        input_grad,
        qkvw[None],
        qkvb,
        outw[None],
        upw[None],
        upb,
        downw[None],
        gains,
        shifts,
    )


def solution(mesh):
    return jax.shard_map(
        body,
        mesh=mesh,
        in_specs=(
            P("dp", "tensor", None),
            P("dp", None),
            P("dp", None),
            P("pipe", "tensor", None),
            P("pipe", None, None, "tensor"),
            P("pipe", None, "tensor"),
            P("pipe", "tensor", None),
            P("pipe", None, "tensor"),
            P("pipe", "tensor"),
            P("pipe", "tensor", None),
            P("pipe", None, None),
            P("pipe", None, None),
            P("dp", "tensor", None),
        ),
        out_specs=(
            P("pipe", "dp", "tensor", None),
            P("pipe", "dp", "tensor", None),
            P("pipe", None, None, "tensor"),
            P("pipe", None, "tensor"),
            P("pipe", "tensor", None),
            P("pipe", None, "tensor"),
            P("pipe", "tensor"),
            P("pipe", "tensor", None),
            P("pipe", None, None),
            P("pipe", None, None),
        ),
        check_vma=False,
    )
```

```python
from functools import partial

import jax
import jax.numpy as jnp
from jax import lax
from jax.experimental import pallas as pl
from jax.experimental.pallas import tpu as pltpu
from jax.sharding import PartitionSpec as P

BF16 = jnp.bfloat16
F32 = jnp.float32
HEAD_DIM = 64
PAIR = 2 * HEAD_DIM
LOG2E = 1.4426950408889634
MASKED = -1e30
VMEM_LIMIT = 16 * 1024 * 1024
COST = 2e10
NORM_EPSILON_TERM = 1e-06

FLAGS = 5

SPACES = {"v": pltpu.VMEM, "s": pltpu.SMEM, "h": pl.ANY}
PLACES = {"v": pltpu.VMEM, "s": pl.ANY, "h": pltpu.HBM}


def shape(dims, dtype=BF16):
    return jax.ShapeDtypeStruct(dims, dtype)


def call(kernel, outs, args, us=0.1, scratch=(), copies=0):
    flops = int(us * COST)
    scratch = list(scratch)
    if copies:
        scratch.append(pltpu.SemaphoreType.DMA((copies,)))
    return pl.pallas_call(
        kernel,
        name=(kernel.func if isinstance(kernel, partial) else kernel).__name__,
        out_shape=[PLACES[space](item.shape, item.dtype) for space, item in outs],
        in_specs=[pl.BlockSpec(memory_space=SPACES[space]) for space, _ in args],
        out_specs=[pl.BlockSpec(memory_space=SPACES[space]) for space, _ in outs],
        scratch_shapes=scratch,
        compiler_params=pltpu.CompilerParams(vmem_limit_bytes=VMEM_LIMIT),
        cost_estimate=pl.CostEstimate(flops=flops, bytes_accessed=0, transcendentals=0),
    )(*[pltpu.with_memory_space_constraint(item, PLACES[space]) for space, item in args])


class Copies:
    def __init__(self, sems):
        self.sems, self.pending = sems, []

    def sem(self):
        at = len(self.pending)
        return self.sems[at] if isinstance(self.sems, list) else self.sems.at[at]

    def start(self, source, target):
        copy = pltpu.make_async_copy(source, target, self.sem())
        copy.start()
        self.pending.append(copy)

    def start_one(self, cases, target):
        sem = self.sem()
        made = []
        for condition, source in cases:
            made.append(pltpu.make_async_copy(source, target, sem))
            pl.when(condition)(made[-1].start)
        self.pending.append(made[0])

    def done(self):
        for copy in self.pending:
            copy.wait()


def loop(count, step):
    lax.fori_loop(0, count, lambda i, _: step(i), None)


def part_of(i, size):
    return pl.ds(pl.multiple_of(i * size, size), size)


def dot(left, right):
    return jnp.dot(left, right, preferred_element_type=F32)


def dot_tn(left, right):
    return lax.dot_general(left, right, (((0,), (0,)), ((), ())), preferred_element_type=F32)


def dot_nt(left, right):
    return lax.dot_general(left, right, (((1,), (1,)), ((), ())), preferred_element_type=F32)


def pack_kernel(gains_in, shifts_in, up_in, qkv_in, perm_ref, out_ref, gains, shifts, up, qkv_b, sems):
    copies = Copies(sems)
    for source, target in ((gains_in, gains), (shifts_in, shifts), (up_in, up), (qkv_in, qkv_b)):
        copies.start(source, target)
    out_ref[...] = jnp.zeros_like(out_ref)
    lane = lax.broadcasted_iota(jnp.int32, (1, out_ref.shape[1]), 1)
    flags = jnp.zeros((1, out_ref.shape[1]), F32)
    for head in range(perm_ref.shape[1]):
        flags = jnp.where(lane == head, perm_ref[0, head, 0].astype(F32), flags)
    out_ref[9:10] = flags
    copies.done()
    out_ref[0:2] = gains[0]
    out_ref[2:6] = shifts[0]
    out_ref[6:7] = up[...].astype(F32)
    out_ref[7:9, 0 : qkv_b.shape[2]] = qkv_b[0].astype(F32)


GAIN1, GAIN2, BIAS_OUT, SHIFT1, BIAS2, SHIFT2, BIAS_UP, BIAS_Q, TURNED = 0, 1, 2, 3, 4, 5, 6, 8, 10


def params_kernel(where_ref, own_ref, other_ref, pair_ref, other_pair_ref, first_out, second_out, flags_copy, flags, sems):
    section, core = where_ref[0], where_ref[1]
    width = own_ref.shape[1]
    local = width // 4
    heads = local // HEAD_DIM
    lane = lax.broadcasted_iota(jnp.int32, (1, width), 1)
    flags[...] = jnp.zeros_like(flags)
    for layer, out_ref in enumerate((first_out, second_out)):
        here = section == layer
        mine = jnp.where(here, own_ref[...], other_ref[...])
        pair = jnp.where(here, pair_ref[...], other_pair_ref[...])
        first = jnp.where(core == 0, mine, pair)
        second = jnp.where(core == 0, pair, mine)
        out_ref[...] = mine
        out_ref[BIAS_UP + 1 : BIAS_UP + 2] = pair[BIAS_UP : BIAS_UP + 1]
        biases = jnp.where(lane < local, first, pltpu.roll(second, local, 1))
        out_ref[BIAS_Q : BIAS_Q + 2] = biases[7:9]
        turned = jnp.where(lane < heads, first, pltpu.roll(second, heads, 1))[9:10]
        lanes = jnp.zeros((1, width), F32)
        for head in range(2 * heads):
            chosen = (lane // HEAD_DIM) % (2 * heads) == head
            lanes = jnp.where(chosen, turned[:, head : head + 1], lanes)
        out_ref[TURNED : TURNED + 1] = lanes
        flags[layer : layer + 1] = turned[:, 0:PAIR]
    copies = Copies(sems)
    copies.start(flags, flags_copy)
    copies.done()


def marks_kernel(where_ref, segments_ref, real_ref, out_ref):
    quarter = out_ref.shape[1] // 2
    out_ref[...] = jnp.zeros_like(out_ref)
    for r in range(4):
        cols = pl.ds(pl.multiple_of((where_ref[4] ^ r) * quarter, PAIR), quarter)
        at = slice((r % 2) * quarter, (r % 2 + 1) * quarter)
        segment = jnp.where(where_ref[0] == 0, segments_ref[0:1, cols], segments_ref[1:2, cols])
        real = jnp.where(where_ref[0] == 0, real_ref[0:1, cols], real_ref[1:2, cols])
        out_ref[1 + r // 2 : 2 + r // 2, at] = jnp.where(real == 1, segment, -1)
        if r % 2 == 0:
            out_ref[0:1, (r // 2) * quarter : (r // 2 + 1) * quarter] = segment


def halve_kernel(where_ref, *refs):
    count = len(refs) // 2
    copies = Copies(refs[-1])
    for source, half in zip(refs[:count], refs[count:-1]):
        columns = half.shape[2]
        copies.start_one(
            [
                (where_ref[2] == side, source.at[:, :, pl.ds(side * columns, columns)])
                for side in range(2)
            ],
            half,
        )
    copies.done()


def halves_of(where, *wholes):
    return call(
        halve_kernel,
        [("v", shape(whole.shape[:2] + (whole.shape[2] // 2,))) for whole in wholes],
        [("s", where)] + [("h", whole) for whole in wholes],
        copies=len(wholes),
    )


def weight_copies(copies, where_ref, layer, k, own, other, target):
    here = where_ref[0] == layer
    if len(other) == 1:
        copies.start_one(
            [(here, own.at[k]), (jnp.logical_not(here), other[0].at[k])], target(slice(None))
        )
        return
    columns = other[0].shape[-1]
    for side in range(2):
        cols = pl.ds(side * columns, columns)
        direct = where_ref[2] == side
        copies.start_one(
            [
                (here, own.at[k, :, cols]),
                (jnp.logical_not(here) & direct, other[0].at[k]),
                (jnp.logical_not(here) & jnp.logical_not(direct), other[1].at[k]),
            ],
            target(cols),
        )


def load_kernel(layer, items, plain, where_ref, *refs):
    sems = refs[-1]
    copies = Copies(sems)
    count = sum(2 * (1 + parts) for _, parts in items)
    sources, plain_in, outs = refs[:count], refs[count : count + plain], refs[count + plain : -1]
    for (by_core, parts), out_ref in zip(items, outs):
        for pair in range(2):
            own, *other = sources[: 1 + parts]
            sources = sources[1 + parts :]
            if by_core:
                rows = out_ref.shape[1] // 2
                slot = (where_ref[1] + pair) % 2
                at = pl.ds(pl.multiple_of(slot * rows, rows), rows)
                for k in range(out_ref.shape[0]):
                    weight_copies(
                        copies, where_ref, layer, k, own, other, lambda cols, k=k: out_ref.at[k, at, cols]
                    )
            else:
                weight_copies(
                    copies, where_ref, layer, 0, own, other, lambda cols: out_ref.at[pair, :, cols]
                )
    for source, target in zip(plain_in, outs[len(items) :]):
        copies.start(source, target)
    copies.done()


def load(layer, where, items, arrays=()):
    outs, sources, kinds, count = [], [], [], len(arrays)
    for by_core, own, other, pair_own, pair_other in items:
        k, rows, columns = own.shape
        outs.append(shape((k, 2 * rows, columns)) if by_core else shape((2, rows, columns)))
        sources += [own, *other, pair_own, *pair_other]
        kinds.append((by_core, len(other)))
        count += 2 * k * len(other)
    outs += [shape(item.shape, item.dtype) for item in arrays]
    return call(
        partial(load_kernel, layer, kinds, len(arrays)),
        [("v", item) for item in outs],
        [("s", where)] + [("h", item) for item in (*sources, *arrays)],
        us=2.4,
        copies=count,
    )


def qkv_kernel(x_ref, w_ref, b_ref, q_ref, kv_ref, x_copy, q_copy, sems):
    copies = Copies(sems)
    copies.start(x_ref, x_copy)
    x = x_ref[...]
    width = q_ref.shape[1]
    q_ref[...] = (dot_nt(x, w_ref[0]) + b_ref[BIAS_Q : BIAS_Q + 1, :width]).astype(BF16)
    copies.start(q_ref, q_copy)
    kv_ref[:, :width] = dot_nt(x, w_ref[1]).astype(BF16)
    kv_ref[:, width:] = (dot_nt(x, w_ref[2]) + b_ref[BIAS_Q + 1 : BIAS_Q + 2, :width]).astype(BF16)
    copies.done()


def qkv(x, w, b):
    rows, width = x.shape[0], w.shape[1]
    return call(
        qkv_kernel,
        [
            ("v", shape((rows, width))),
            ("v", shape((rows, 2 * width))),
            ("h", shape(x.shape)),
            ("h", shape((rows, width))),
        ],
        [("v", x), ("v", w), ("v", b)],
        1.1,
        copies=2,
    )


def lanes_of(rows):
    return lax.broadcasted_iota(jnp.int32, (rows, PAIR), 1)


def fill_bias(bias, side, marks_ref):
    rows = bias.shape[1]
    wanted = jnp.transpose(marks_ref[:, side * rows : (side + 1) * rows])[:, 0:1]
    for j in range(2):
        bias[j] = jnp.where(wanted == marks_ref[1 + j : 2 + j, :], 0.0, MASKED).astype(F32)


def block_of(where_ref, layer, head, turned):
    return where_ref[FLAGS + 6 * layer + head] ^ turned


def attn_rows(layer, where_ref, turned, q_ref, kv_ref, marks_ref, o_ref, lse_ref, bias):
    rows, width = q_ref.shape
    fill_bias(bias, turned, marks_ref)
    lanes = lanes_of(rows)
    low = lanes < HEAD_DIM
    scale = HEAD_DIM**-0.5 * LOG2E
    lse_ref[...] = jnp.zeros_like(lse_ref)

    def step(tile):
        cols, vcols = part_of(tile, PAIR), part_of(tile + width // PAIR, PAIR)
        q = q_ref[:, cols]
        mixed = []
        for side in range(2):
            head = 2 * tile + side
            block = block_of(where_ref, layer, head, turned)
            q_head = jnp.where(low if side == 0 else ~low, q, jnp.zeros_like(q))
            s = dot_nt(q_head, kv_ref[block, :, cols]) * scale + bias[block]
            top = jnp.maximum(jnp.max(s, axis=1, keepdims=True), 0.0)
            e = jnp.exp2(s - top)
            total = jnp.exp2(-top) + jnp.sum(e, axis=1, keepdims=True)
            p = (e * (1.0 / total)).astype(BF16)
            mixed.append(dot(p, kv_ref[block, :, vcols]))
            lse_ref[...] = jnp.where(lanes == head, top + jnp.log2(total), lse_ref[...])
        o_ref[:, cols] = jnp.where(low, mixed[0], mixed[1]).astype(BF16)

    loop(width // PAIR, step)


def attn_far_kernel(
    layer, where_ref, q_ref, kv0_ref, kv1_ref, kv2_ref, kv3_ref, marks_ref, w_ref,
    out_ref, kv_ref, kv_copy, o_copy, lse_copy, bias, o_ref, lse_ref, sems,
):
    copies = Copies(sems)
    half = kv0_ref.shape[0]
    for block, pair in enumerate(((kv0_ref, kv1_ref), (kv2_ref, kv3_ref))):
        kv_ref[block, :half] = pair[0][...]
        kv_ref[block, half:] = pair[1][...]
    copies.start(kv_ref, kv_copy)
    attn_rows(layer, where_ref, 1, q_ref, kv_ref, marks_ref, o_ref, lse_ref, bias)
    copies.start(o_ref, o_copy)
    copies.start(lse_ref, lse_copy)
    out_ref[...] = dot(o_ref[...], w_ref[0]).astype(out_ref.dtype)
    copies.done()


def attn_own_kernel(
    layer, where_ref, q_ref, kv_ref, marks_ref, w_ref, out_ref, o_copy, lse_copy, bias, o_ref, lse_ref, sems
):
    copies = Copies(sems)
    attn_rows(layer, where_ref, 0, q_ref, kv_ref, marks_ref, o_ref, lse_ref, bias)
    copies.start(o_ref, o_copy)
    copies.start(lse_ref, lse_copy)
    out_ref[...] = dot(o_ref[...], w_ref[0]).astype(out_ref.dtype)
    copies.done()


def attn(layer, where, q, kv, marks, w):
    rows, width = q.shape
    far = len(kv) > 1
    outs = [("v", shape((rows, w.shape[2]), BF16 if far else F32))]
    if far:
        joined = shape((2, 2 * rows, kv[0].shape[1]))
        outs += [("v", joined), ("h", joined)]
    outs += [("h", shape((rows, width))), ("h", shape((rows, PAIR), F32))]
    args = [("s", where)] + [("v", item) for item in (q, *kv, marks, w)]
    return call(
        partial(attn_far_kernel if far else attn_own_kernel, layer),
        outs,
        args,
        4.6,
        scratch=[
            pltpu.VMEM((2, rows, 2 * rows), F32),
            pltpu.VMEM((rows, width), BF16),
            pltpu.VMEM((rows, PAIR), F32),
        ],
        copies=3 if far else 2,
    )


def normed_rows(resid):
    centred = resid - jnp.mean(resid, axis=1, keepdims=True)
    inverse = lax.rsqrt(jnp.mean(centred * centred, axis=1, keepdims=True) + NORM_EPSILON_TERM)
    return centred * inverse, inverse


def norm1_kernel(x_ref, own_ref, far_ref, norms_ref, low_ref, full_ref, resid_copy, low_copy, resid, sems):
    copies = Copies(sems)
    projected = own_ref[...] + far_ref[...].astype(F32)
    total = x_ref[...].astype(F32) + projected + norms_ref[BIAS_OUT : BIAS_OUT + 1, :]
    resid[...] = total
    copies.start(resid, resid_copy)
    hidden = normed_rows(total)[0] * norms_ref[GAIN1 : GAIN1 + 1, :] + norms_ref[SHIFT1 : SHIFT1 + 1, :]
    full_ref[...] = hidden
    low_ref[...] = hidden.astype(BF16)
    copies.start(low_ref, low_copy)
    copies.done()


def norm1(x, own, far, norms):
    return call(
        norm1_kernel,
        [("v", shape(x.shape)), ("v", shape(x.shape, F32)), ("h", shape(x.shape, F32)), ("h", shape(x.shape))],
        [("v", x), ("v", own), ("v", far), ("v", norms)],
        scratch=[pltpu.VMEM(x.shape, F32)],
        us=1.2,
        copies=2,
    )


def norm2_kernel(h_ref, own_ref, far_ref, norms_ref, low_ref, resid_copy, low_copy, resid, sems):
    copies = Copies(sems)
    branch = own_ref[...] + far_ref[...].astype(F32)
    total = h_ref[...] + branch + norms_ref[BIAS2 : BIAS2 + 1, :]
    resid[...] = total
    copies.start(resid, resid_copy)
    out = normed_rows(total)[0] * norms_ref[GAIN2 : GAIN2 + 1, :] + norms_ref[SHIFT2 : SHIFT2 + 1, :]
    low_ref[...] = out.astype(BF16)
    copies.start(low_ref, low_copy)
    copies.done()


def norm2(h, own, far, norms):
    return call(
        norm2_kernel,
        [("v", shape(h.shape)), ("h", shape(h.shape, F32)), ("h", shape(h.shape))],
        [("v", h), ("v", own), ("v", far), ("v", norms)],
        scratch=[pltpu.VMEM(h.shape, F32)],
        us=1.2,
        copies=2,
    )


TAIL = tuple(
    0.5 * c
    for c in (
        0.05029408002973294, -0.1830316054165625, 0.16930258232763196, -0.005798692821681883,
        0.14152663657068731, 0.16851528425000623, 0.20784663429852349, 0.22566934002005623,
        0.22567586682378352,
    )
)


def gelu_and_slope(u):
    bell = jnp.exp2(u * u * (-0.5 * LOG2E))
    t = 1.0 / (1.0 + jnp.abs(u) * (0.4 * 0.5**0.5))
    poly = TAIL[0]
    for c in TAIL[1:]:
        poly = poly * t + c
    tail = poly * t * bell
    below = jnp.where(u < 0.0, tail, 1.0 - tail)
    return u * below, below + u * bell * 0.3989422804014327


UNITS = 768


def ffn_kernel(far, h_ref, up_ref, down_ref, b_ref, out_ref, act_copy, slope_copy, *rest):
    act_ref, slope_ref, total_ref, sems = rest[-4:]
    steps = up_ref.shape[2] // UNITS
    if far:
        rows_copy = pltpu.make_async_copy(h_ref, rest[0], sems.at[4 * steps])
        rows_copy.start()
    total_ref[...] = jnp.zeros_like(total_ref)

    def copies_of(i):
        half, cols = i // steps, part_of(i % steps, UNITS)
        return [
            pltpu.make_async_copy(kept.at[half, :, cols], copy.at[half, :, cols], sems.at[2 * i + k])
            for k, (kept, copy) in enumerate(((act_ref, act_copy), (slope_ref, slope_copy)))
        ]

    def step(i):
        half, cols = i // steps, part_of(i % steps, UNITS)
        pre = dot(h_ref[...], up_ref[half, :, cols]) + b_ref[pl.ds(BIAS_UP + half, 1), cols]
        act, slope = gelu_and_slope(pre)
        act = act.astype(BF16)
        act_ref[half, :, cols] = act
        slope_ref[half, :, cols] = slope.astype(BF16)
        for copy in copies_of(i):
            copy.start()
        total_ref[...] += dot(act, down_ref[half, cols, :])

    loop(2 * steps, step)
    out_ref[...] = total_ref[...].astype(out_ref.dtype)

    def finish(i):
        for copy in copies_of(i):
            copy.wait()

    loop(2 * steps, finish)
    if far:
        rows_copy.wait()


def ffn(h, up, down, b, far):
    rows, width = h.shape
    units = up.shape[2]
    outs = [
        ("v", shape((rows, width), BF16 if far else F32)),
        ("h", shape((2, rows, units))),
        ("h", shape((2, rows, units))),
    ]
    if far:
        outs.append(("h", shape(h.shape)))
    return call(
        partial(ffn_kernel, far),
        outs,
        [("v", h), ("v", up), ("v", down), ("v", b)],
        0.1,
        scratch=[pltpu.VMEM((2, rows, units), BF16)] * 2 + [pltpu.VMEM((rows, width), F32)],
        copies=4 * (units // UNITS) + 1,
    )


def norm_back(upstream, resid, gain, low_ref, full_ref, sums_ref):
    normed, inverse = normed_rows(resid)
    scaled = upstream * gain
    inner = (
        scaled
        - jnp.mean(scaled, axis=1, keepdims=True)
        - normed * jnp.mean(scaled * normed, axis=1, keepdims=True)
    )
    grad = inverse * inner
    full_ref[...] = grad
    low_ref[...] = grad.astype(BF16)
    sums_ref[...] = jnp.zeros_like(sums_ref)
    sums_ref[0:1] = jnp.sum(upstream * normed, axis=0, keepdims=True)
    sums_ref[1:2] = jnp.sum(upstream, axis=0, keepdims=True)
    sums_ref[2:3] = jnp.sum(grad, axis=0, keepdims=True)


def norm2_back_kernel(inner, *refs):
    if inner:
        own_ref, far_ref, resid1_ref, resid_in, norms_ref, *refs = refs
        low_ref, full_ref, sums_ref, grad_copy, resid, grad_ref, sems = refs
    else:
        up_ref, resid_in, norms_ref, low_ref, full_ref, sums_ref, resid, sems = refs
    copies = Copies(sems)
    copies.start(resid_in, resid)
    if inner:
        grad_in = (own_ref[...] + far_ref[...].astype(F32) + resid1_ref[...]).astype(BF16)
        grad_ref[...] = grad_in
        copies.start(grad_ref, grad_copy)
    else:
        grad_in = up_ref[...]
    copies.done()
    gain = norms_ref[GAIN2 : GAIN2 + 1, :]
    norm_back(grad_in.astype(F32), resid[...], gain, low_ref, full_ref, sums_ref)


def norm2_back(upstream, resid, norms):
    dims = upstream[0].shape
    inner = len(upstream) > 1
    outs = [("v", shape(dims)), ("v", shape(dims, F32)), ("v", shape((8, dims[1]), F32))]
    scratch = [pltpu.VMEM(dims, F32)]
    if inner:
        outs.append(("h", shape(dims)))
        scratch.append(pltpu.VMEM(dims, BF16))
    return call(
        partial(norm2_back_kernel, inner),
        outs,
        [("v", item) for item in upstream] + [("h", resid), ("v", norms)],
        scratch=scratch,
        us=1.7,
        copies=2,
    )


def norm1_back_kernel(own_ref, far_ref, skip_ref, resid_in, norms_ref, low_ref, full_ref, sums_ref, resid, sems):
    copies = Copies(sems)
    copies.start(resid_in, resid)
    upstream = own_ref[...] + far_ref[...].astype(F32) + skip_ref[...]
    copies.done()
    gain = norms_ref[GAIN1 : GAIN1 + 1, :]
    norm_back(upstream, resid[...], gain, low_ref, full_ref, sums_ref)


def norm1_back(own, far, skip, resid, norms):
    dims = own.shape
    return call(
        norm1_back_kernel,
        [("v", shape(dims)), ("v", shape(dims, F32)), ("v", shape((8, dims[1]), F32))],
        [("v", own), ("v", far), ("v", skip), ("h", resid), ("v", norms)],
        scratch=[pltpu.VMEM(dims, F32)],
        us=1.7,
        copies=1,
    )


def ffn_back_kernel(df_ref, slope_ref, up_ref, down_ref, dh_ref, du_ref, db_ref, total_ref):
    units = up_ref.shape[2]
    steps = units // UNITS
    total_ref[...] = jnp.zeros_like(total_ref)

    def step(i):
        half, cols = i // steps, part_of(i % steps, UNITS)
        du = dot_nt(df_ref[...], down_ref[half, cols, :]) * slope_ref[half, :, cols].astype(F32)
        du = du.astype(BF16)
        du_ref[:, part_of(i, UNITS)] = du
        db_ref[pl.ds(half, 1), cols] = jnp.sum(du.astype(F32), axis=0, keepdims=True)
        total_ref[...] += dot_nt(du, up_ref[half, :, cols])

    loop(2 * steps, step)
    dh_ref[...] = total_ref[...].astype(dh_ref.dtype)


def ffn_back(df, slope, up, down, far):
    rows, width = df.shape
    units = 2 * up.shape[2]
    return call(
        ffn_back_kernel,
        [
            ("v", shape((rows, width), BF16 if far else F32)),
            ("v", shape((rows, units))),
            ("v", shape((2, units // 2), F32)),
        ],
        [("v", df), ("v", slope), ("v", up), ("v", down)],
        1.8,
        scratch=[pltpu.VMEM((rows, width), F32)],
    )


def ffn_grads_of(half, h, act, df, du):
    units = act[0].shape[2]
    cols = slice(half * units, (half + 1) * units)
    up = dot_tn(h[0][...], du[0][:, cols]) + dot_tn(h[1][...], du[1][:, cols])
    down = dot_tn(act[0][half], df[0][...]) + dot_tn(act[1][half], df[1][...])
    return up, down


def ffn_pair_kernel(h0, h1, a0, a1, df0, df1, du0, du1, up_ref, down_ref):
    up, down = ffn_grads_of(1, (h0, h1), (a0, a1), (df0, df1), (du0, du1))
    up_ref[...] = up.astype(BF16)
    down_ref[...] = down.astype(BF16)


def ffn_own_kernel(where_ref, h0, h1, a0, a1, df0, df1, du0, du1, up_got, down_got, *outs):
    up, down = ffn_grads_of(0, (h0, h1), (a0, a1), (df0, df1), (du0, du1))
    up += up_got[...].astype(F32)
    down += down_got[...].astype(F32)
    first = where_ref[0] == 0
    half = outs[0].shape[0]
    for part in range(2):
        rows = slice(part * half, (part + 1) * half)
        outs[2 * part][...] = jnp.where(first, down[rows], up[rows]).astype(BF16)
        outs[2 * part + 1][...] = jnp.where(first, up[rows], down[rows])


def ffn_pair(args):
    rows, width = args[0].shape
    units = args[2].shape[2]
    return call(
        ffn_pair_kernel,
        [("v", shape((width, units)))] * 2,
        [("v", item) for item in args],
        1.4,
    )


def ffn_own(where, args, got):
    rows, width = args[0].shape
    units = args[2].shape[2]
    return call(
        ffn_own_kernel,
        [("v", shape((width // 2, units))), ("v", shape((width // 2, units), F32))] * 2,
        [("s", where)] + [("v", item) for item in (*args, *got)],
        2.2,
    )


def attn_back_kernel(
    layer, turned, where_ref, dz_ref, q_ref, kv_ref, marks_ref, lse_ref, w_ref,
    dq_ref, dkv_ref, dkv_pair_ref, bias, do_ref,
):
    rows, width = q_ref.shape
    fill_bias(bias, turned, marks_ref)
    low = lanes_of(rows) < HEAD_DIM
    scale = HEAD_DIM**-0.5
    do_ref[...] = dot_nt(dz_ref[...], w_ref[0]).astype(BF16)
    lanes = lanes_of(rows)
    tiles = width // PAIR

    def step(tile):
        cols, vcols = part_of(tile, PAIR), part_of(tile + tiles, PAIR)
        q, do = q_ref[:, cols], do_ref[:, cols]
        dq, dk, dv = [], 0.0, 0.0
        for side in range(2):
            head = 2 * tile + side
            block = block_of(where_ref, layer, head, turned)
            part = low if side == 0 else ~low
            q_head = jnp.where(part, q, jnp.zeros_like(q))
            do_head = jnp.where(part, do, jnp.zeros_like(do))
            k = kv_ref[block, :, cols]
            s = dot_nt(q_head, k) * (scale * LOG2E) + bias[block]
            log_total = jnp.sum(jnp.where(lanes == head, lse_ref[...], 0.0), axis=1, keepdims=True)
            p = jnp.exp2(s - log_total)
            dp = dot_nt(do_head, kv_ref[block, :, vcols])
            centre = jnp.sum(p * dp, axis=1, keepdims=True)
            ds = (p * (dp - centre)).astype(BF16)
            dq.append(dot(ds, k))
            dv += dot_tn(p.astype(BF16), do_head)
            dk += dot_tn(ds, q_head)
        dq_ref[:, cols] = (jnp.where(low, dq[0], dq[1]) * scale).astype(BF16)
        dkv_ref[:, cols] = dk[:rows] * scale
        dkv_ref[:, vcols] = dv[:rows]
        dkv_pair_ref[:, cols] = (dk[rows:] * scale).astype(BF16)
        dkv_pair_ref[:, vcols] = dv[rows:].astype(BF16)

    loop(tiles, step)


def attn_back(layer, turned, where, dz, q, kv, marks, lse, w):
    rows, width = q.shape
    return call(
        partial(attn_back_kernel, layer, turned),
        [("v", shape((rows, width))), ("v", shape((rows, 2 * width), F32)), ("v", shape((rows, 2 * width)))],
        [("s", where)] + [("v", item) for item in (dz, q, kv, marks, lse, w)],
        4.4,
        scratch=[pltpu.VMEM((2, rows, 2 * rows), F32), pltpu.VMEM((rows, width), BF16)],
    )


def row_grads_kernel(
    small_ref, dq0_ref, dq1_ref, kv0_ref, kv1_ref, pair0_ref, pair1_ref, w_ref, dx_ref, d0_ref, d1_ref
):
    width = dq0_ref.shape[1]
    turned = small_ref[TURNED : TURNED + 1, :] == 1.0
    near = kv0_ref[...] + pair0_ref[...].astype(F32)
    far = kv1_ref[...] + pair1_ref[...].astype(F32)
    d0_ref[:, :width] = dq0_ref[...]
    d1_ref[:, :width] = dq1_ref[...]
    d0_ref[:, width:] = jnp.where(turned, far, near).astype(BF16)
    d1_ref[:, width:] = jnp.where(turned, near, far).astype(BF16)
    total = None
    for k in range(3):
        part = dot(d1_ref[:, k * width : (k + 1) * width], w_ref[k])
        total = part if total is None else total + part
    dx_ref[...] = total.astype(BF16)


def row_grads(small, dq, kv, pair, w):
    rows, width = dq[0].shape
    return call(
        row_grads_kernel,
        [("v", shape((rows, w.shape[2])))] + [("v", shape((rows, 3 * width)))] * 2,
        [("v", item) for item in (small, *dq, *kv, *pair, w)],
        0.9,
    )


def attn_grads_kernel(
    where_ref, d0_ref, d1_ref, x0_ref, x1_ref, o0_ref, o1_ref, dz0_ref, dz1_ref, w_ref,
    dx_ref, own_ref, pair_ref, db_ref,
):
    width = o0_ref.shape[1]
    first_core = where_ref[1] == 0
    share = width // 2
    db_ref[...] = jnp.zeros_like(db_ref)
    for k in range(4):
        cols = slice(k * width, (k + 1) * width)
        if k < 3:
            left, right = (d0_ref[:, cols], d1_ref[:, cols]), (x0_ref[...], x1_ref[...])
        else:
            left, right = (o0_ref[...], o1_ref[...]), (dz0_ref[...], dz1_ref[...])
        if k in (0, 2):
            sums = jnp.sum(left[0].astype(F32), axis=0, keepdims=True)
            sums += jnp.sum(left[1].astype(F32), axis=0, keepdims=True)
            db_ref[0:1, k // 2 * width : (k // 2 + 1) * width] = sums
        both = dot_tn(left[0], right[0]) + dot_tn(left[1], right[1])
        rows = slice(k * share, (k + 1) * share)
        own_ref[rows] = jnp.where(first_core, both[:share], both[share:])
        pair_ref[rows] = jnp.where(first_core, both[share:], both[:share]).astype(BF16)
    total = None
    for k in range(3):
        part = dot(d0_ref[:, k * width : (k + 1) * width], w_ref[k])
        total = part if total is None else total + part
    dx_ref[...] = total


def attn_grads(where, d, x, o, dz, w):
    rows, width = o[0].shape
    columns = x[0].shape[1]
    return call(
        attn_grads_kernel,
        [
            ("v", shape((rows, columns), F32)),
            ("v", shape((2 * width, columns), F32)),
            ("v", shape((2 * width, columns))),
            ("v", shape((8, 2 * width), F32)),
        ],
        [("s", where)] + [("v", item) for item in (*d, *x, *o, *dz, w)],
        2.7,
    )


def split_kernel(where_ref, own_ref, got_ref, sent_ref, kept_ref):
    half = kept_ref.shape[0]
    first = where_ref[0] == 0
    top = own_ref[:half] + got_ref[:half].astype(F32)
    bottom = own_ref[half:] + got_ref[half:].astype(F32)
    kept_ref[...] = jnp.where(first, top, bottom)
    sent_ref[...] = jnp.where(first, bottom, top).astype(BF16)


def split(where, own, got):
    rows, columns = own.shape
    return call(
        split_kernel,
        [("v", shape((rows // 2, columns))), ("v", shape((rows // 2, columns), F32))],
        [("s", where), ("v", own), ("v", got)],
    )


def add_kernel(where_ref, *refs):
    parts, out_ref = len(refs) // 2, refs[-1]
    rows = refs[0].shape[0]
    for part in range(parts):
        total = refs[part][...] + refs[parts + part][...].astype(F32)
        out_ref[part * rows : (part + 1) * rows] = total.astype(BF16)


def halve_sum_kernel(bit, parts, where_ref, *refs):
    kept, got, (sent_ref, own_ref) = refs[:parts], refs[parts : 2 * parts], refs[2 * parts :]
    mine = (where_ref[3] >> bit) & 1
    if parts == 2:
        for half in range(2):

            @pl.when(mine == half)
            def _():
                own_ref[...] = kept[half][...] + got[half][...].astype(F32)
                sent_ref[...] = (kept[1 - half][...] + got[1 - half][...].astype(F32)).astype(BF16)

        return
    rows = own_ref.shape[0]
    at = pl.ds(pl.multiple_of(mine * rows, 16), rows)
    own_ref[...] = kept[0][at] + got[0][at].astype(F32)
    at = pl.ds(pl.multiple_of((1 - mine) * rows, 16), rows)
    sent_ref[...] = (kept[0][at] + got[0][at].astype(F32)).astype(BF16)


def join_kernel(bit, where_ref, own_ref, got_ref, out_ref):
    rows = own_ref.shape[0]
    mine = (where_ref[3] >> bit) & 1
    out_ref[pl.ds(pl.multiple_of(mine * rows, 16), rows)] = own_ref[...]
    out_ref[pl.ds(pl.multiple_of((1 - mine) * rows, 16), rows)] = got_ref[...]


def last_join_kernel(part, where_ref, own_ref, got_ref, later_ref, out_ref, sent_ref):
    join_kernel(0, where_ref, own_ref, got_ref, out_ref)
    rows = out_ref.shape[0]
    later = later_ref[part * rows : (part + 1) * rows]
    sent_ref[...] = jnp.where(where_ref[0] == 0, later, out_ref[...])


def results_kernel(kind, where_ref, *refs):
    *pieces, first_ref, second_ref, buffer, sems = refs
    copies = Copies(sems)
    first = where_ref[0] == 0
    rows = buffer.shape[1]
    half = rows // 2
    count = len(pieces) // 2
    size = rows // count

    def piece(refs, part):
        at = part * half
        return refs[at // size][at % size : at % size + half]

    for side in range(2):
        for part in range(2):
            at = slice(part * half, (part + 1) * half)
            ours, got = piece(pieces[:count], part), piece(pieces[count : 2 * count], part)
            values = jnp.where(first, ours, got) if side == 0 else jnp.where(first, got, pieces[-1][at])
            buffer[side, at] = values.astype(F32)
            if kind == "ffn":
                target = (first_ref, second_ref)[side].at[pl.ds(part * half, half)]
            else:
                k = 2 * side + part
                target = first_ref.at[k] if k < 3 else second_ref
            copies.start(buffer.at[side, pl.ds(part * half, half)], target)
    copies.done()


def results(kind, where, pieces):
    rows, columns = pieces[-1].shape
    if kind == "attn":
        outs = [shape((3, rows // 2, columns), F32), shape((rows // 2, columns), F32)]
    else:
        outs = [shape((rows, columns), F32)] * 2
    return call(
        partial(results_kernel, kind),
        [("h", item) for item in outs],
        [("s", where)] + [("v", item) for item in pieces],
        us=2.5,
        scratch=[pltpu.VMEM((2, rows, columns), F32)],
        copies=4,
    )


def pick_kernel(where_ref, first_in, second_in, out_ref, sems):
    copies = Copies(sems)
    first = where_ref[0] == 0
    copies.start_one([(first, second_in), (jnp.logical_not(first), first_in)], out_ref)
    copies.done()


def place_kernel(where_ref, first_in, second_in, got_ref, out_ref, buffer, sems):
    section = where_ref[0]
    copies = Copies(sems)
    copies.start_one([(section == 0, first_in), (section == 1, second_in)], buffer.at[section])
    buffer[1 - section] = got_ref[...]
    copies.done()
    out = Copies([sems.at[1]])
    out.start(buffer, out_ref.at[0])
    out.done()


def grad_in_kernel(where_ref, own_ref, far_ref, skip_ref, later_in, sent_ref, out_copy, later, out, sems):
    copies = Copies(sems)
    copies.start(later_in, later)
    grad = (own_ref[...] + far_ref[...].astype(F32) + skip_ref[...]).astype(BF16)
    out[...] = grad
    copies.start(out, out_copy)
    copies.done()
    sent_ref[...] = jnp.where(where_ref[0] == 0, later[...], grad)


def pack_sums_kernel(where_ref, *refs):
    own_ref, pair_ref = refs[-2:]
    for layer in range(2):
        norm1_ref, norm2_ref, up0_ref, up1_ref, qkv_ref = refs[5 * layer : 5 * layer + 5]
        at = 8 * layer
        for row, source in (
            (GAIN1, norm1_ref[0:1]),
            (GAIN2, norm2_ref[0:1]),
            (BIAS_OUT, norm1_ref[2:3]),
            (SHIFT1, norm1_ref[1:2]),
            (BIAS2, norm2_ref[2:3]),
            (SHIFT2, norm2_ref[1:2]),
            (7, qkv_ref[0:1]),
        ):
            own_ref[at + row : at + row + 1] = source
            pair_ref[at + row : at + row + 1] = source
        own_ref[at + 6 : at + 7] = up0_ref[0:1] + up1_ref[0:1]
        pair_ref[at + 6 : at + 7] = up0_ref[1:2] + up1_ref[1:2]


def small_add_kernel(where_ref, own_ref, got_ref, total_ref, shared_ref):
    total = own_ref[...] + got_ref[...]
    total_ref[...] = total
    row = lax.broadcasted_iota(jnp.int32, total.shape, 0)
    shared_ref[...] = jnp.where(row % 8 < BIAS_UP, total, 0.0)


def small_results_kernel(where_ref, own_ref, got_ref, *refs):
    outs, (gains, shifts, up, qkv_b), sems = refs[:4], refs[4:8], refs[8]
    total = own_ref[...] + got_ref[...]
    total = jnp.where(where_ref[0] == 0, total[:8], total[8:])
    gains[0] = total[0:2]
    shifts[0] = total[2:6]
    up[...] = total[6:7]
    local = qkv_b.shape[2]
    for k in range(2):
        both = total[7:8, 2 * k * local : 2 * (k + 1) * local]
        qkv_b[0, k : k + 1] = jnp.where(where_ref[1] == 0, both[:, :local], both[:, local:])
    copies = Copies(sems)
    for source, target in zip((gains, shifts, up, qkv_b), outs):
        copies.start(source, target)
    copies.done()


def swap(value, axis, bit):
    count = lax.axis_size(axis)
    return lax.ppermute(value, axis, [(source, source ^ bit) for source in range(count)])


def core_swap(value):
    return swap(value, "tensor", 1)


def chip_swap(value):
    return swap(value, "tensor", 2)


def tie(value, *after):
    return lax.optimization_barrier((value, *after))[0]


class Sum:
    def __init__(self, *pieces):
        self.sent, self.later = None, None
        self.kept = [kept for _, kept in pieces]
        self.got = [swap(sent, "pipe", 1) for sent, _ in pieces]
        count = lax.axis_size("dp")
        self.bits = count.bit_length() - 1
        self.halving = count == 1 << self.bits and self.kept[0].shape[0] % (16 * count) == 0

    def add(self, where):
        rows, columns = self.kept[0].shape
        (self.total,) = call(
            add_kernel,
            [("v", shape((rows * len(self.kept), columns)))],
            [("s", where)] + [("v", item) for item in (*self.kept, *self.got)],
        )
        return self.total

    def whole(self, where, *after):
        total = self.add(where)
        self.total = lax.psum(tie(total, *after), "dp")
        return total

    def halve(self, bit, where):
        parts = len(self.kept)
        rows, columns = self.kept[0].shape
        dims = (rows * parts // 2, columns)
        sent, kept = call(
            partial(halve_sum_kernel, bit, parts),
            [("v", shape(dims)), ("v", shape(dims, F32))],
            [("s", where)] + [("v", item) for item in (*self.kept, *self.got)],
        )
        self.kept, self.got = [kept], [swap(sent, "dp", 1 << bit)]
        return sent

    def join(self, bit, where):
        rows, columns = self.total.shape
        got = swap(self.total, "dp", 1 << bit)
        if bit or self.later is None:
            (self.total,) = call(
                partial(join_kernel, bit),
                [("v", shape((2 * rows, columns)))],
                [("s", where), ("v", self.total), ("v", got)],
            )
            return self.total
        later, part = self.later
        self.total, self.sent = call(
            partial(last_join_kernel, part),
            [("v", shape((2 * rows, columns)))] * 2,
            [("s", where), ("v", self.total), ("v", got), ("v", later.total)],
        )
        return self.total

    def steps(self):
        if not self.halving:
            return [self.whole]
        bits = range(self.bits)
        return (
            [partial(self.halve, bit) for bit in bits]
            + [self.add]
            + [partial(self.join, bit) for bit in reversed(bits)]
        )

    def finish(self):
        if self.sent is None:
            later, part = self.later
            rows = self.total.shape[0]
            piece = later.total[part * rows : (part + 1) * rows]
            self.sent = jnp.where(lax.axis_index("pipe") == 0, piece, self.total)
        self.other = swap(self.sent, "pipe", 1)


def layer_forward(layer, own_in, far_in, w_qkv, small, marks, where, hooks):
    own_q, own_kv, own_x_kept, own_q_kept = qkv(own_in, w_qkv, small)
    own_pair = core_swap(own_kv)
    far_q, far_kv, far_x_kept, far_q_kept = qkv(far_in, w_qkv, small)
    far_pair = core_swap(far_kv)
    w_out = hooks["out"](far_q)
    far_out, kv, kv_kept, far_o, far_lse = attn(
        layer, where, far_q, (own_kv, own_pair, far_kv, far_pair), marks, w_out
    )
    far_sent = far_out
    far_out = chip_swap(far_out)
    own_out, own_o, own_lse = attn(layer, where, own_q, (kv,), marks, w_out)
    own_h, hidden, resid1, own_h_kept = norm1(own_in, own_out, far_out, small)
    far_h = chip_swap(own_h)
    w_up, w_down = hooks["ffn"](far_sent, own_h)
    own_branch, own_act, own_slope = ffn(own_h, w_up, w_down, small, False)
    far_h = tie(far_h, own_branch)
    far_branch, far_act, far_slope, far_h_kept = ffn(far_h, w_up, w_down, small, True)
    own_branch = tie(own_branch, *hooks["next"](far_branch))
    output, resid2, output_kept = norm2(hidden, own_branch, chip_swap(far_branch), small)
    kept = dict(
        x=(own_x_kept, far_x_kept),
        q=(own_q_kept, far_q_kept),
        kv=kv_kept,
        lse=(own_lse, far_lse),
        o=(own_o, far_o),
        resid=(resid1, resid2),
        weights=(w_qkv, w_out, w_up, w_down),
        h=(own_h_kept, far_h_kept),
        act=(own_act, far_act),
        slope=(own_slope, far_slope),
    )
    return output, output_kept, kept


def layer_backward(layer, upstream, kept, small, marks, where, hooks):
    own_df, skip2, norm2_sums, *grad_in = norm2_back(upstream, kept["resid"][1], small)
    far_df = chip_swap(own_df)
    w_qkv, w_out, w_up, w_down = kept["weights"]
    own_slope, far_slope = load(layer, tie(where, own_df), [], kept["slope"])
    own_dh, own_du, own_db = ffn_back(own_df, own_slope, w_up, w_down, False)
    far_df = tie(far_df, own_dh, *hooks["df"](own_dh))
    far_dh, far_du, far_db = ffn_back(far_df, far_slope, w_up, w_down, True)
    names = ("act", "h", "q", "lse", "x", "o")
    kv, *rows = load(
        layer,
        tie(where, far_dh, *hooks["dh"](far_dh)),
        [],
        [kept["kv"]] + [item for name in names for item in kept[name]],
    )
    own_act, far_act, own_h, far_h, own_q, far_q, own_lse, far_lse, own_x, far_x, own_o, far_o = rows
    grads = (own_h, far_h, own_act, far_act, own_df, far_df, own_du, far_du)
    pair = ffn_pair(grads)
    got = [core_swap(item) for item in pair]
    own_dh = tie(own_dh, pair[0])
    own_dz, skip1, norm1_sums = norm1_back(own_dh, chip_swap(far_dh), skip2, kept["resid"][0], small)
    far_dz = chip_swap(own_dz)
    parts = ffn_own(tie(where, own_dz), grads, got)
    own_dq, own_dkv, own_send = attn_back(
        layer, 0, tie(where, parts[0]), own_dz, own_q, kv, marks, own_lse, w_out
    )
    own_pair = core_swap(own_send)
    far_dz = tie(far_dz, own_send, *hooks["dz"](own_send, parts))
    far_dq, far_dkv, far_send = attn_back(layer, 1, where, far_dz, far_q, kv, marks, far_lse, w_out)
    far_pair = core_swap(tie(far_send, *hooks["send"](far_send)))
    far_dx, own_d, far_d = row_grads(
        small, (own_dq, far_dq), (own_dkv, far_dkv), (own_pair, far_pair), w_qkv
    )
    own_dx, attn_own, attn_pair, qkv_sums = attn_grads(
        tie(where, far_dx, *hooks["dx"](far_dx)),
        (own_d, far_d),
        (own_x, far_x),
        (own_o, far_o),
        (own_dz, far_dz),
        w_qkv,
    )
    far_dx = chip_swap(far_dx)
    sums = (norm1_sums, norm2_sums, own_db, far_db, qkv_sums)
    return (own_dx, far_dx, skip1), grad_in, sums, (attn_own, core_swap(attn_pair))


def body(
    tokens,
    segment_ids,
    pad_mask,
    block_perm,
    qkv_weight,
    qkv_bias,
    out_weight,
    up_weight,
    up_bias,
    down_weight,
    norm_gain,
    shift_bias,
    cotangent,
):
    section = lax.axis_index("pipe")
    place = lax.axis_index("tensor")
    replica = lax.axis_index("dp")
    paired = lax.axis_size("dp") % 2 == 0
    width = tokens.shape[2]
    local = qkv_bias.shape[2]
    here = jnp.stack([section, place % 2, replica % 2, replica, place]).astype(jnp.int32)
    qkv_rows = jnp.transpose(qkv_weight[0], (0, 2, 1))

    def other_half(half, whole):
        if paired:
            return swap(half, "dp", 1)
        even = replica % 2 == 0
        rest = jnp.where(even, whole[..., width // 2 :], whole[..., : width // 2])
        return swap(rest, "pipe", 1)

    (qkv_half,) = halves_of(here, qkv_rows)
    qkv_x = swap(qkv_half, "pipe", 1)
    rows = lax.optimization_barrier(lax.dynamic_index_in_dim(tokens, section, 0, keepdims=False))
    far_rows = chip_swap(rows)
    (own_small,) = call(
        pack_kernel,
        [("v", shape((16, width), F32))],
        [("h", norm_gain), ("h", shift_bias), ("h", up_bias), ("h", qkv_bias), ("s", block_perm)],
        scratch=[
            pltpu.VMEM(item.shape, item.dtype) for item in (norm_gain, shift_bias, up_bias, qkv_bias)
        ],
        copies=4,
    )
    other_small = swap(own_small, "pipe", 1)
    up_half, down_half = halves_of(tie(here, own_small, qkv_half), up_weight, down_weight)
    up_x = swap(up_half, "pipe", 1)
    out_x = swap(tie(out_weight, qkv_x), "pipe", 1)
    (marks,) = call(
        marks_kernel,
        [("v", shape((8, segment_ids.shape[1] // 2), jnp.int32))],
        [("s", tie(here, up_x)), ("v", segment_ids), ("v", pad_mask)],
    )
    *smalls, flags = call(
        params_kernel,
        [("v", shape((16, width), F32))] * 2 + [("h", shape((8, PAIR), F32))],
        [("s", here)]
        + [
            ("v", item)
            for item in (own_small, other_small, core_swap(own_small), core_swap(other_small))
        ],
        scratch=[pltpu.VMEM((8, PAIR), F32)],
        copies=1,
    )
    heads = 2 * block_perm.shape[1]
    where = jnp.concatenate([here, flags[:2, :heads].reshape(-1).astype(jnp.int32)])
    def item(by_core, own, other, after=(), later=()):
        pair_own = core_swap(tie(own, *after) if after else own)
        pair_other = tuple(core_swap(tie(part, *later) if later else part) for part in other)
        return by_core, own, other, pair_own, pair_other

    other_qkv = other_half(tie(qkv_x, up_half, other_small, far_rows), qkv_rows)
    items = dict(qkv=item(True, qkv_rows, (qkv_x, other_qkv)))
    (first_qkv,) = load(0, tie(where, marks, *smalls, far_rows, up_x), [items["qkv"]])

    def first_out(after):
        fetched["down"] = swap(tie(down_half, up_x), "pipe", 1)
        fetched["up"] = other_half(tie(up_x, marks), up_weight)
        items["out"] = item(True, out_weight, (out_x,), (first_qkv,), (first_qkv,))
        return load(0, tie(where, after), [items["out"]])[0]

    fetched = {}

    def first_ffn(early, after):
        down_x = fetched["down"]
        other_down = other_half(tie(down_x, early), down_weight)
        items["up"] = item(False, up_weight, (up_x, fetched["up"]), (early,), (early,))
        items["down"] = item(False, down_weight, (down_x, other_down), (early,), (after,))
        return load_ffn(0, (), tie(where, after))

    def load_ffn(layer, arrays, after):
        return load(layer, after, [items["up"], items["down"]], arrays)

    second = []

    def load_second(after):
        second.extend(load(1, tie(where, after), [items["qkv"], items["out"]]))
        return second

    out_first, first_kept, kept_first = layer_forward(
        0,
        rows,
        far_rows,
        first_qkv,
        smalls[0],
        marks,
        where,
        {"out": first_out, "ffn": first_ffn, "next": load_second},
    )
    def second_ffn(early, after):
        return load_ffn(1, (), tie(where, after))

    out_second, second_kept, kept_second = layer_forward(
        1,
        out_first,
        chip_swap(out_first),
        second[0],
        smalls[1],
        marks,
        where,
        {
            "out": lambda after: second[1],
            "ffn": second_ffn,
            "next": lambda after: (),
        },
    )

    def place_outputs(first, second, got, after):
        return call(
            place_kernel,
            [("h", shape((1, 2) + first.shape))],
            [("s", after), ("h", first), ("h", second), ("v", got)],
            us=1.5,
            scratch=[pltpu.VMEM((2,) + first.shape, BF16)],
            copies=2,
        )[0]

    sums, steps = {}, {}

    def begin(name, *pieces):
        sums[name] = Sum(*pieces)
        steps[name] = sums[name].steps()

    def run(after, *names):
        for name in names:
            if steps[name]:
                after = steps[name].pop(0)(tie(where, after))
        return after

    upstream = lax.dynamic_index_in_dim(cotangent, section, 0, keepdims=False)
    outputs = []

    def nothing(*_):
        return ()

    def later_df(after):
        (picked,) = call(
            pick_kernel,
            [("v", shape(rows.shape))],
            [("s", tie(where, after)), ("h", first_kept), ("h", second_kept)],
            copies=1,
        )
        outputs.append(swap(picked, "pipe", 1))
        return (picked,)

    def later_dz(after, parts):
        begin("ab1", parts[0:2], parts[2:4])
        return outputs

    grads, _, small_second, attn_second = layer_backward(
        1,
        (upstream,),
        kept_second,
        smalls[1],
        marks,
        where,
        {
            "df": later_df,
            "dh": nothing,
            "dz": later_dz,
            "send": lambda after: sums["ab1"].got[:1],
            "dx": nothing,
        },
    )

    def first_df(after):
        sent, kept = split(tie(where, after), *attn_second)
        begin("c1", (sent, kept))
        return (run(sent, "ab1"),)

    def first_dz(after, parts):
        begin("a0", parts[0:2])
        begin("b0", parts[2:4])
        return (run(after, "ab1", "c1"),)

    def first_send(after):
        return (run(after, "ab1", "c1", "a0"),)

    def first_dx(after):
        return (run(after, "c1", "a0", "b0"),)

    grads, (grad_second,), small_first, attn_first = layer_backward(
        0,
        grads,
        kept_first,
        smalls[0],
        marks,
        where,
        {"df": first_df, "dh": nothing, "dz": first_dz, "send": first_send, "dx": nothing},
    )
    last = [attn_first[0]]

    def now():
        return tie(where, *last)

    def then(*values):
        last[:] = values

    def step(*names):
        then(run(last[-1], *names))

    def small_add(total, got):
        total, shared = call(
            small_add_kernel,
            [("v", shape((16, width), F32))] * 2,
            [("s", now()), ("v", total), ("v", got)],
        )
        then(total)
        return total, shared

    hops = [("pipe", 1)]
    count = lax.axis_size("dp")
    if not count & (count - 1):
        hops += [("dp", 1 << bit) for bit in range(count.bit_length() - 1)]
    total, pair_sums = call(
        pack_sums_kernel,
        [("v", shape((16, width), F32))] * 2,
        [("s", now())] + [("v", value) for value in (*small_first, *small_second)],
    )
    then(total)
    got = core_swap(pair_sums)
    sent, kept = split(now(), *attn_first)
    then(sent)
    begin("c0", (sent, kept))
    step("c1", "a0", "b0", "c0")
    total, shared = small_add(total, got)
    got = chip_swap(shared)
    step("a0", "b0", "c1", "ab1")
    total, _ = small_add(total, got)
    if len(hops) == 1:
        total = lax.psum(total, "dp")
    got = swap(total, *hops[0])
    sent, grad_first = call(
        grad_in_kernel,
        [("v", shape(rows.shape)), ("h", shape(rows.shape))],
        [("s", now())] + [("v", value) for value in grads] + [("h", grad_second)],
        scratch=[pltpu.VMEM(rows.shape, BF16)] * 2,
        copies=2,
    )
    then(sent)
    grad_got = swap(sent, "pipe", 1)
    step("a0", "c0", "b0")
    while steps["c1"]:
        step("c1")
    then(last[-1], grad_got)

    def last_of(*names):
        for name in names:
            while steps[name]:
                step(name)

    def finish(name, later, part):
        sums[name].later = (sums[later], part)
        last_of(name)
        sums[name].finish()

    for at, hop in enumerate(hops[1:]):
        total, _ = small_add(total, got)
        got = swap(total, *hop)
        if at == 0:
            step("c0", "b0")
            last_of("ab1")
            finish("a0", "ab1", 0)
        elif at == 1:
            step("c0")
            finish("b0", "ab1", 1)
    if len(hops) < 2:
        last_of("ab1")
        finish("a0", "ab1", 0)
    if len(hops) < 3:
        finish("b0", "ab1", 1)
    then(last[-1], sums["a0"].other)
    input_grad = place_outputs(grad_first, grad_second, grad_got, now())
    layer_out = place_outputs(first_kept, second_kept, outputs[0], tie(where, input_grad))
    then(layer_out)
    finish("c0", "c1", 0)
    outs = [shape(item.shape, F32) for item in (norm_gain, shift_bias, up_bias, qkv_bias)]
    gains, shifts, upb, qkvb = call(
        small_results_kernel,
        [("h", item) for item in outs],
        [("s", now()), ("v", total), ("v", got)],
        scratch=[pltpu.VMEM(item.shape, F32) for item in outs],
        copies=4,
    )
    then(gains)

    def pieces(later, *names):
        return [
            *(sums[name].total for name in names),
            *(sums[name].other for name in names),
            sums[later].total,
        ]

    upw, downw = results("ffn", now(), pieces("ab1", "a0", "b0"))
    qkvw, outw = results("attn", tie(where, upw), pieces("c1", "c0"))
    qkvw = jnp.transpose(qkvw, (0, 2, 1))
    return (
        layer_out,
        input_grad,
        qkvw[None],
        qkvb,
        outw[None],
        upw[None],
        upb,
        downw[None],
        gains,
        shifts,
    )


def solution(mesh):
    return jax.shard_map(
        body,
        mesh=mesh,
        in_specs=(
            P("dp", "tensor", None),
            P("dp", None),
            P("dp", None),
            P("pipe", "tensor", None),
            P("pipe", None, None, "tensor"),
            P("pipe", None, "tensor"),
            P("pipe", "tensor", None),
            P("pipe", None, "tensor"),
            P("pipe", "tensor"),
            P("pipe", "tensor", None),
            P("pipe", None, None),
            P("pipe", None, None),
            P("dp", "tensor", None),
        ),
        out_specs=(
            P("pipe", "dp", "tensor", None),
            P("pipe", "dp", "tensor", None),
            P("pipe", None, None, "tensor"),
            P("pipe", None, "tensor"),
            P("pipe", "tensor", None),
            P("pipe", None, "tensor"),
            P("pipe", "tensor"),
            P("pipe", "tensor", None),
            P("pipe", None, None),
            P("pipe", None, None),
        ),
        check_vma=False,
    )
```

```python
from functools import partial

import jax
import jax.numpy as jnp
from jax import lax
from jax.experimental import pallas as pl
from jax.experimental.pallas import tpu as pltpu
from jax.sharding import PartitionSpec as P

BF16 = jnp.bfloat16
F32 = jnp.float32
HEAD_DIM = 64
PAIR = 2 * HEAD_DIM
LOG2E = 1.4426950408889634
MASKED = -1e30
VMEM_LIMIT = 16 * 1024 * 1024
COST = 2e10
NORM_EPSILON_TERM = 1e-06

FLAGS = 5

SPACES = {"v": pltpu.VMEM, "s": pltpu.SMEM, "h": pl.ANY}
PLACES = {"v": pltpu.VMEM, "s": pl.ANY, "h": pltpu.HBM}


def shape(dims, dtype=BF16):
    return jax.ShapeDtypeStruct(dims, dtype)


def call(kernel, outs, args, us=0.1, scratch=(), copies=0):
    flops = int(us * COST)
    scratch = list(scratch)
    if copies:
        scratch.append(pltpu.SemaphoreType.DMA((copies,)))
    return pl.pallas_call(
        kernel,
        name=(kernel.func if isinstance(kernel, partial) else kernel).__name__,
        out_shape=[PLACES[space](item.shape, item.dtype) for space, item in outs],
        in_specs=[pl.BlockSpec(memory_space=SPACES[space]) for space, _ in args],
        out_specs=[pl.BlockSpec(memory_space=SPACES[space]) for space, _ in outs],
        scratch_shapes=scratch,
        compiler_params=pltpu.CompilerParams(vmem_limit_bytes=VMEM_LIMIT),
        cost_estimate=pl.CostEstimate(flops=flops, bytes_accessed=0, transcendentals=0),
    )(*[pltpu.with_memory_space_constraint(item, PLACES[space]) for space, item in args])


class Copies:
    def __init__(self, sems):
        self.sems, self.pending = sems, []

    def sem(self):
        at = len(self.pending)
        return self.sems[at] if isinstance(self.sems, list) else self.sems.at[at]

    def start(self, source, target):
        copy = pltpu.make_async_copy(source, target, self.sem())
        copy.start()
        self.pending.append(copy)

    def start_one(self, cases, target):
        sem = self.sem()
        made = []
        for condition, source in cases:
            made.append(pltpu.make_async_copy(source, target, sem))
            pl.when(condition)(made[-1].start)
        self.pending.append(made[0])

    def done(self):
        for copy in self.pending:
            copy.wait()


def loop(count, step):
    lax.fori_loop(0, count, lambda i, _: step(i), None)


def part_of(i, size):
    return pl.ds(pl.multiple_of(i * size, size), size)


def dot(left, right):
    return jnp.dot(left, right, preferred_element_type=F32)


def dot_tn(left, right):
    return lax.dot_general(left, right, (((0,), (0,)), ((), ())), preferred_element_type=F32)


def dot_nt(left, right):
    return lax.dot_general(left, right, (((1,), (1,)), ((), ())), preferred_element_type=F32)


def pack_kernel(gains_in, shifts_in, up_in, qkv_in, perm_ref, out_ref, gains, shifts, up, qkv_b, sems):
    copies = Copies(sems)
    for source, target in ((gains_in, gains), (shifts_in, shifts), (up_in, up), (qkv_in, qkv_b)):
        copies.start(source, target)
    out_ref[...] = jnp.zeros_like(out_ref)
    lane = lax.broadcasted_iota(jnp.int32, (1, out_ref.shape[1]), 1)
    flags = jnp.zeros((1, out_ref.shape[1]), F32)
    for head in range(perm_ref.shape[1]):
        flags = jnp.where(lane == head, perm_ref[0, head, 0].astype(F32), flags)
    out_ref[9:10] = flags
    copies.done()
    out_ref[0:2] = gains[0]
    out_ref[2:6] = shifts[0]
    out_ref[6:7] = up[...].astype(F32)
    out_ref[7:9, 0 : qkv_b.shape[2]] = qkv_b[0].astype(F32)


GAIN1, GAIN2, BIAS_OUT, SHIFT1, BIAS2, SHIFT2, BIAS_UP, BIAS_Q, TURNED = 0, 1, 2, 3, 4, 5, 6, 8, 10


def params_kernel(where_ref, own_ref, other_ref, pair_ref, other_pair_ref, first_out, second_out, flags_copy, flags, sems):
    section, core = where_ref[0], where_ref[1]
    width = own_ref.shape[1]
    local = width // 4
    heads = local // HEAD_DIM
    lane = lax.broadcasted_iota(jnp.int32, (1, width), 1)
    flags[...] = jnp.zeros_like(flags)
    for layer, out_ref in enumerate((first_out, second_out)):
        here = section == layer
        mine = jnp.where(here, own_ref[...], other_ref[...])
        pair = jnp.where(here, pair_ref[...], other_pair_ref[...])
        first = jnp.where(core == 0, mine, pair)
        second = jnp.where(core == 0, pair, mine)
        out_ref[...] = mine
        out_ref[BIAS_UP + 1 : BIAS_UP + 2] = pair[BIAS_UP : BIAS_UP + 1]
        biases = jnp.where(lane < local, first, pltpu.roll(second, local, 1))
        out_ref[BIAS_Q : BIAS_Q + 2] = biases[7:9]
        turned = jnp.where(lane < heads, first, pltpu.roll(second, heads, 1))[9:10]
        lanes = jnp.zeros((1, width), F32)
        for head in range(2 * heads):
            chosen = (lane // HEAD_DIM) % (2 * heads) == head
            lanes = jnp.where(chosen, turned[:, head : head + 1], lanes)
        out_ref[TURNED : TURNED + 1] = lanes
        flags[layer : layer + 1] = turned[:, 0:PAIR]
    copies = Copies(sems)
    copies.start(flags, flags_copy)
    copies.done()


def marks_kernel(where_ref, segments_ref, real_ref, out_ref):
    quarter = out_ref.shape[1] // 2
    out_ref[...] = jnp.zeros_like(out_ref)
    for r in range(4):
        cols = pl.ds(pl.multiple_of((where_ref[4] ^ r) * quarter, PAIR), quarter)
        at = slice((r % 2) * quarter, (r % 2 + 1) * quarter)
        segment = jnp.where(where_ref[0] == 0, segments_ref[0:1, cols], segments_ref[1:2, cols])
        real = jnp.where(where_ref[0] == 0, real_ref[0:1, cols], real_ref[1:2, cols])
        out_ref[1 + r // 2 : 2 + r // 2, at] = jnp.where(real == 1, segment, -1)
        if r % 2 == 0:
            out_ref[0:1, (r // 2) * quarter : (r // 2 + 1) * quarter] = segment


def halve_kernel(where_ref, *refs):
    count = len(refs) // 2
    copies = Copies(refs[-1])
    for source, half in zip(refs[:count], refs[count:-1]):
        columns = half.shape[2]
        copies.start_one(
            [
                (where_ref[2] == side, source.at[:, :, pl.ds(side * columns, columns)])
                for side in range(2)
            ],
            half,
        )
    copies.done()


def halves_of(where, *wholes):
    return call(
        halve_kernel,
        [("v", shape(whole.shape[:2] + (whole.shape[2] // 2,))) for whole in wholes],
        [("s", where)] + [("h", whole) for whole in wholes],
        copies=len(wholes),
    )


def weight_copies(copies, where_ref, layer, k, own, other, target):
    here = where_ref[0] == layer
    if len(other) == 1:
        copies.start_one(
            [(here, own.at[k]), (jnp.logical_not(here), other[0].at[k])], target(slice(None))
        )
        return
    columns = other[0].shape[-1]
    for side in range(2):
        cols = pl.ds(side * columns, columns)
        direct = where_ref[2] == side
        copies.start_one(
            [
                (here, own.at[k, :, cols]),
                (jnp.logical_not(here) & direct, other[0].at[k]),
                (jnp.logical_not(here) & jnp.logical_not(direct), other[1].at[k]),
            ],
            target(cols),
        )


def load_kernel(layer, items, plain, where_ref, *refs):
    sems = refs[-1]
    copies = Copies(sems)
    count = sum(2 * (1 + parts) for _, parts in items)
    sources, plain_in, outs = refs[:count], refs[count : count + plain], refs[count + plain : -1]
    for (by_core, parts), out_ref in zip(items, outs):
        for pair in range(2):
            own, *other = sources[: 1 + parts]
            sources = sources[1 + parts :]
            if by_core:
                rows = out_ref.shape[1] // 2
                slot = (where_ref[1] + pair) % 2
                at = pl.ds(pl.multiple_of(slot * rows, rows), rows)
                for k in range(out_ref.shape[0]):
                    weight_copies(
                        copies, where_ref, layer, k, own, other, lambda cols, k=k: out_ref.at[k, at, cols]
                    )
            else:
                weight_copies(
                    copies, where_ref, layer, 0, own, other, lambda cols: out_ref.at[pair, :, cols]
                )
    for source, target in zip(plain_in, outs[len(items) :]):
        copies.start(source, target)
    copies.done()


def load(layer, where, items, arrays=()):
    outs, sources, kinds, count = [], [], [], len(arrays)
    for by_core, own, other, pair_own, pair_other in items:
        k, rows, columns = own.shape
        outs.append(shape((k, 2 * rows, columns)) if by_core else shape((2, rows, columns)))
        sources += [own, *other, pair_own, *pair_other]
        kinds.append((by_core, len(other)))
        count += 2 * k * len(other)
    outs += [shape(item.shape, item.dtype) for item in arrays]
    return call(
        partial(load_kernel, layer, kinds, len(arrays)),
        [("v", item) for item in outs],
        [("s", where)] + [("h", item) for item in (*sources, *arrays)],
        us=2.4,
        copies=count,
    )


def qkv_kernel(x_ref, w_ref, b_ref, q_ref, kv_ref, x_copy, q_copy, sems):
    copies = Copies(sems)
    copies.start(x_ref, x_copy)
    x = x_ref[...]
    width = q_ref.shape[1]
    q_ref[...] = (dot_nt(x, w_ref[0]) + b_ref[BIAS_Q : BIAS_Q + 1, :width]).astype(BF16)
    copies.start(q_ref, q_copy)
    kv_ref[:, :width] = dot_nt(x, w_ref[1]).astype(BF16)
    kv_ref[:, width:] = (dot_nt(x, w_ref[2]) + b_ref[BIAS_Q + 1 : BIAS_Q + 2, :width]).astype(BF16)
    copies.done()


def qkv(x, w, b):
    rows, width = x.shape[0], w.shape[1]
    return call(
        qkv_kernel,
        [
            ("v", shape((rows, width))),
            ("v", shape((rows, 2 * width))),
            ("h", shape(x.shape)),
            ("h", shape((rows, width))),
        ],
        [("v", x), ("v", w), ("v", b)],
        1.1,
        copies=2,
    )


def lanes_of(rows):
    return lax.broadcasted_iota(jnp.int32, (rows, PAIR), 1)


def fill_bias(bias, side, marks_ref):
    rows = bias.shape[1]
    wanted = jnp.transpose(marks_ref[:, side * rows : (side + 1) * rows])[:, 0:1]
    for j in range(2):
        bias[j] = jnp.where(wanted == marks_ref[1 + j : 2 + j, :], 0.0, MASKED).astype(F32)


def block_of(where_ref, layer, head, turned):
    return where_ref[FLAGS + 6 * layer + head] ^ turned


def attn_rows(layer, where_ref, turned, q_ref, kv_ref, marks_ref, o_ref, lse_ref, bias):
    rows, width = q_ref.shape
    fill_bias(bias, turned, marks_ref)
    lanes = lanes_of(rows)
    low = lanes < HEAD_DIM
    scale = HEAD_DIM**-0.5 * LOG2E
    lse_ref[...] = jnp.zeros_like(lse_ref)

    def step(tile):
        cols, vcols = part_of(tile, PAIR), part_of(tile + width // PAIR, PAIR)
        q = q_ref[:, cols]
        mixed = []
        for side in range(2):
            head = 2 * tile + side
            block = block_of(where_ref, layer, head, turned)
            q_head = jnp.where(low if side == 0 else ~low, q, jnp.zeros_like(q))
            s = dot_nt(q_head, kv_ref[block, :, cols]) * scale + bias[block]
            top = jnp.maximum(jnp.max(s, axis=1, keepdims=True), 0.0)
            e = jnp.exp2(s - top)
            total = jnp.exp2(-top) + jnp.sum(e, axis=1, keepdims=True)
            p = (e * (1.0 / total)).astype(BF16)
            mixed.append(dot(p, kv_ref[block, :, vcols]))
            lse_ref[...] = jnp.where(lanes == head, top + jnp.log2(total), lse_ref[...])
        o_ref[:, cols] = jnp.where(low, mixed[0], mixed[1]).astype(BF16)

    loop(width // PAIR, step)


def attn_far_kernel(
    layer, where_ref, q_ref, kv0_ref, kv1_ref, kv2_ref, kv3_ref, marks_ref, w_ref,
    out_ref, kv_ref, kv_copy, o_copy, lse_copy, bias, o_ref, lse_ref, sems,
):
    copies = Copies(sems)
    half = kv0_ref.shape[0]
    for block, pair in enumerate(((kv0_ref, kv1_ref), (kv2_ref, kv3_ref))):
        kv_ref[block, :half] = pair[0][...]
        kv_ref[block, half:] = pair[1][...]
    copies.start(kv_ref, kv_copy)
    attn_rows(layer, where_ref, 1, q_ref, kv_ref, marks_ref, o_ref, lse_ref, bias)
    copies.start(o_ref, o_copy)
    copies.start(lse_ref, lse_copy)
    out_ref[...] = dot(o_ref[...], w_ref[0]).astype(out_ref.dtype)
    copies.done()


def attn_own_kernel(
    layer, where_ref, q_ref, kv_ref, marks_ref, w_ref, out_ref, o_copy, lse_copy, bias, o_ref, lse_ref, sems
):
    copies = Copies(sems)
    attn_rows(layer, where_ref, 0, q_ref, kv_ref, marks_ref, o_ref, lse_ref, bias)
    copies.start(o_ref, o_copy)
    copies.start(lse_ref, lse_copy)
    out_ref[...] = dot(o_ref[...], w_ref[0]).astype(out_ref.dtype)
    copies.done()


def attn(layer, where, q, kv, marks, w):
    rows, width = q.shape
    far = len(kv) > 1
    outs = [("v", shape((rows, w.shape[2]), BF16 if far else F32))]
    if far:
        joined = shape((2, 2 * rows, kv[0].shape[1]))
        outs += [("v", joined), ("h", joined)]
    outs += [("h", shape((rows, width))), ("h", shape((rows, PAIR), F32))]
    args = [("s", where)] + [("v", item) for item in (q, *kv, marks, w)]
    return call(
        partial(attn_far_kernel if far else attn_own_kernel, layer),
        outs,
        args,
        4.6,
        scratch=[
            pltpu.VMEM((2, rows, 2 * rows), F32),
            pltpu.VMEM((rows, width), BF16),
            pltpu.VMEM((rows, PAIR), F32),
        ],
        copies=3 if far else 2,
    )


def normed_rows(resid):
    centred = resid - jnp.mean(resid, axis=1, keepdims=True)
    inverse = lax.rsqrt(jnp.mean(centred * centred, axis=1, keepdims=True) + NORM_EPSILON_TERM)
    return centred * inverse, inverse


def norm1_kernel(x_ref, own_ref, far_ref, norms_ref, low_ref, full_ref, resid_copy, low_copy, resid, sems):
    copies = Copies(sems)
    projected = own_ref[...] + far_ref[...].astype(F32)
    total = x_ref[...].astype(F32) + projected + norms_ref[BIAS_OUT : BIAS_OUT + 1, :]
    resid[...] = total
    copies.start(resid, resid_copy)
    hidden = normed_rows(total)[0] * norms_ref[GAIN1 : GAIN1 + 1, :] + norms_ref[SHIFT1 : SHIFT1 + 1, :]
    full_ref[...] = hidden
    low_ref[...] = hidden.astype(BF16)
    copies.start(low_ref, low_copy)
    copies.done()


def norm1(x, own, far, norms):
    return call(
        norm1_kernel,
        [("v", shape(x.shape)), ("v", shape(x.shape, F32)), ("h", shape(x.shape, F32)), ("h", shape(x.shape))],
        [("v", x), ("v", own), ("v", far), ("v", norms)],
        scratch=[pltpu.VMEM(x.shape, F32)],
        us=1.2,
        copies=2,
    )


def norm2_kernel(h_ref, own_ref, far_ref, norms_ref, low_ref, resid_copy, low_copy, resid, sems):
    copies = Copies(sems)
    branch = own_ref[...] + far_ref[...].astype(F32)
    total = h_ref[...] + branch + norms_ref[BIAS2 : BIAS2 + 1, :]
    resid[...] = total
    copies.start(resid, resid_copy)
    out = normed_rows(total)[0] * norms_ref[GAIN2 : GAIN2 + 1, :] + norms_ref[SHIFT2 : SHIFT2 + 1, :]
    low_ref[...] = out.astype(BF16)
    copies.start(low_ref, low_copy)
    copies.done()


def norm2(h, own, far, norms):
    return call(
        norm2_kernel,
        [("v", shape(h.shape)), ("h", shape(h.shape, F32)), ("h", shape(h.shape))],
        [("v", h), ("v", own), ("v", far), ("v", norms)],
        scratch=[pltpu.VMEM(h.shape, F32)],
        us=1.2,
        copies=2,
    )


TAIL = tuple(
    0.5 * c
    for c in (
        0.05029408002973294, -0.1830316054165625, 0.16930258232763196, -0.005798692821681883,
        0.14152663657068731, 0.16851528425000623, 0.20784663429852349, 0.22566934002005623,
        0.22567586682378352,
    )
)


def gelu_and_slope(u):
    bell = jnp.exp2(u * u * (-0.5 * LOG2E))
    t = 1.0 / (1.0 + jnp.abs(u) * (0.4 * 0.5**0.5))
    poly = TAIL[0]
    for c in TAIL[1:]:
        poly = poly * t + c
    tail = poly * t * bell
    below = jnp.where(u < 0.0, tail, 1.0 - tail)
    return u * below, below + u * bell * 0.3989422804014327


UNITS = 768


def ffn_kernel(far, h_ref, up_ref, down_ref, b_ref, out_ref, act_copy, slope_copy, *rest):
    act_ref, slope_ref, total_ref, sems = rest[-4:]
    steps = up_ref.shape[2] // UNITS
    if far:
        rows_copy = pltpu.make_async_copy(h_ref, rest[0], sems.at[4 * steps])
        rows_copy.start()
    total_ref[...] = jnp.zeros_like(total_ref)

    def copies_of(i):
        half, cols = i // steps, part_of(i % steps, UNITS)
        return [
            pltpu.make_async_copy(kept.at[half, :, cols], copy.at[half, :, cols], sems.at[2 * i + k])
            for k, (kept, copy) in enumerate(((act_ref, act_copy), (slope_ref, slope_copy)))
        ]

    def step(i):
        half, cols = i // steps, part_of(i % steps, UNITS)
        pre = dot(h_ref[...], up_ref[half, :, cols]) + b_ref[pl.ds(BIAS_UP + half, 1), cols]
        act, slope = gelu_and_slope(pre)
        act = act.astype(BF16)
        act_ref[half, :, cols] = act
        slope_ref[half, :, cols] = slope.astype(BF16)
        for copy in copies_of(i):
            copy.start()
        total_ref[...] += dot(act, down_ref[half, cols, :])

    loop(2 * steps, step)
    out_ref[...] = total_ref[...].astype(out_ref.dtype)

    def finish(i):
        for copy in copies_of(i):
            copy.wait()

    loop(2 * steps, finish)
    if far:
        rows_copy.wait()


def ffn(h, up, down, b, far):
    rows, width = h.shape
    units = up.shape[2]
    outs = [
        ("v", shape((rows, width), BF16 if far else F32)),
        ("h", shape((2, rows, units))),
        ("h", shape((2, rows, units))),
    ]
    if far:
        outs.append(("h", shape(h.shape)))
    return call(
        partial(ffn_kernel, far),
        outs,
        [("v", h), ("v", up), ("v", down), ("v", b)],
        0.1,
        scratch=[pltpu.VMEM((2, rows, units), BF16)] * 2 + [pltpu.VMEM((rows, width), F32)],
        copies=4 * (units // UNITS) + 1,
    )


def norm_back(upstream, resid, gain, low_ref, full_ref, sums_ref):
    normed, inverse = normed_rows(resid)
    scaled = upstream * gain
    inner = (
        scaled
        - jnp.mean(scaled, axis=1, keepdims=True)
        - normed * jnp.mean(scaled * normed, axis=1, keepdims=True)
    )
    grad = inverse * inner
    full_ref[...] = grad
    low_ref[...] = grad.astype(BF16)
    sums_ref[...] = jnp.zeros_like(sums_ref)
    sums_ref[0:1] = jnp.sum(upstream * normed, axis=0, keepdims=True)
    sums_ref[1:2] = jnp.sum(upstream, axis=0, keepdims=True)
    sums_ref[2:3] = jnp.sum(grad, axis=0, keepdims=True)


def norm2_back_kernel(inner, *refs):
    if inner:
        own_ref, far_ref, resid1_ref, resid_in, norms_ref, *refs = refs
        low_ref, full_ref, sums_ref, grad_copy, resid, grad_ref, sems = refs
    else:
        up_ref, resid_in, norms_ref, low_ref, full_ref, sums_ref, resid, sems = refs
    copies = Copies(sems)
    copies.start(resid_in, resid)
    if inner:
        grad_in = (own_ref[...] + far_ref[...].astype(F32) + resid1_ref[...]).astype(BF16)
        grad_ref[...] = grad_in
        copies.start(grad_ref, grad_copy)
    else:
        grad_in = up_ref[...]
    copies.done()
    gain = norms_ref[GAIN2 : GAIN2 + 1, :]
    norm_back(grad_in.astype(F32), resid[...], gain, low_ref, full_ref, sums_ref)


def turn_kernel(h_ref, own_ref, far_ref, up_ref, norms_ref, low_ref, full_ref, sums_ref, out_copy, out, sems):
    branch = own_ref[...] + far_ref[...].astype(F32)
    resid = h_ref[...] + branch + norms_ref[BIAS2 : BIAS2 + 1, :]
    gain = norms_ref[GAIN2 : GAIN2 + 1, :]
    out[...] = (normed_rows(resid)[0] * gain + norms_ref[SHIFT2 : SHIFT2 + 1, :]).astype(BF16)
    copies = Copies(sems)
    copies.start(out, out_copy)
    norm_back(up_ref[...].astype(F32), resid, gain, low_ref, full_ref, sums_ref)
    copies.done()


def turn(h, own, far, upstream, norms):
    dims = h.shape
    return call(
        turn_kernel,
        [
            ("v", shape(dims)),
            ("v", shape(dims, F32)),
            ("v", shape((8, dims[1]), F32)),
            ("h", shape(dims)),
        ],
        [("v", item) for item in (h, own, far, upstream, norms)],
        scratch=[pltpu.VMEM(dims, BF16)],
        us=2.5,
        copies=1,
    )


def norm2_back(upstream, resid, norms):
    dims = upstream[0].shape
    inner = len(upstream) > 1
    outs = [("v", shape(dims)), ("v", shape(dims, F32)), ("v", shape((8, dims[1]), F32))]
    scratch = [pltpu.VMEM(dims, F32)]
    if inner:
        outs.append(("h", shape(dims)))
        scratch.append(pltpu.VMEM(dims, BF16))
    return call(
        partial(norm2_back_kernel, inner),
        outs,
        [("v", item) for item in upstream] + [("h", resid), ("v", norms)],
        scratch=scratch,
        us=1.7,
        copies=2,
    )


def norm1_back_kernel(own_ref, far_ref, skip_ref, resid_in, norms_ref, low_ref, full_ref, sums_ref, resid, sems):
    copies = Copies(sems)
    copies.start(resid_in, resid)
    upstream = own_ref[...] + far_ref[...].astype(F32) + skip_ref[...]
    copies.done()
    gain = norms_ref[GAIN1 : GAIN1 + 1, :]
    norm_back(upstream, resid[...], gain, low_ref, full_ref, sums_ref)


def norm1_back(own, far, skip, resid, norms):
    dims = own.shape
    return call(
        norm1_back_kernel,
        [("v", shape(dims)), ("v", shape(dims, F32)), ("v", shape((8, dims[1]), F32))],
        [("v", own), ("v", far), ("v", skip), ("h", resid), ("v", norms)],
        scratch=[pltpu.VMEM(dims, F32)],
        us=1.7,
        copies=1,
    )


def ffn_back_kernel(df_ref, slope_ref, up_ref, down_ref, dh_ref, du_ref, db_ref, total_ref):
    units = up_ref.shape[2]
    steps = units // UNITS
    total_ref[...] = jnp.zeros_like(total_ref)

    def step(i):
        half, cols = i // steps, part_of(i % steps, UNITS)
        du = dot_nt(df_ref[...], down_ref[half, cols, :]) * slope_ref[half, :, cols].astype(F32)
        du = du.astype(BF16)
        du_ref[:, part_of(i, UNITS)] = du
        db_ref[pl.ds(half, 1), cols] = jnp.sum(du.astype(F32), axis=0, keepdims=True)
        total_ref[...] += dot_nt(du, up_ref[half, :, cols])

    loop(2 * steps, step)
    dh_ref[...] = total_ref[...].astype(dh_ref.dtype)


def ffn_back(df, slope, up, down, far):
    rows, width = df.shape
    units = 2 * up.shape[2]
    return call(
        ffn_back_kernel,
        [
            ("v", shape((rows, width), BF16 if far else F32)),
            ("v", shape((rows, units))),
            ("v", shape((2, units // 2), F32)),
        ],
        [("v", df), ("v", slope), ("v", up), ("v", down)],
        1.8,
        scratch=[pltpu.VMEM((rows, width), F32)],
    )


def ffn_grads_of(half, h, act, df, du):
    units = act[0].shape[2]
    cols = slice(half * units, (half + 1) * units)
    up = dot_tn(h[0][...], du[0][:, cols]) + dot_tn(h[1][...], du[1][:, cols])
    down = dot_tn(act[0][half], df[0][...]) + dot_tn(act[1][half], df[1][...])
    return up, down


def ffn_pair_kernel(h0, h1, a0, a1, df0, df1, du0, du1, up_ref, down_ref):
    up, down = ffn_grads_of(1, (h0, h1), (a0, a1), (df0, df1), (du0, du1))
    up_ref[...] = up.astype(BF16)
    down_ref[...] = down.astype(BF16)


def ffn_own_kernel(where_ref, h0, h1, a0, a1, df0, df1, du0, du1, up_got, down_got, *outs):
    up, down = ffn_grads_of(0, (h0, h1), (a0, a1), (df0, df1), (du0, du1))
    up += up_got[...].astype(F32)
    down += down_got[...].astype(F32)
    first = where_ref[0] == 0
    half = outs[0].shape[0]
    for part in range(2):
        rows = slice(part * half, (part + 1) * half)
        outs[2 * part][...] = jnp.where(first, down[rows], up[rows]).astype(BF16)
        outs[2 * part + 1][...] = jnp.where(first, up[rows], down[rows])


def ffn_pair(args):
    rows, width = args[0].shape
    units = args[2].shape[2]
    return call(
        ffn_pair_kernel,
        [("v", shape((width, units)))] * 2,
        [("v", item) for item in args],
        1.4,
    )


def ffn_own(where, args, got):
    rows, width = args[0].shape
    units = args[2].shape[2]
    return call(
        ffn_own_kernel,
        [("v", shape((width // 2, units))), ("v", shape((width // 2, units), F32))] * 2,
        [("s", where)] + [("v", item) for item in (*args, *got)],
        2.2,
    )


def attn_back_kernel(
    layer, turned, where_ref, dz_ref, q_ref, kv_ref, marks_ref, lse_ref, w_ref,
    dq_ref, dkv_ref, dkv_pair_ref, bias, do_ref,
):
    rows, width = q_ref.shape
    fill_bias(bias, turned, marks_ref)
    low = lanes_of(rows) < HEAD_DIM
    scale = HEAD_DIM**-0.5
    do_ref[...] = dot_nt(dz_ref[...], w_ref[0]).astype(BF16)
    lanes = lanes_of(rows)
    tiles = width // PAIR

    def step(tile):
        cols, vcols = part_of(tile, PAIR), part_of(tile + tiles, PAIR)
        q, do = q_ref[:, cols], do_ref[:, cols]
        dq, dk, dv = [], 0.0, 0.0
        for side in range(2):
            head = 2 * tile + side
            block = block_of(where_ref, layer, head, turned)
            part = low if side == 0 else ~low
            q_head = jnp.where(part, q, jnp.zeros_like(q))
            do_head = jnp.where(part, do, jnp.zeros_like(do))
            k = kv_ref[block, :, cols]
            s = dot_nt(q_head, k) * (scale * LOG2E) + bias[block]
            log_total = jnp.sum(jnp.where(lanes == head, lse_ref[...], 0.0), axis=1, keepdims=True)
            p = jnp.exp2(s - log_total)
            dp = dot_nt(do_head, kv_ref[block, :, vcols])
            centre = jnp.sum(p * dp, axis=1, keepdims=True)
            ds = (p * (dp - centre)).astype(BF16)
            dq.append(dot(ds, k))
            dv += dot_tn(p.astype(BF16), do_head)
            dk += dot_tn(ds, q_head)
        dq_ref[:, cols] = (jnp.where(low, dq[0], dq[1]) * scale).astype(BF16)
        dkv_ref[:, cols] = dk[:rows] * scale
        dkv_ref[:, vcols] = dv[:rows]
        dkv_pair_ref[:, cols] = (dk[rows:] * scale).astype(BF16)
        dkv_pair_ref[:, vcols] = dv[rows:].astype(BF16)

    loop(tiles, step)


def attn_back(layer, turned, where, dz, q, kv, marks, lse, w):
    rows, width = q.shape
    return call(
        partial(attn_back_kernel, layer, turned),
        [("v", shape((rows, width))), ("v", shape((rows, 2 * width), F32)), ("v", shape((rows, 2 * width)))],
        [("s", where)] + [("v", item) for item in (dz, q, kv, marks, lse, w)],
        4.4,
        scratch=[pltpu.VMEM((2, rows, 2 * rows), F32), pltpu.VMEM((rows, width), BF16)],
    )


def row_grads_kernel(
    small_ref, dq0_ref, dq1_ref, kv0_ref, kv1_ref, pair0_ref, pair1_ref, w_ref, dx_ref, d0_ref, d1_ref
):
    width = dq0_ref.shape[1]
    turned = small_ref[TURNED : TURNED + 1, :] == 1.0
    near = kv0_ref[...] + pair0_ref[...].astype(F32)
    far = kv1_ref[...] + pair1_ref[...].astype(F32)
    d0_ref[:, :width] = dq0_ref[...]
    d1_ref[:, :width] = dq1_ref[...]
    d0_ref[:, width:] = jnp.where(turned, far, near).astype(BF16)
    d1_ref[:, width:] = jnp.where(turned, near, far).astype(BF16)
    total = None
    for k in range(3):
        part = dot(d1_ref[:, k * width : (k + 1) * width], w_ref[k])
        total = part if total is None else total + part
    dx_ref[...] = total.astype(BF16)


def row_grads(small, dq, kv, pair, w):
    rows, width = dq[0].shape
    return call(
        row_grads_kernel,
        [("v", shape((rows, w.shape[2])))] + [("v", shape((rows, 3 * width)))] * 2,
        [("v", item) for item in (small, *dq, *kv, *pair, w)],
        0.9,
    )


def attn_grads_kernel(
    where_ref, d0_ref, d1_ref, x0_ref, x1_ref, o0_ref, o1_ref, dz0_ref, dz1_ref, w_ref,
    dx_ref, own_ref, pair_ref, db_ref,
):
    width = o0_ref.shape[1]
    first_core = where_ref[1] == 0
    share = width // 2
    db_ref[...] = jnp.zeros_like(db_ref)
    for k in range(4):
        cols = slice(k * width, (k + 1) * width)
        if k < 3:
            left, right = (d0_ref[:, cols], d1_ref[:, cols]), (x0_ref[...], x1_ref[...])
        else:
            left, right = (o0_ref[...], o1_ref[...]), (dz0_ref[...], dz1_ref[...])
        if k in (0, 2):
            sums = jnp.sum(left[0].astype(F32), axis=0, keepdims=True)
            sums += jnp.sum(left[1].astype(F32), axis=0, keepdims=True)
            db_ref[0:1, k // 2 * width : (k // 2 + 1) * width] = sums
        both = dot_tn(left[0], right[0]) + dot_tn(left[1], right[1])
        rows = slice(k * share, (k + 1) * share)
        own_ref[rows] = jnp.where(first_core, both[:share], both[share:])
        pair_ref[rows] = jnp.where(first_core, both[share:], both[:share]).astype(BF16)
    total = None
    for k in range(3):
        part = dot(d0_ref[:, k * width : (k + 1) * width], w_ref[k])
        total = part if total is None else total + part
    dx_ref[...] = total


def attn_grads(where, d, x, o, dz, w):
    rows, width = o[0].shape
    columns = x[0].shape[1]
    return call(
        attn_grads_kernel,
        [
            ("v", shape((rows, columns), F32)),
            ("v", shape((2 * width, columns), F32)),
            ("v", shape((2 * width, columns))),
            ("v", shape((8, 2 * width), F32)),
        ],
        [("s", where)] + [("v", item) for item in (*d, *x, *o, *dz, w)],
        2.7,
    )


def split_kernel(where_ref, own_ref, got_ref, sent_ref, kept_ref):
    half = kept_ref.shape[0]
    first = where_ref[0] == 0
    top = own_ref[:half] + got_ref[:half].astype(F32)
    bottom = own_ref[half:] + got_ref[half:].astype(F32)
    kept_ref[...] = jnp.where(first, top, bottom)
    sent_ref[...] = jnp.where(first, bottom, top).astype(BF16)


def split(where, own, got):
    rows, columns = own.shape
    return call(
        split_kernel,
        [("v", shape((rows // 2, columns))), ("v", shape((rows // 2, columns), F32))],
        [("s", where), ("v", own), ("v", got)],
    )


def add_kernel(where_ref, *refs):
    parts, out_ref = len(refs) // 2, refs[-1]
    rows = refs[0].shape[0]
    for part in range(parts):
        total = refs[part][...] + refs[parts + part][...].astype(F32)
        out_ref[part * rows : (part + 1) * rows] = total.astype(BF16)


def halve_sum_kernel(bit, parts, where_ref, *refs):
    kept, got, (sent_ref, own_ref) = refs[:parts], refs[parts : 2 * parts], refs[2 * parts :]
    mine = (where_ref[3] >> bit) & 1
    if parts == 2:
        for half in range(2):

            @pl.when(mine == half)
            def _():
                own_ref[...] = kept[half][...] + got[half][...].astype(F32)
                sent_ref[...] = (kept[1 - half][...] + got[1 - half][...].astype(F32)).astype(BF16)

        return
    rows = own_ref.shape[0]
    at = pl.ds(pl.multiple_of(mine * rows, 16), rows)
    own_ref[...] = kept[0][at] + got[0][at].astype(F32)
    at = pl.ds(pl.multiple_of((1 - mine) * rows, 16), rows)
    sent_ref[...] = (kept[0][at] + got[0][at].astype(F32)).astype(BF16)


def join_kernel(bit, where_ref, own_ref, got_ref, out_ref):
    rows = own_ref.shape[0]
    mine = (where_ref[3] >> bit) & 1
    out_ref[pl.ds(pl.multiple_of(mine * rows, 16), rows)] = own_ref[...]
    out_ref[pl.ds(pl.multiple_of((1 - mine) * rows, 16), rows)] = got_ref[...]


def last_join_kernel(part, where_ref, own_ref, got_ref, later_ref, out_ref, sent_ref):
    join_kernel(0, where_ref, own_ref, got_ref, out_ref)
    rows = out_ref.shape[0]
    later = later_ref[part * rows : (part + 1) * rows]
    sent_ref[...] = jnp.where(where_ref[0] == 0, later, out_ref[...])


def results_kernel(kind, where_ref, *refs):
    *pieces, first_ref, second_ref, buffer, sems = refs
    copies = Copies(sems)
    first = where_ref[0] == 0
    rows = buffer.shape[1]
    half = rows // 2
    count = len(pieces) // 2
    size = rows // count

    def piece(refs, part):
        at = part * half
        return refs[at // size][at % size : at % size + half]

    for side in range(2):
        for part in range(2):
            at = slice(part * half, (part + 1) * half)
            ours, got = piece(pieces[:count], part), piece(pieces[count : 2 * count], part)
            values = jnp.where(first, ours, got) if side == 0 else jnp.where(first, got, pieces[-1][at])
            buffer[side, at] = values.astype(F32)
            if kind == "ffn":
                target = (first_ref, second_ref)[side].at[pl.ds(part * half, half)]
            else:
                k = 2 * side + part
                target = first_ref.at[k] if k < 3 else second_ref
            copies.start(buffer.at[side, pl.ds(part * half, half)], target)
    copies.done()


def results(kind, where, pieces):
    rows, columns = pieces[-1].shape
    if kind == "attn":
        outs = [shape((3, rows // 2, columns), F32), shape((rows // 2, columns), F32)]
    else:
        outs = [shape((rows, columns), F32)] * 2
    return call(
        partial(results_kernel, kind),
        [("h", item) for item in outs],
        [("s", where)] + [("v", item) for item in pieces],
        us=2.5,
        scratch=[pltpu.VMEM((2, rows, columns), F32)],
        copies=4,
    )


def pick_kernel(where_ref, first_in, second_in, out_ref, sems):
    copies = Copies(sems)
    first = where_ref[0] == 0
    copies.start_one([(first, second_in), (jnp.logical_not(first), first_in)], out_ref)
    copies.done()


def place_kernel(where_ref, first_in, second_in, got_ref, out_ref, buffer, sems):
    section = where_ref[0]
    copies = Copies(sems)
    copies.start_one([(section == 0, first_in), (section == 1, second_in)], buffer.at[section])
    buffer[1 - section] = got_ref[...]
    copies.done()
    out = Copies([sems.at[1]])
    out.start(buffer, out_ref.at[0])
    out.done()


def grad_in_kernel(where_ref, own_ref, far_ref, skip_ref, later_in, sent_ref, out_copy, later, out, sems):
    copies = Copies(sems)
    copies.start(later_in, later)
    grad = (own_ref[...] + far_ref[...].astype(F32) + skip_ref[...]).astype(BF16)
    out[...] = grad
    copies.start(out, out_copy)
    copies.done()
    sent_ref[...] = jnp.where(where_ref[0] == 0, later[...], grad)


def pack_sums_kernel(where_ref, *refs):
    own_ref, pair_ref = refs[-2:]
    for layer in range(2):
        norm1_ref, norm2_ref, up0_ref, up1_ref, qkv_ref = refs[5 * layer : 5 * layer + 5]
        at = 8 * layer
        for row, source in (
            (GAIN1, norm1_ref[0:1]),
            (GAIN2, norm2_ref[0:1]),
            (BIAS_OUT, norm1_ref[2:3]),
            (SHIFT1, norm1_ref[1:2]),
            (BIAS2, norm2_ref[2:3]),
            (SHIFT2, norm2_ref[1:2]),
            (7, qkv_ref[0:1]),
        ):
            own_ref[at + row : at + row + 1] = source
            pair_ref[at + row : at + row + 1] = source
        own_ref[at + 6 : at + 7] = up0_ref[0:1] + up1_ref[0:1]
        pair_ref[at + 6 : at + 7] = up0_ref[1:2] + up1_ref[1:2]


def small_add_kernel(where_ref, own_ref, got_ref, total_ref, shared_ref):
    total = own_ref[...] + got_ref[...]
    total_ref[...] = total
    row = lax.broadcasted_iota(jnp.int32, total.shape, 0)
    shared_ref[...] = jnp.where(row % 8 < BIAS_UP, total, 0.0)


def small_results_kernel(where_ref, own_ref, got_ref, *refs):
    outs, (gains, shifts, up, qkv_b), sems = refs[:4], refs[4:8], refs[8]
    total = own_ref[...] + got_ref[...]
    total = jnp.where(where_ref[0] == 0, total[:8], total[8:])
    gains[0] = total[0:2]
    shifts[0] = total[2:6]
    up[...] = total[6:7]
    local = qkv_b.shape[2]
    for k in range(2):
        both = total[7:8, 2 * k * local : 2 * (k + 1) * local]
        qkv_b[0, k : k + 1] = jnp.where(where_ref[1] == 0, both[:, :local], both[:, local:])
    copies = Copies(sems)
    for source, target in zip((gains, shifts, up, qkv_b), outs):
        copies.start(source, target)
    copies.done()


def swap(value, axis, bit):
    count = lax.axis_size(axis)
    return lax.ppermute(value, axis, [(source, source ^ bit) for source in range(count)])


def core_swap(value):
    return swap(value, "tensor", 1)


def chip_swap(value):
    return swap(value, "tensor", 2)


def tie(value, *after):
    return lax.optimization_barrier((value, *after))[0]


class Sum:
    def __init__(self, *pieces):
        self.sent, self.later = None, None
        self.kept = [kept for _, kept in pieces]
        self.got = [swap(sent, "pipe", 1) for sent, _ in pieces]
        count = lax.axis_size("dp")
        self.bits = count.bit_length() - 1
        self.halving = count == 1 << self.bits and self.kept[0].shape[0] % (16 * count) == 0

    def add(self, where):
        rows, columns = self.kept[0].shape
        (self.total,) = call(
            add_kernel,
            [("v", shape((rows * len(self.kept), columns)))],
            [("s", where)] + [("v", item) for item in (*self.kept, *self.got)],
        )
        return self.total

    def whole(self, where, *after):
        total = self.add(where)
        self.total = lax.psum(tie(total, *after), "dp")
        return total

    def halve(self, bit, where):
        parts = len(self.kept)
        rows, columns = self.kept[0].shape
        dims = (rows * parts // 2, columns)
        sent, kept = call(
            partial(halve_sum_kernel, bit, parts),
            [("v", shape(dims)), ("v", shape(dims, F32))],
            [("s", where)] + [("v", item) for item in (*self.kept, *self.got)],
        )
        self.kept, self.got = [kept], [swap(sent, "dp", 1 << bit)]
        return sent

    def join(self, bit, where):
        rows, columns = self.total.shape
        got = swap(self.total, "dp", 1 << bit)
        if bit or self.later is None:
            (self.total,) = call(
                partial(join_kernel, bit),
                [("v", shape((2 * rows, columns)))],
                [("s", where), ("v", self.total), ("v", got)],
            )
            return self.total
        later, part = self.later
        self.total, self.sent = call(
            partial(last_join_kernel, part),
            [("v", shape((2 * rows, columns)))] * 2,
            [("s", where), ("v", self.total), ("v", got), ("v", later.total)],
        )
        return self.total

    def steps(self):
        if not self.halving:
            return [self.whole]
        bits = range(self.bits)
        return (
            [partial(self.halve, bit) for bit in bits]
            + [self.add]
            + [partial(self.join, bit) for bit in reversed(bits)]
        )

    def finish(self):
        if self.sent is None:
            later, part = self.later
            rows = self.total.shape[0]
            piece = later.total[part * rows : (part + 1) * rows]
            self.sent = jnp.where(lax.axis_index("pipe") == 0, piece, self.total)
        self.other = swap(self.sent, "pipe", 1)


def layer_forward(layer, own_in, far_in, w_qkv, small, marks, where, hooks, upstream=None):
    own_q, own_kv, own_x_kept, own_q_kept = qkv(own_in, w_qkv, small)
    own_pair = core_swap(own_kv)
    far_q, far_kv, far_x_kept, far_q_kept = qkv(far_in, w_qkv, small)
    far_pair = core_swap(far_kv)
    w_out = hooks["out"](far_q)
    far_out, kv, kv_kept, far_o, far_lse = attn(
        layer, where, far_q, (own_kv, own_pair, far_kv, far_pair), marks, w_out
    )
    far_sent = far_out
    far_out = chip_swap(far_out)
    own_out, own_o, own_lse = attn(layer, where, own_q, (kv,), marks, w_out)
    own_h, hidden, resid1, own_h_kept = norm1(own_in, own_out, far_out, small)
    far_h = chip_swap(own_h)
    w_up, w_down = hooks["ffn"](far_sent, own_h)
    own_branch, own_act, own_slope = ffn(own_h, w_up, w_down, small, False)
    far_h = tie(far_h, own_branch)
    far_branch, far_act, far_slope, far_h_kept = ffn(far_h, w_up, w_down, small, True)
    own_branch = tie(own_branch, *hooks["next"](far_branch))
    branch = (hidden, own_branch, chip_swap(far_branch))
    turned = None
    if upstream is None:
        output, resid2, output_kept = norm2(*branch, small)
    else:
        *turned, output_kept = turn(*branch, upstream, small)
        output, resid2 = None, None
    kept = dict(
        x=(own_x_kept, far_x_kept),
        q=(own_q_kept, far_q_kept),
        kv=kv_kept,
        lse=(own_lse, far_lse),
        o=(own_o, far_o),
        resid=(resid1, resid2),
        turned=turned,
        weights=(w_qkv, w_out, w_up, w_down),
        h=(own_h_kept, far_h_kept),
        act=(own_act, far_act),
        slope=(own_slope, far_slope),
    )
    return output, output_kept, kept


def layer_backward(layer, upstream, kept, small, marks, where, hooks):
    if kept["turned"] is None:
        own_df, skip2, norm2_sums, *grad_in = norm2_back(upstream, kept["resid"][1], small)
    else:
        (own_df, skip2, norm2_sums), grad_in = kept["turned"], []
    far_df = chip_swap(own_df)
    w_qkv, w_out, w_up, w_down = kept["weights"]
    own_slope, far_slope = load(layer, tie(where, own_df), [], kept["slope"])
    own_dh, own_du, own_db = ffn_back(own_df, own_slope, w_up, w_down, False)
    far_df = tie(far_df, own_dh, *hooks["df"](own_dh))
    far_dh, far_du, far_db = ffn_back(far_df, far_slope, w_up, w_down, True)
    names = ("act", "h", "q", "lse", "x", "o")
    kv, *rows = load(
        layer,
        tie(where, far_dh, *hooks["dh"](far_dh)),
        [],
        [kept["kv"]] + [item for name in names for item in kept[name]],
    )
    own_act, far_act, own_h, far_h, own_q, far_q, own_lse, far_lse, own_x, far_x, own_o, far_o = rows
    grads = (own_h, far_h, own_act, far_act, own_df, far_df, own_du, far_du)
    pair = ffn_pair(grads)
    got = [core_swap(item) for item in pair]
    own_dh = tie(own_dh, pair[0], *hooks["norm"](pair[0]))
    own_dz, skip1, norm1_sums = norm1_back(own_dh, chip_swap(far_dh), skip2, kept["resid"][0], small)
    far_dz = chip_swap(own_dz)
    parts = ffn_own(tie(where, own_dz), grads, got)
    own_dq, own_dkv, own_send = attn_back(
        layer, 0, tie(where, parts[0]), own_dz, own_q, kv, marks, own_lse, w_out
    )
    own_pair = core_swap(own_send)
    far_dz = tie(far_dz, own_send, *hooks["dz"](own_send, parts))
    far_dq, far_dkv, far_send = attn_back(layer, 1, where, far_dz, far_q, kv, marks, far_lse, w_out)
    far_pair = core_swap(tie(far_send, *hooks["send"](far_send)))
    far_dx, own_d, far_d = row_grads(
        small, (own_dq, far_dq), (own_dkv, far_dkv), (own_pair, far_pair), w_qkv
    )
    own_dx, attn_own, attn_pair, qkv_sums = attn_grads(
        tie(where, far_dx, *hooks["dx"](far_dx)),
        (own_d, far_d),
        (own_x, far_x),
        (own_o, far_o),
        (own_dz, far_dz),
        w_qkv,
    )
    far_dx = chip_swap(far_dx)
    sums = (norm1_sums, norm2_sums, own_db, far_db, qkv_sums)
    return (own_dx, far_dx, skip1), grad_in, sums, (attn_own, core_swap(attn_pair))


def body(
    tokens,
    segment_ids,
    pad_mask,
    block_perm,
    qkv_weight,
    qkv_bias,
    out_weight,
    up_weight,
    up_bias,
    down_weight,
    norm_gain,
    shift_bias,
    cotangent,
):
    section = lax.axis_index("pipe")
    place = lax.axis_index("tensor")
    replica = lax.axis_index("dp")
    paired = lax.axis_size("dp") % 2 == 0
    width = tokens.shape[2]
    local = qkv_bias.shape[2]
    here = jnp.stack([section, place % 2, replica % 2, replica, place]).astype(jnp.int32)
    qkv_rows = jnp.transpose(qkv_weight[0], (0, 2, 1))

    def other_half(half, whole):
        if paired:
            return swap(half, "dp", 1)
        even = replica % 2 == 0
        rest = jnp.where(even, whole[..., width // 2 :], whole[..., : width // 2])
        return swap(rest, "pipe", 1)

    (qkv_half,) = halves_of(here, qkv_rows)
    qkv_x = swap(qkv_half, "pipe", 1)
    rows = lax.optimization_barrier(lax.dynamic_index_in_dim(tokens, section, 0, keepdims=False))
    far_rows = chip_swap(rows)
    (own_small,) = call(
        pack_kernel,
        [("v", shape((16, width), F32))],
        [("h", norm_gain), ("h", shift_bias), ("h", up_bias), ("h", qkv_bias), ("s", block_perm)],
        scratch=[
            pltpu.VMEM(item.shape, item.dtype) for item in (norm_gain, shift_bias, up_bias, qkv_bias)
        ],
        copies=4,
    )
    other_small = swap(own_small, "pipe", 1)
    up_half, down_half = halves_of(tie(here, own_small, qkv_half), up_weight, down_weight)
    up_x = swap(up_half, "pipe", 1)
    out_x = swap(tie(out_weight, qkv_x), "pipe", 1)
    (marks,) = call(
        marks_kernel,
        [("v", shape((8, segment_ids.shape[1] // 2), jnp.int32))],
        [("s", tie(here, up_x)), ("v", segment_ids), ("v", pad_mask)],
    )
    *smalls, flags = call(
        params_kernel,
        [("v", shape((16, width), F32))] * 2 + [("h", shape((8, PAIR), F32))],
        [("s", here)]
        + [
            ("v", item)
            for item in (own_small, other_small, core_swap(own_small), core_swap(other_small))
        ],
        scratch=[pltpu.VMEM((8, PAIR), F32)],
        copies=1,
    )
    heads = 2 * block_perm.shape[1]
    where = jnp.concatenate([here, flags[:2, :heads].reshape(-1).astype(jnp.int32)])
    def item(by_core, own, other, after=(), later=()):
        pair_own = core_swap(tie(own, *after) if after else own)
        pair_other = tuple(core_swap(tie(part, *later) if later else part) for part in other)
        return by_core, own, other, pair_own, pair_other

    other_qkv = other_half(tie(qkv_x, up_half, other_small, far_rows), qkv_rows)
    items = dict(qkv=item(True, qkv_rows, (qkv_x, other_qkv)))
    (first_qkv,) = load(0, tie(where, marks, *smalls, far_rows, up_x), [items["qkv"]])

    def first_out(after):
        fetched["down"] = swap(tie(down_half, up_x), "pipe", 1)
        fetched["up"] = other_half(tie(up_x, marks), up_weight)
        items["out"] = item(True, out_weight, (out_x,), (first_qkv,), (first_qkv,))
        return load(0, tie(where, after), [items["out"]])[0]

    fetched = {}

    def first_ffn(early, after):
        down_x = fetched["down"]
        other_down = other_half(tie(down_x, early), down_weight)
        items["up"] = item(False, up_weight, (up_x, fetched["up"]), (early,), (early,))
        items["down"] = item(False, down_weight, (down_x, other_down), (early,), (after,))
        return load_ffn(0, (), tie(where, after))

    def load_ffn(layer, arrays, after):
        return load(layer, after, [items["up"], items["down"]], arrays)

    second = []

    def load_second(after):
        second.extend(load(1, tie(where, after), [items["qkv"], items["out"]]))
        return second

    out_first, first_kept, kept_first = layer_forward(
        0,
        rows,
        far_rows,
        first_qkv,
        smalls[0],
        marks,
        where,
        {"out": first_out, "ffn": first_ffn, "next": load_second},
    )
    def second_ffn(early, after):
        return load_ffn(1, (), tie(where, after))

    upstream = lax.dynamic_index_in_dim(cotangent, section, 0, keepdims=False)
    _, second_kept, kept_second = layer_forward(
        1,
        out_first,
        chip_swap(out_first),
        second[0],
        smalls[1],
        marks,
        where,
        {
            "out": lambda after: second[1],
            "ffn": second_ffn,
            "next": lambda after: (),
        },
        upstream,
    )

    def place_outputs(first, second, got, after):
        return call(
            place_kernel,
            [("h", shape((1, 2) + first.shape))],
            [("s", after), ("h", first), ("h", second), ("v", got)],
            us=1.5,
            scratch=[pltpu.VMEM((2,) + first.shape, BF16)],
            copies=2,
        )[0]

    sums, steps = {}, {}

    def begin(name, *pieces):
        sums[name] = Sum(*pieces)
        steps[name] = sums[name].steps()

    def run(after, *names):
        for name in names:
            if steps[name]:
                after = steps[name].pop(0)(tie(where, after))
        return after

    outputs = []

    def nothing(*_):
        return ()

    def later_df(after):
        (picked,) = call(
            pick_kernel,
            [("v", shape(rows.shape))],
            [("s", tie(where, after)), ("h", first_kept), ("h", second_kept)],
            copies=1,
        )
        outputs.append(swap(picked, "pipe", 1))
        return (picked,)

    def later_dz(after, parts):
        begin("ab1", parts[0:2], parts[2:4])
        return outputs

    grads, _, small_second, attn_second = layer_backward(
        1,
        None,
        kept_second,
        smalls[1],
        marks,
        where,
        {
            "df": later_df,
            "dh": nothing,
            "norm": nothing,
            "dz": later_dz,
            "send": lambda after: sums["ab1"].got[:1],
            "dx": nothing,
        },
    )

    def first_df(after):
        sent, kept = split(tie(where, after), *attn_second)
        begin("c1", (sent, kept))
        return (run(sent, "ab1"),)

    def first_dz(after, parts):
        begin("a0", parts[0:2])
        begin("b0", parts[2:4])
        return (run(after, "ab1", "c1"),)

    def first_send(after):
        return (run(after, "ab1", "c1", "a0"),)

    def first_dx(after):
        return (run(after, "c1", "a0", "b0"),)

    grads, (grad_second,), small_first, attn_first = layer_backward(
        0,
        grads,
        kept_first,
        smalls[0],
        marks,
        where,
        {
            "df": first_df,
            "dh": nothing,
            "norm": lambda after: (run(after, "ab1"),),
            "dz": first_dz,
            "send": first_send,
            "dx": nothing,
        },
    )
    last = [attn_first[0]]

    def now():
        return tie(where, *last)

    def then(*values):
        last[:] = values

    def step(*names):
        then(run(last[-1], *names))

    def small_add(total, got):
        total, shared = call(
            small_add_kernel,
            [("v", shape((16, width), F32))] * 2,
            [("s", now()), ("v", total), ("v", got)],
        )
        then(total)
        return total, shared

    hops = [("pipe", 1)]
    count = lax.axis_size("dp")
    if not count & (count - 1):
        hops += [("dp", 1 << bit) for bit in range(count.bit_length() - 1)]
    total, pair_sums = call(
        pack_sums_kernel,
        [("v", shape((16, width), F32))] * 2,
        [("s", now())] + [("v", value) for value in (*small_first, *small_second)],
    )
    then(total)
    got = core_swap(pair_sums)
    sent, kept = split(now(), *attn_first)
    then(sent)
    begin("c0", (sent, kept))
    step("c1", "a0", "b0", "c0")
    total, shared = small_add(total, got)
    got = chip_swap(shared)
    step("a0", "b0", "c1", "ab1")
    total, _ = small_add(total, got)
    if len(hops) == 1:
        total = lax.psum(total, "dp")
    got = swap(total, *hops[0])
    sent, grad_first = call(
        grad_in_kernel,
        [("v", shape(rows.shape)), ("h", shape(rows.shape))],
        [("s", now())] + [("v", value) for value in grads] + [("h", grad_second)],
        scratch=[pltpu.VMEM(rows.shape, BF16)] * 2,
        copies=2,
    )
    then(sent)
    grad_got = swap(sent, "pipe", 1)
    step("a0", "c0", "b0")
    while steps["c1"]:
        step("c1")
    then(last[-1], grad_got)

    def last_of(*names):
        for name in names:
            while steps[name]:
                step(name)

    def finish(name, later, part):
        sums[name].later = (sums[later], part)
        last_of(name)
        sums[name].finish()

    for at, hop in enumerate(hops[1:]):
        total, _ = small_add(total, got)
        got = swap(total, *hop)
        if at == 0:
            last_of("ab1")
            finish("a0", "ab1", 0)
            step("c0", "b0")
        elif at == 1:
            step("c0")
            finish("b0", "ab1", 1)
    if len(hops) < 2:
        last_of("ab1")
        finish("a0", "ab1", 0)
    if len(hops) < 3:
        finish("b0", "ab1", 1)
    then(last[-1], sums["a0"].other)
    input_grad = place_outputs(grad_first, grad_second, grad_got, now())
    layer_out = place_outputs(first_kept, second_kept, outputs[0], tie(where, input_grad))
    then(layer_out)
    finish("c0", "c1", 0)
    outs = [shape(item.shape, F32) for item in (norm_gain, shift_bias, up_bias, qkv_bias)]
    gains, shifts, upb, qkvb = call(
        small_results_kernel,
        [("h", item) for item in outs],
        [("s", now()), ("v", total), ("v", got)],
        scratch=[pltpu.VMEM(item.shape, F32) for item in outs],
        copies=4,
    )
    then(gains)

    def pieces(later, *names):
        return [
            *(sums[name].total for name in names),
            *(sums[name].other for name in names),
            sums[later].total,
        ]

    upw, downw = results("ffn", now(), pieces("ab1", "a0", "b0"))
    qkvw, outw = results("attn", tie(where, upw), pieces("c1", "c0"))
    qkvw = jnp.transpose(qkvw, (0, 2, 1))
    return (
        layer_out,
        input_grad,
        qkvw[None],
        qkvb,
        outw[None],
        upw[None],
        upb,
        downw[None],
        gains,
        shifts,
    )


def solution(mesh):
    return jax.shard_map(
        body,
        mesh=mesh,
        in_specs=(
            P("dp", "tensor", None),
            P("dp", None),
            P("dp", None),
            P("pipe", "tensor", None),
            P("pipe", None, None, "tensor"),
            P("pipe", None, "tensor"),
            P("pipe", "tensor", None),
            P("pipe", None, "tensor"),
            P("pipe", "tensor"),
            P("pipe", "tensor", None),
            P("pipe", None, None),
            P("pipe", None, None),
            P("dp", "tensor", None),
        ),
        out_specs=(
            P("pipe", "dp", "tensor", None),
            P("pipe", "dp", "tensor", None),
            P("pipe", None, None, "tensor"),
            P("pipe", None, "tensor"),
            P("pipe", "tensor", None),
            P("pipe", None, "tensor"),
            P("pipe", "tensor"),
            P("pipe", "tensor", None),
            P("pipe", None, None),
            P("pipe", None, None),
        ),
        check_vma=False,
    )
```

```python
from functools import partial

import jax
import jax.numpy as jnp
from jax import lax
from jax.experimental import pallas as pl
from jax.experimental.pallas import tpu as pltpu
from jax.sharding import PartitionSpec as P

BF16 = jnp.bfloat16
F32 = jnp.float32
HEAD_DIM = 64
PAIR = 2 * HEAD_DIM
LOG2E = 1.4426950408889634
MASKED = -1e30
VMEM_LIMIT = 16 * 1024 * 1024
COST = 2e10
NORM_EPSILON_TERM = 1e-06

FLAGS = 5

SPACES = {"v": pltpu.VMEM, "s": pltpu.SMEM, "h": pl.ANY}
PLACES = {"v": pltpu.VMEM, "s": pl.ANY, "h": pltpu.HBM}


def shape(dims, dtype=BF16):
    return jax.ShapeDtypeStruct(dims, dtype)


def call(kernel, outs, args, us=0.1, scratch=(), copies=0):
    flops = int(us * COST)
    scratch = list(scratch)
    if copies:
        scratch.append(pltpu.SemaphoreType.DMA((copies,)))
    return pl.pallas_call(
        kernel,
        name=(kernel.func if isinstance(kernel, partial) else kernel).__name__,
        out_shape=[PLACES[space](item.shape, item.dtype) for space, item in outs],
        in_specs=[pl.BlockSpec(memory_space=SPACES[space]) for space, _ in args],
        out_specs=[pl.BlockSpec(memory_space=SPACES[space]) for space, _ in outs],
        scratch_shapes=scratch,
        compiler_params=pltpu.CompilerParams(vmem_limit_bytes=VMEM_LIMIT),
        cost_estimate=pl.CostEstimate(flops=flops, bytes_accessed=0, transcendentals=0),
    )(*[pltpu.with_memory_space_constraint(item, PLACES[space]) for space, item in args])


class Copies:
    def __init__(self, sems):
        self.sems, self.pending = sems, []

    def sem(self):
        at = len(self.pending)
        return self.sems[at] if isinstance(self.sems, list) else self.sems.at[at]

    def start(self, source, target):
        copy = pltpu.make_async_copy(source, target, self.sem())
        copy.start()
        self.pending.append(copy)

    def start_one(self, cases, target):
        sem = self.sem()
        made = []
        for condition, source in cases:
            made.append(pltpu.make_async_copy(source, target, sem))
            pl.when(condition)(made[-1].start)
        self.pending.append(made[0])

    def done(self):
        for copy in self.pending:
            copy.wait()


def loop(count, step):
    lax.fori_loop(0, count, lambda i, _: step(i), None)


def part_of(i, size):
    return pl.ds(pl.multiple_of(i * size, size), size)


def dot(left, right):
    return jnp.dot(left, right, preferred_element_type=F32)


def dot_tn(left, right):
    return lax.dot_general(left, right, (((0,), (0,)), ((), ())), preferred_element_type=F32)


def dot_nt(left, right):
    return lax.dot_general(left, right, (((1,), (1,)), ((), ())), preferred_element_type=F32)


def pack_kernel(gains_in, shifts_in, up_in, qkv_in, perm_ref, out_ref, gains, shifts, up, qkv_b, sems):
    copies = Copies(sems)
    for source, target in ((gains_in, gains), (shifts_in, shifts), (up_in, up), (qkv_in, qkv_b)):
        copies.start(source, target)
    out_ref[...] = jnp.zeros_like(out_ref)
    lane = lax.broadcasted_iota(jnp.int32, (1, out_ref.shape[1]), 1)
    flags = jnp.zeros((1, out_ref.shape[1]), F32)
    for head in range(perm_ref.shape[1]):
        flags = jnp.where(lane == head, perm_ref[0, head, 0].astype(F32), flags)
    out_ref[9:10] = flags
    copies.done()
    out_ref[0:2] = gains[0]
    out_ref[2:6] = shifts[0]
    out_ref[6:7] = up[...].astype(F32)
    out_ref[7:9, 0 : qkv_b.shape[2]] = qkv_b[0].astype(F32)


GAIN1, GAIN2, BIAS_OUT, SHIFT1, BIAS2, SHIFT2, BIAS_UP, BIAS_Q, TURNED = 0, 1, 2, 3, 4, 5, 6, 8, 10


def params_kernel(where_ref, own_ref, other_ref, pair_ref, other_pair_ref, first_out, second_out, flags_copy, flags, sems):
    section, core = where_ref[0], where_ref[1]
    width = own_ref.shape[1]
    local = width // 4
    heads = local // HEAD_DIM
    lane = lax.broadcasted_iota(jnp.int32, (1, width), 1)
    flags[...] = jnp.zeros_like(flags)
    for layer, out_ref in enumerate((first_out, second_out)):
        here = section == layer
        mine = jnp.where(here, own_ref[...], other_ref[...])
        pair = jnp.where(here, pair_ref[...], other_pair_ref[...])
        first = jnp.where(core == 0, mine, pair)
        second = jnp.where(core == 0, pair, mine)
        out_ref[...] = mine
        out_ref[BIAS_UP + 1 : BIAS_UP + 2] = pair[BIAS_UP : BIAS_UP + 1]
        biases = jnp.where(lane < local, first, pltpu.roll(second, local, 1))
        out_ref[BIAS_Q : BIAS_Q + 2] = biases[7:9]
        turned = jnp.where(lane < heads, first, pltpu.roll(second, heads, 1))[9:10]
        lanes = jnp.zeros((1, width), F32)
        for head in range(2 * heads):
            chosen = (lane // HEAD_DIM) % (2 * heads) == head
            lanes = jnp.where(chosen, turned[:, head : head + 1], lanes)
        out_ref[TURNED : TURNED + 1] = lanes
        flags[layer : layer + 1] = turned[:, 0:PAIR]
    copies = Copies(sems)
    copies.start(flags, flags_copy)
    copies.done()


def marks_kernel(where_ref, segments_ref, real_ref, out_ref):
    quarter = out_ref.shape[1] // 2
    out_ref[...] = jnp.zeros_like(out_ref)
    for r in range(4):
        cols = pl.ds(pl.multiple_of((where_ref[4] ^ r) * quarter, PAIR), quarter)
        at = slice((r % 2) * quarter, (r % 2 + 1) * quarter)
        segment = jnp.where(where_ref[0] == 0, segments_ref[0:1, cols], segments_ref[1:2, cols])
        real = jnp.where(where_ref[0] == 0, real_ref[0:1, cols], real_ref[1:2, cols])
        out_ref[1 + r // 2 : 2 + r // 2, at] = jnp.where(real == 1, segment, -1)
        if r % 2 == 0:
            out_ref[0:1, (r // 2) * quarter : (r // 2 + 1) * quarter] = segment


def halve_kernel(where_ref, *refs):
    count = len(refs) // 2
    copies = Copies(refs[-1])
    for source, half in zip(refs[:count], refs[count:-1]):
        columns = half.shape[2]
        copies.start_one(
            [
                (where_ref[2] == side, source.at[:, :, pl.ds(side * columns, columns)])
                for side in range(2)
            ],
            half,
        )
    copies.done()


def halves_of(where, *wholes):
    return call(
        halve_kernel,
        [("v", shape(whole.shape[:2] + (whole.shape[2] // 2,))) for whole in wholes],
        [("s", where)] + [("h", whole) for whole in wholes],
        copies=len(wholes),
    )


def weight_copies(copies, where_ref, layer, k, own, other, target):
    here = where_ref[0] == layer
    if len(other) == 1:
        copies.start_one(
            [(here, own.at[k]), (jnp.logical_not(here), other[0].at[k])], target(slice(None))
        )
        return
    columns = other[0].shape[-1]
    for side in range(2):
        cols = pl.ds(side * columns, columns)
        direct = where_ref[2] == side
        copies.start_one(
            [
                (here, own.at[k, :, cols]),
                (jnp.logical_not(here) & direct, other[0].at[k]),
                (jnp.logical_not(here) & jnp.logical_not(direct), other[1].at[k]),
            ],
            target(cols),
        )


def load_kernel(layer, items, plain, where_ref, *refs):
    sems = refs[-1]
    copies = Copies(sems)
    count = sum(2 * (1 + parts) for _, parts in items)
    sources, plain_in, outs = refs[:count], refs[count : count + plain], refs[count + plain : -1]
    for (by_core, parts), out_ref in zip(items, outs):
        for pair in range(2):
            own, *other = sources[: 1 + parts]
            sources = sources[1 + parts :]
            if by_core:
                rows = out_ref.shape[1] // 2
                slot = (where_ref[1] + pair) % 2
                at = pl.ds(pl.multiple_of(slot * rows, rows), rows)
                for k in range(out_ref.shape[0]):
                    weight_copies(
                        copies, where_ref, layer, k, own, other, lambda cols, k=k: out_ref.at[k, at, cols]
                    )
            else:
                weight_copies(
                    copies, where_ref, layer, 0, own, other, lambda cols: out_ref.at[pair, :, cols]
                )
    for source, target in zip(plain_in, outs[len(items) :]):
        copies.start(source, target)
    copies.done()


def load(layer, where, items, arrays=()):
    outs, sources, kinds, count = [], [], [], len(arrays)
    for by_core, own, other, pair_own, pair_other in items:
        k, rows, columns = own.shape
        outs.append(shape((k, 2 * rows, columns)) if by_core else shape((2, rows, columns)))
        sources += [own, *other, pair_own, *pair_other]
        kinds.append((by_core, len(other)))
        count += 2 * k * len(other)
    outs += [shape(item.shape, item.dtype) for item in arrays]
    return call(
        partial(load_kernel, layer, kinds, len(arrays)),
        [("v", item) for item in outs],
        [("s", where)] + [("h", item) for item in (*sources, *arrays)],
        us=2.4,
        copies=count,
    )


def qkv_kernel(x_ref, w_ref, b_ref, q_ref, kv_ref, x_copy, q_copy, sems):
    copies = Copies(sems)
    copies.start(x_ref, x_copy)
    x = x_ref[...]
    width = q_ref.shape[1]
    q_ref[...] = (dot_nt(x, w_ref[0]) + b_ref[BIAS_Q : BIAS_Q + 1, :width]).astype(BF16)
    copies.start(q_ref, q_copy)
    kv_ref[:, :width] = dot_nt(x, w_ref[1]).astype(BF16)
    kv_ref[:, width:] = (dot_nt(x, w_ref[2]) + b_ref[BIAS_Q + 1 : BIAS_Q + 2, :width]).astype(BF16)
    copies.done()


def qkv(x, w, b):
    rows, width = x.shape[0], w.shape[1]
    return call(
        qkv_kernel,
        [
            ("v", shape((rows, width))),
            ("v", shape((rows, 2 * width))),
            ("h", shape(x.shape)),
            ("h", shape((rows, width))),
        ],
        [("v", x), ("v", w), ("v", b)],
        1.1,
        copies=2,
    )


def lanes_of(rows):
    return lax.broadcasted_iota(jnp.int32, (rows, PAIR), 1)


def fill_bias(bias, side, marks_ref):
    rows = bias.shape[1]
    wanted = jnp.transpose(marks_ref[:, side * rows : (side + 1) * rows])[:, 0:1]
    for j in range(2):
        bias[j] = jnp.where(wanted == marks_ref[1 + j : 2 + j, :], 0.0, MASKED).astype(F32)


def block_of(where_ref, layer, head, turned):
    return where_ref[FLAGS + 6 * layer + head] ^ turned


def attn_rows(layer, where_ref, turned, q_ref, kv_ref, marks_ref, o_ref, lse_ref, bias):
    rows, width = q_ref.shape
    fill_bias(bias, turned, marks_ref)
    lanes = lanes_of(rows)
    low = lanes < HEAD_DIM
    scale = HEAD_DIM**-0.5 * LOG2E
    lse_ref[...] = jnp.zeros_like(lse_ref)

    def step(tile):
        cols, vcols = part_of(tile, PAIR), part_of(tile + width // PAIR, PAIR)
        q = q_ref[:, cols]
        mixed = []
        for side in range(2):
            head = 2 * tile + side
            block = block_of(where_ref, layer, head, turned)
            q_head = jnp.where(low if side == 0 else ~low, q, jnp.zeros_like(q))
            s = dot_nt(q_head, kv_ref[block, :, cols]) * scale + bias[block]
            top = jnp.maximum(jnp.max(s, axis=1, keepdims=True), 0.0)
            e = jnp.exp2(s - top)
            total = jnp.exp2(-top) + jnp.sum(e, axis=1, keepdims=True)
            mixed.append(dot(e.astype(BF16), kv_ref[block, :, vcols]) * (1.0 / total))
            lse_ref[...] = jnp.where(lanes == head, top + jnp.log2(total), lse_ref[...])
        o_ref[:, cols] = jnp.where(low, mixed[0], mixed[1]).astype(BF16)

    loop(width // PAIR, step)


def attn_far_kernel(
    layer, where_ref, q_ref, kv0_ref, kv1_ref, kv2_ref, kv3_ref, marks_ref, w_ref,
    out_ref, kv_ref, kv_copy, o_copy, lse_copy, bias, o_ref, lse_ref, sems,
):
    copies = Copies(sems)
    half = kv0_ref.shape[0]
    for block, pair in enumerate(((kv0_ref, kv1_ref), (kv2_ref, kv3_ref))):
        kv_ref[block, :half] = pair[0][...]
        kv_ref[block, half:] = pair[1][...]
    copies.start(kv_ref, kv_copy)
    attn_rows(layer, where_ref, 1, q_ref, kv_ref, marks_ref, o_ref, lse_ref, bias)
    copies.start(o_ref, o_copy)
    copies.start(lse_ref, lse_copy)
    out_ref[...] = dot(o_ref[...], w_ref[0]).astype(out_ref.dtype)
    copies.done()


def attn_own_kernel(
    layer, where_ref, q_ref, kv_ref, marks_ref, w_ref, out_ref, o_copy, lse_copy, bias, o_ref, lse_ref, sems
):
    copies = Copies(sems)
    attn_rows(layer, where_ref, 0, q_ref, kv_ref, marks_ref, o_ref, lse_ref, bias)
    copies.start(o_ref, o_copy)
    copies.start(lse_ref, lse_copy)
    out_ref[...] = dot(o_ref[...], w_ref[0]).astype(out_ref.dtype)
    copies.done()


def attn(layer, where, q, kv, marks, w):
    rows, width = q.shape
    far = len(kv) > 1
    outs = [("v", shape((rows, w.shape[2]), BF16 if far else F32))]
    if far:
        joined = shape((2, 2 * rows, kv[0].shape[1]))
        outs += [("v", joined), ("h", joined)]
    outs += [("h", shape((rows, width))), ("h", shape((rows, PAIR), F32))]
    args = [("s", where)] + [("v", item) for item in (q, *kv, marks, w)]
    return call(
        partial(attn_far_kernel if far else attn_own_kernel, layer),
        outs,
        args,
        4.6,
        scratch=[
            pltpu.VMEM((2, rows, 2 * rows), F32),
            pltpu.VMEM((rows, width), BF16),
            pltpu.VMEM((rows, PAIR), F32),
        ],
        copies=3 if far else 2,
    )


def normed_rows(resid):
    centred = resid - jnp.mean(resid, axis=1, keepdims=True)
    inverse = lax.rsqrt(jnp.mean(centred * centred, axis=1, keepdims=True) + NORM_EPSILON_TERM)
    return centred * inverse, inverse


def norm1_kernel(x_ref, own_ref, far_ref, norms_ref, low_ref, full_ref, resid_copy, low_copy, resid, sems):
    copies = Copies(sems)
    projected = own_ref[...] + far_ref[...].astype(F32)
    total = x_ref[...].astype(F32) + projected + norms_ref[BIAS_OUT : BIAS_OUT + 1, :]
    resid[...] = total
    copies.start(resid, resid_copy)
    hidden = normed_rows(total)[0] * norms_ref[GAIN1 : GAIN1 + 1, :] + norms_ref[SHIFT1 : SHIFT1 + 1, :]
    full_ref[...] = hidden
    low_ref[...] = hidden.astype(BF16)
    copies.start(low_ref, low_copy)
    copies.done()


def norm1(x, own, far, norms):
    return call(
        norm1_kernel,
        [("v", shape(x.shape)), ("v", shape(x.shape, F32)), ("h", shape(x.shape, F32)), ("h", shape(x.shape))],
        [("v", x), ("v", own), ("v", far), ("v", norms)],
        scratch=[pltpu.VMEM(x.shape, F32)],
        us=1.2,
        copies=2,
    )


def norm2_kernel(h_ref, own_ref, far_ref, norms_ref, low_ref, resid_copy, low_copy, resid, sems):
    copies = Copies(sems)
    branch = own_ref[...] + far_ref[...].astype(F32)
    total = h_ref[...] + branch + norms_ref[BIAS2 : BIAS2 + 1, :]
    resid[...] = total
    copies.start(resid, resid_copy)
    out = normed_rows(total)[0] * norms_ref[GAIN2 : GAIN2 + 1, :] + norms_ref[SHIFT2 : SHIFT2 + 1, :]
    low_ref[...] = out.astype(BF16)
    copies.start(low_ref, low_copy)
    copies.done()


def norm2(h, own, far, norms):
    return call(
        norm2_kernel,
        [("v", shape(h.shape)), ("h", shape(h.shape, F32)), ("h", shape(h.shape))],
        [("v", h), ("v", own), ("v", far), ("v", norms)],
        scratch=[pltpu.VMEM(h.shape, F32)],
        us=1.2,
        copies=2,
    )


TAIL = tuple(
    0.5 * c
    for c in (
        0.05029408002973294, -0.1830316054165625, 0.16930258232763196, -0.005798692821681883,
        0.14152663657068731, 0.16851528425000623, 0.20784663429852349, 0.22566934002005623,
        0.22567586682378352,
    )
)


def gelu_and_slope(u):
    bell = jnp.exp2(u * u * (-0.5 * LOG2E))
    t = 1.0 / (1.0 + jnp.abs(u) * (0.4 * 0.5**0.5))
    poly = TAIL[0]
    for c in TAIL[1:]:
        poly = poly * t + c
    tail = poly * t * bell
    below = jnp.where(u < 0.0, tail, 1.0 - tail)
    return u * below, below + u * bell * 0.3989422804014327


UNITS = 768


def ffn_kernel(far, h_ref, up_ref, down_ref, b_ref, out_ref, act_copy, slope_copy, *rest):
    act_ref, slope_ref, total_ref, sems = rest[-4:]
    steps = up_ref.shape[2] // UNITS
    if far:
        rows_copy = pltpu.make_async_copy(h_ref, rest[0], sems.at[4 * steps])
        rows_copy.start()
    total_ref[...] = jnp.zeros_like(total_ref)

    def copies_of(i):
        half, cols = i // steps, part_of(i % steps, UNITS)
        return [
            pltpu.make_async_copy(kept.at[half, :, cols], copy.at[half, :, cols], sems.at[2 * i + k])
            for k, (kept, copy) in enumerate(((act_ref, act_copy), (slope_ref, slope_copy)))
        ]

    def step(i):
        half, cols = i // steps, part_of(i % steps, UNITS)
        pre = dot(h_ref[...], up_ref[half, :, cols]) + b_ref[pl.ds(BIAS_UP + half, 1), cols]
        act, slope = gelu_and_slope(pre)
        act = act.astype(BF16)
        act_ref[half, :, cols] = act
        slope_ref[half, :, cols] = slope.astype(BF16)
        for copy in copies_of(i):
            copy.start()
        total_ref[...] += dot(act, down_ref[half, cols, :])

    loop(2 * steps, step)
    out_ref[...] = total_ref[...].astype(out_ref.dtype)

    def finish(i):
        for copy in copies_of(i):
            copy.wait()

    loop(2 * steps, finish)
    if far:
        rows_copy.wait()


def ffn(h, up, down, b, far):
    rows, width = h.shape
    units = up.shape[2]
    outs = [
        ("v", shape((rows, width), BF16 if far else F32)),
        ("h", shape((2, rows, units))),
        ("h", shape((2, rows, units))),
    ]
    if far:
        outs.append(("h", shape(h.shape)))
    return call(
        partial(ffn_kernel, far),
        outs,
        [("v", h), ("v", up), ("v", down), ("v", b)],
        0.1,
        scratch=[pltpu.VMEM((2, rows, units), BF16)] * 2 + [pltpu.VMEM((rows, width), F32)],
        copies=4 * (units // UNITS) + 1,
    )


def norm_back(upstream, resid, gain, low_ref, full_ref, sums_ref):
    normed, inverse = normed_rows(resid)
    scaled = upstream * gain
    inner = (
        scaled
        - jnp.mean(scaled, axis=1, keepdims=True)
        - normed * jnp.mean(scaled * normed, axis=1, keepdims=True)
    )
    grad = inverse * inner
    full_ref[...] = grad
    low_ref[...] = grad.astype(BF16)
    sums_ref[...] = jnp.zeros_like(sums_ref)
    sums_ref[0:1] = jnp.sum(upstream * normed, axis=0, keepdims=True)
    sums_ref[1:2] = jnp.sum(upstream, axis=0, keepdims=True)
    sums_ref[2:3] = jnp.sum(grad, axis=0, keepdims=True)


def norm2_back_kernel(inner, *refs):
    if inner:
        own_ref, far_ref, resid1_ref, resid_in, norms_ref, *refs = refs
        low_ref, full_ref, sums_ref, grad_copy, resid, grad_ref, sems = refs
    else:
        up_ref, resid_in, norms_ref, low_ref, full_ref, sums_ref, resid, sems = refs
    copies = Copies(sems)
    copies.start(resid_in, resid)
    if inner:
        grad_in = (own_ref[...] + far_ref[...].astype(F32) + resid1_ref[...]).astype(BF16)
        grad_ref[...] = grad_in
        copies.start(grad_ref, grad_copy)
    else:
        grad_in = up_ref[...]
    copies.done()
    gain = norms_ref[GAIN2 : GAIN2 + 1, :]
    norm_back(grad_in.astype(F32), resid[...], gain, low_ref, full_ref, sums_ref)


def turn_kernel(h_ref, own_ref, far_ref, up_ref, norms_ref, low_ref, full_ref, sums_ref, out_copy, out, sems):
    branch = own_ref[...] + far_ref[...].astype(F32)
    resid = h_ref[...] + branch + norms_ref[BIAS2 : BIAS2 + 1, :]
    gain = norms_ref[GAIN2 : GAIN2 + 1, :]
    out[...] = (normed_rows(resid)[0] * gain + norms_ref[SHIFT2 : SHIFT2 + 1, :]).astype(BF16)
    copies = Copies(sems)
    copies.start(out, out_copy)
    norm_back(up_ref[...].astype(F32), resid, gain, low_ref, full_ref, sums_ref)
    copies.done()


def turn(h, own, far, upstream, norms):
    dims = h.shape
    return call(
        turn_kernel,
        [
            ("v", shape(dims)),
            ("v", shape(dims, F32)),
            ("v", shape((8, dims[1]), F32)),
            ("h", shape(dims)),
        ],
        [("v", item) for item in (h, own, far, upstream, norms)],
        scratch=[pltpu.VMEM(dims, BF16)],
        us=2.5,
        copies=1,
    )


def norm2_back(upstream, resid, norms):
    dims = upstream[0].shape
    inner = len(upstream) > 1
    outs = [("v", shape(dims)), ("v", shape(dims, F32)), ("v", shape((8, dims[1]), F32))]
    scratch = [pltpu.VMEM(dims, F32)]
    if inner:
        outs.append(("h", shape(dims)))
        scratch.append(pltpu.VMEM(dims, BF16))
    return call(
        partial(norm2_back_kernel, inner),
        outs,
        [("v", item) for item in upstream] + [("h", resid), ("v", norms)],
        scratch=scratch,
        us=1.7,
        copies=2,
    )


def norm1_back_kernel(own_ref, far_ref, skip_ref, resid_in, norms_ref, low_ref, full_ref, sums_ref, resid, sems):
    copies = Copies(sems)
    copies.start(resid_in, resid)
    upstream = own_ref[...] + far_ref[...].astype(F32) + skip_ref[...]
    copies.done()
    gain = norms_ref[GAIN1 : GAIN1 + 1, :]
    norm_back(upstream, resid[...], gain, low_ref, full_ref, sums_ref)


def norm1_back(own, far, skip, resid, norms):
    dims = own.shape
    return call(
        norm1_back_kernel,
        [("v", shape(dims)), ("v", shape(dims, F32)), ("v", shape((8, dims[1]), F32))],
        [("v", own), ("v", far), ("v", skip), ("h", resid), ("v", norms)],
        scratch=[pltpu.VMEM(dims, F32)],
        us=1.7,
        copies=1,
    )


def ffn_back_kernel(df_ref, slope_ref, up_ref, down_ref, dh_ref, du_ref, db_ref, total_ref):
    units = up_ref.shape[2]
    steps = units // UNITS
    total_ref[...] = jnp.zeros_like(total_ref)

    def step(i):
        half, cols = i // steps, part_of(i % steps, UNITS)
        du = dot_nt(df_ref[...], down_ref[half, cols, :]) * slope_ref[half, :, cols].astype(F32)
        du = du.astype(BF16)
        du_ref[:, part_of(i, UNITS)] = du
        db_ref[pl.ds(half, 1), cols] = jnp.sum(du.astype(F32), axis=0, keepdims=True)
        total_ref[...] += dot_nt(du, up_ref[half, :, cols])

    loop(2 * steps, step)
    dh_ref[...] = total_ref[...].astype(dh_ref.dtype)


def ffn_back(df, slope, up, down, far):
    rows, width = df.shape
    units = 2 * up.shape[2]
    return call(
        ffn_back_kernel,
        [
            ("v", shape((rows, width), BF16 if far else F32)),
            ("v", shape((rows, units))),
            ("v", shape((2, units // 2), F32)),
        ],
        [("v", df), ("v", slope), ("v", up), ("v", down)],
        1.8,
        scratch=[pltpu.VMEM((rows, width), F32)],
    )


def ffn_grads_of(half, h, act, df, du):
    units = act[0].shape[2]
    cols = slice(half * units, (half + 1) * units)
    up = dot_tn(h[0][...], du[0][:, cols]) + dot_tn(h[1][...], du[1][:, cols])
    down = dot_tn(act[0][half], df[0][...]) + dot_tn(act[1][half], df[1][...])
    return up, down


def ffn_pair_kernel(h0, h1, a0, a1, df0, df1, du0, du1, up_ref, down_ref):
    up, down = ffn_grads_of(1, (h0, h1), (a0, a1), (df0, df1), (du0, du1))
    up_ref[...] = up.astype(BF16)
    down_ref[...] = down.astype(BF16)


def ffn_own_kernel(where_ref, h0, h1, a0, a1, df0, df1, du0, du1, up_got, down_got, *outs):
    up, down = ffn_grads_of(0, (h0, h1), (a0, a1), (df0, df1), (du0, du1))
    up += up_got[...].astype(F32)
    down += down_got[...].astype(F32)
    first = where_ref[0] == 0
    half = outs[0].shape[0]
    for part in range(2):
        rows = slice(part * half, (part + 1) * half)
        outs[2 * part][...] = jnp.where(first, down[rows], up[rows]).astype(BF16)
        outs[2 * part + 1][...] = jnp.where(first, up[rows], down[rows])


def ffn_pair(args):
    rows, width = args[0].shape
    units = args[2].shape[2]
    return call(
        ffn_pair_kernel,
        [("v", shape((width, units)))] * 2,
        [("v", item) for item in args],
        1.4,
    )


def ffn_own(where, args, got):
    rows, width = args[0].shape
    units = args[2].shape[2]
    return call(
        ffn_own_kernel,
        [("v", shape((width // 2, units))), ("v", shape((width // 2, units), F32))] * 2,
        [("s", where)] + [("v", item) for item in (*args, *got)],
        2.2,
    )


def attn_back_kernel(
    layer, turned, where_ref, dz_ref, q_ref, kv_ref, marks_ref, lse_ref, w_ref,
    dq_ref, dkv_ref, dkv_pair_ref, bias, do_ref,
):
    rows, width = q_ref.shape
    fill_bias(bias, turned, marks_ref)
    low = lanes_of(rows) < HEAD_DIM
    scale = HEAD_DIM**-0.5
    do_ref[...] = dot_nt(dz_ref[...], w_ref[0]).astype(BF16)
    lanes = lanes_of(rows)
    tiles = width // PAIR

    def step(tile):
        cols, vcols = part_of(tile, PAIR), part_of(tile + tiles, PAIR)
        q, do = q_ref[:, cols], do_ref[:, cols]
        dq, dk, dv = [], 0.0, 0.0
        for side in range(2):
            head = 2 * tile + side
            block = block_of(where_ref, layer, head, turned)
            part = low if side == 0 else ~low
            q_head = jnp.where(part, q, jnp.zeros_like(q))
            do_head = jnp.where(part, do, jnp.zeros_like(do))
            k = kv_ref[block, :, cols]
            s = dot_nt(q_head, k) * (scale * LOG2E) + bias[block]
            log_total = jnp.sum(jnp.where(lanes == head, lse_ref[...], 0.0), axis=1, keepdims=True)
            p = jnp.exp2(s - log_total)
            dp = dot_nt(do_head, kv_ref[block, :, vcols])
            centre = jnp.sum(p * dp, axis=1, keepdims=True)
            ds = (p * (dp - centre)).astype(BF16)
            dq.append(dot(ds, k))
            dv += dot_tn(p.astype(BF16), do_head)
            dk += dot_tn(ds, q_head)
        dq_ref[:, cols] = (jnp.where(low, dq[0], dq[1]) * scale).astype(BF16)
        dkv_ref[:, cols] = dk[:rows] * scale
        dkv_ref[:, vcols] = dv[:rows]
        dkv_pair_ref[:, cols] = (dk[rows:] * scale).astype(BF16)
        dkv_pair_ref[:, vcols] = dv[rows:].astype(BF16)

    loop(tiles, step)


def attn_back(layer, turned, where, dz, q, kv, marks, lse, w):
    rows, width = q.shape
    return call(
        partial(attn_back_kernel, layer, turned),
        [("v", shape((rows, width))), ("v", shape((rows, 2 * width), F32)), ("v", shape((rows, 2 * width)))],
        [("s", where)] + [("v", item) for item in (dz, q, kv, marks, lse, w)],
        4.4,
        scratch=[pltpu.VMEM((2, rows, 2 * rows), F32), pltpu.VMEM((rows, width), BF16)],
    )


def row_grads_kernel(
    small_ref, dq0_ref, dq1_ref, kv0_ref, kv1_ref, pair0_ref, pair1_ref, w_ref, dx_ref, d0_ref, d1_ref
):
    width = dq0_ref.shape[1]
    turned = small_ref[TURNED : TURNED + 1, :] == 1.0
    near = kv0_ref[...] + pair0_ref[...].astype(F32)
    far = kv1_ref[...] + pair1_ref[...].astype(F32)
    d0_ref[:, :width] = dq0_ref[...]
    d1_ref[:, :width] = dq1_ref[...]
    d0_ref[:, width:] = jnp.where(turned, far, near).astype(BF16)
    d1_ref[:, width:] = jnp.where(turned, near, far).astype(BF16)
    total = None
    for k in range(3):
        part = dot(d1_ref[:, k * width : (k + 1) * width], w_ref[k])
        total = part if total is None else total + part
    dx_ref[...] = total.astype(BF16)


def row_grads(small, dq, kv, pair, w):
    rows, width = dq[0].shape
    return call(
        row_grads_kernel,
        [("v", shape((rows, w.shape[2])))] + [("v", shape((rows, 3 * width)))] * 2,
        [("v", item) for item in (small, *dq, *kv, *pair, w)],
        0.9,
    )


def attn_grads_kernel(
    where_ref, d0_ref, d1_ref, x0_ref, x1_ref, o0_ref, o1_ref, dz0_ref, dz1_ref, w_ref,
    dx_ref, own_ref, pair_ref, db_ref,
):
    width = o0_ref.shape[1]
    first_core = where_ref[1] == 0
    share = width // 2
    db_ref[...] = jnp.zeros_like(db_ref)
    for k in range(4):
        cols = slice(k * width, (k + 1) * width)
        if k < 3:
            left, right = (d0_ref[:, cols], d1_ref[:, cols]), (x0_ref[...], x1_ref[...])
        else:
            left, right = (o0_ref[...], o1_ref[...]), (dz0_ref[...], dz1_ref[...])
        if k in (0, 2):
            sums = jnp.sum(left[0].astype(F32), axis=0, keepdims=True)
            sums += jnp.sum(left[1].astype(F32), axis=0, keepdims=True)
            db_ref[0:1, k // 2 * width : (k // 2 + 1) * width] = sums
        both = dot_tn(left[0], right[0]) + dot_tn(left[1], right[1])
        rows = slice(k * share, (k + 1) * share)
        own_ref[rows] = jnp.where(first_core, both[:share], both[share:])
        pair_ref[rows] = jnp.where(first_core, both[share:], both[:share]).astype(BF16)
    total = None
    for k in range(3):
        part = dot(d0_ref[:, k * width : (k + 1) * width], w_ref[k])
        total = part if total is None else total + part
    dx_ref[...] = total


def attn_grads(where, d, x, o, dz, w):
    rows, width = o[0].shape
    columns = x[0].shape[1]
    return call(
        attn_grads_kernel,
        [
            ("v", shape((rows, columns), F32)),
            ("v", shape((2 * width, columns), F32)),
            ("v", shape((2 * width, columns))),
            ("v", shape((8, 2 * width), F32)),
        ],
        [("s", where)] + [("v", item) for item in (*d, *x, *o, *dz, w)],
        2.7,
    )


def split_kernel(where_ref, own_ref, got_ref, sent_ref, kept_ref):
    half = kept_ref.shape[0]
    first = where_ref[0] == 0
    top = own_ref[:half] + got_ref[:half].astype(F32)
    bottom = own_ref[half:] + got_ref[half:].astype(F32)
    kept_ref[...] = jnp.where(first, top, bottom)
    sent_ref[...] = jnp.where(first, bottom, top).astype(BF16)


def split(where, own, got):
    rows, columns = own.shape
    return call(
        split_kernel,
        [("v", shape((rows // 2, columns))), ("v", shape((rows // 2, columns), F32))],
        [("s", where), ("v", own), ("v", got)],
    )


def add_kernel(where_ref, *refs):
    parts, out_ref = len(refs) // 2, refs[-1]
    rows = refs[0].shape[0]
    for part in range(parts):
        total = refs[part][...] + refs[parts + part][...].astype(F32)
        out_ref[part * rows : (part + 1) * rows] = total.astype(BF16)


def halve_sum_kernel(bit, parts, where_ref, *refs):
    kept, got, (sent_ref, own_ref) = refs[:parts], refs[parts : 2 * parts], refs[2 * parts :]
    mine = (where_ref[3] >> bit) & 1
    if parts == 2:
        for half in range(2):

            @pl.when(mine == half)
            def _():
                own_ref[...] = kept[half][...] + got[half][...].astype(F32)
                sent_ref[...] = (kept[1 - half][...] + got[1 - half][...].astype(F32)).astype(BF16)

        return
    rows = own_ref.shape[0]
    at = pl.ds(pl.multiple_of(mine * rows, 16), rows)
    own_ref[...] = kept[0][at] + got[0][at].astype(F32)
    at = pl.ds(pl.multiple_of((1 - mine) * rows, 16), rows)
    sent_ref[...] = (kept[0][at] + got[0][at].astype(F32)).astype(BF16)


def join_kernel(bit, where_ref, own_ref, got_ref, out_ref):
    rows = own_ref.shape[0]
    mine = (where_ref[3] >> bit) & 1
    out_ref[pl.ds(pl.multiple_of(mine * rows, 16), rows)] = own_ref[...]
    out_ref[pl.ds(pl.multiple_of((1 - mine) * rows, 16), rows)] = got_ref[...]


def last_join_kernel(part, where_ref, own_ref, got_ref, later_ref, out_ref, sent_ref):
    join_kernel(0, where_ref, own_ref, got_ref, out_ref)
    rows = out_ref.shape[0]
    later = later_ref[part * rows : (part + 1) * rows]
    sent_ref[...] = jnp.where(where_ref[0] == 0, later, out_ref[...])


def results_kernel(kind, where_ref, *refs):
    *pieces, first_ref, second_ref, buffer, sems = refs
    copies = Copies(sems)
    first = where_ref[0] == 0
    rows = buffer.shape[1]
    half = rows // 2
    count = len(pieces) // 2
    size = rows // count

    def piece(refs, part):
        at = part * half
        return refs[at // size][at % size : at % size + half]

    for side in range(2):
        for part in range(2):
            at = slice(part * half, (part + 1) * half)
            ours, got = piece(pieces[:count], part), piece(pieces[count : 2 * count], part)
            values = jnp.where(first, ours, got) if side == 0 else jnp.where(first, got, pieces[-1][at])
            buffer[side, at] = values.astype(F32)
            if kind == "ffn":
                target = (first_ref, second_ref)[side].at[pl.ds(part * half, half)]
            else:
                k = 2 * side + part
                target = first_ref.at[k] if k < 3 else second_ref
            copies.start(buffer.at[side, pl.ds(part * half, half)], target)
    copies.done()


def results(kind, where, pieces):
    rows, columns = pieces[-1].shape
    if kind == "attn":
        outs = [shape((3, rows // 2, columns), F32), shape((rows // 2, columns), F32)]
    else:
        outs = [shape((rows, columns), F32)] * 2
    return call(
        partial(results_kernel, kind),
        [("h", item) for item in outs],
        [("s", where)] + [("v", item) for item in pieces],
        us=2.5,
        scratch=[pltpu.VMEM((2, rows, columns), F32)],
        copies=4,
    )


def pick_kernel(where_ref, first_in, second_in, out_ref, sems):
    copies = Copies(sems)
    first = where_ref[0] == 0
    copies.start_one([(first, second_in), (jnp.logical_not(first), first_in)], out_ref)
    copies.done()


def place_kernel(where_ref, first_in, second_in, got_ref, out_ref, buffer, sems):
    section = where_ref[0]
    copies = Copies(sems)
    copies.start_one([(section == 0, first_in), (section == 1, second_in)], buffer.at[section])
    buffer[1 - section] = got_ref[...]
    copies.done()
    out = Copies([sems.at[1]])
    out.start(buffer, out_ref.at[0])
    out.done()


def grad_in_kernel(where_ref, own_ref, far_ref, skip_ref, later_in, sent_ref, out_copy, later, out, sems):
    copies = Copies(sems)
    copies.start(later_in, later)
    grad = (own_ref[...] + far_ref[...].astype(F32) + skip_ref[...]).astype(BF16)
    out[...] = grad
    copies.start(out, out_copy)
    copies.done()
    sent_ref[...] = jnp.where(where_ref[0] == 0, later[...], grad)


def pack_sums_kernel(where_ref, *refs):
    own_ref, pair_ref = refs[-2:]
    for layer in range(2):
        norm1_ref, norm2_ref, up0_ref, up1_ref, qkv_ref = refs[5 * layer : 5 * layer + 5]
        at = 8 * layer
        for row, source in (
            (GAIN1, norm1_ref[0:1]),
            (GAIN2, norm2_ref[0:1]),
            (BIAS_OUT, norm1_ref[2:3]),
            (SHIFT1, norm1_ref[1:2]),
            (BIAS2, norm2_ref[2:3]),
            (SHIFT2, norm2_ref[1:2]),
            (7, qkv_ref[0:1]),
        ):
            own_ref[at + row : at + row + 1] = source
            pair_ref[at + row : at + row + 1] = source
        own_ref[at + 6 : at + 7] = up0_ref[0:1] + up1_ref[0:1]
        pair_ref[at + 6 : at + 7] = up0_ref[1:2] + up1_ref[1:2]


def small_add_kernel(where_ref, own_ref, got_ref, total_ref, shared_ref):
    total = own_ref[...] + got_ref[...]
    total_ref[...] = total
    row = lax.broadcasted_iota(jnp.int32, total.shape, 0)
    shared_ref[...] = jnp.where(row % 8 < BIAS_UP, total, 0.0)


def small_results_kernel(where_ref, own_ref, got_ref, *refs):
    outs, (gains, shifts, up, qkv_b), sems = refs[:4], refs[4:8], refs[8]
    total = own_ref[...] + got_ref[...]
    total = jnp.where(where_ref[0] == 0, total[:8], total[8:])
    gains[0] = total[0:2]
    shifts[0] = total[2:6]
    up[...] = total[6:7]
    local = qkv_b.shape[2]
    for k in range(2):
        both = total[7:8, 2 * k * local : 2 * (k + 1) * local]
        qkv_b[0, k : k + 1] = jnp.where(where_ref[1] == 0, both[:, :local], both[:, local:])
    copies = Copies(sems)
    for source, target in zip((gains, shifts, up, qkv_b), outs):
        copies.start(source, target)
    copies.done()


def swap(value, axis, bit):
    count = lax.axis_size(axis)
    return lax.ppermute(value, axis, [(source, source ^ bit) for source in range(count)])


def core_swap(value):
    return swap(value, "tensor", 1)


def chip_swap(value):
    return swap(value, "tensor", 2)


def tie(value, *after):
    return lax.optimization_barrier((value, *after))[0]


class Sum:
    def __init__(self, *pieces):
        self.sent, self.later = None, None
        self.kept = [kept for _, kept in pieces]
        self.got = [swap(sent, "pipe", 1) for sent, _ in pieces]
        count = lax.axis_size("dp")
        self.bits = count.bit_length() - 1
        self.halving = count == 1 << self.bits and self.kept[0].shape[0] % (16 * count) == 0

    def add(self, where):
        rows, columns = self.kept[0].shape
        (self.total,) = call(
            add_kernel,
            [("v", shape((rows * len(self.kept), columns)))],
            [("s", where)] + [("v", item) for item in (*self.kept, *self.got)],
        )
        return self.total

    def whole(self, where, *after):
        total = self.add(where)
        self.total = lax.psum(tie(total, *after), "dp")
        return total

    def halve(self, bit, where):
        parts = len(self.kept)
        rows, columns = self.kept[0].shape
        dims = (rows * parts // 2, columns)
        sent, kept = call(
            partial(halve_sum_kernel, bit, parts),
            [("v", shape(dims)), ("v", shape(dims, F32))],
            [("s", where)] + [("v", item) for item in (*self.kept, *self.got)],
        )
        self.kept, self.got = [kept], [swap(sent, "dp", 1 << bit)]
        return sent

    def join(self, bit, where):
        rows, columns = self.total.shape
        got = swap(self.total, "dp", 1 << bit)
        if bit or self.later is None:
            (self.total,) = call(
                partial(join_kernel, bit),
                [("v", shape((2 * rows, columns)))],
                [("s", where), ("v", self.total), ("v", got)],
            )
            return self.total
        later, part = self.later
        self.total, self.sent = call(
            partial(last_join_kernel, part),
            [("v", shape((2 * rows, columns)))] * 2,
            [("s", where), ("v", self.total), ("v", got), ("v", later.total)],
        )
        return self.total

    def steps(self):
        if not self.halving:
            return [self.whole]
        bits = range(self.bits)
        return (
            [partial(self.halve, bit) for bit in bits]
            + [self.add]
            + [partial(self.join, bit) for bit in reversed(bits)]
        )

    def finish(self):
        if self.sent is None:
            later, part = self.later
            rows = self.total.shape[0]
            piece = later.total[part * rows : (part + 1) * rows]
            self.sent = jnp.where(lax.axis_index("pipe") == 0, piece, self.total)
        self.other = swap(self.sent, "pipe", 1)


def layer_forward(layer, own_in, far_in, w_qkv, small, marks, where, hooks, upstream=None):
    own_q, own_kv, own_x_kept, own_q_kept = qkv(own_in, w_qkv, small)
    own_pair = core_swap(own_kv)
    far_q, far_kv, far_x_kept, far_q_kept = qkv(far_in, w_qkv, small)
    far_pair = core_swap(far_kv)
    w_out = hooks["out"](far_q)
    far_out, kv, kv_kept, far_o, far_lse = attn(
        layer, where, far_q, (own_kv, own_pair, far_kv, far_pair), marks, w_out
    )
    far_sent = far_out
    far_out = chip_swap(far_out)
    own_out, own_o, own_lse = attn(layer, where, own_q, (kv,), marks, w_out)
    own_h, hidden, resid1, own_h_kept = norm1(own_in, own_out, far_out, small)
    far_h = chip_swap(own_h)
    w_up, w_down = hooks["ffn"](far_sent, own_h)
    own_branch, own_act, own_slope = ffn(own_h, w_up, w_down, small, False)
    far_h = tie(far_h, own_branch)
    far_branch, far_act, far_slope, far_h_kept = ffn(far_h, w_up, w_down, small, True)
    own_branch = tie(own_branch, *hooks["next"](far_branch))
    branch = (hidden, own_branch, chip_swap(far_branch))
    turned = None
    if upstream is None:
        output, resid2, output_kept = norm2(*branch, small)
    else:
        *turned, output_kept = turn(*branch, upstream, small)
        output, resid2 = None, None
    kept = dict(
        x=(own_x_kept, far_x_kept),
        q=(own_q_kept, far_q_kept),
        kv=kv_kept,
        lse=(own_lse, far_lse),
        o=(own_o, far_o),
        resid=(resid1, resid2),
        turned=turned,
        weights=(w_qkv, w_out, w_up, w_down),
        h=(own_h_kept, far_h_kept),
        act=(own_act, far_act),
        slope=(own_slope, far_slope),
    )
    return output, output_kept, kept


def layer_backward(layer, upstream, kept, small, marks, where, hooks):
    if kept["turned"] is None:
        own_df, skip2, norm2_sums, *grad_in = norm2_back(upstream, kept["resid"][1], small)
    else:
        (own_df, skip2, norm2_sums), grad_in = kept["turned"], []
    far_df = chip_swap(own_df)
    w_qkv, w_out, w_up, w_down = kept["weights"]
    own_slope, far_slope = load(layer, tie(where, own_df), [], kept["slope"])
    own_dh, own_du, own_db = ffn_back(own_df, own_slope, w_up, w_down, False)
    far_df = tie(far_df, own_dh, *hooks["df"](own_dh))
    far_dh, far_du, far_db = ffn_back(far_df, far_slope, w_up, w_down, True)
    names = ("act", "h", "q", "lse", "x", "o")
    kv, *rows = load(
        layer,
        tie(where, far_dh, *hooks["dh"](far_dh)),
        [],
        [kept["kv"]] + [item for name in names for item in kept[name]],
    )
    own_act, far_act, own_h, far_h, own_q, far_q, own_lse, far_lse, own_x, far_x, own_o, far_o = rows
    grads = (own_h, far_h, own_act, far_act, own_df, far_df, own_du, far_du)
    pair = ffn_pair(grads)
    got = [core_swap(item) for item in pair]
    own_dh = tie(own_dh, pair[0], *hooks["norm"](pair[0]))
    own_dz, skip1, norm1_sums = norm1_back(own_dh, chip_swap(far_dh), skip2, kept["resid"][0], small)
    far_dz = chip_swap(own_dz)
    parts = ffn_own(tie(where, own_dz), grads, got)
    own_dq, own_dkv, own_send = attn_back(
        layer, 0, tie(where, parts[0]), own_dz, own_q, kv, marks, own_lse, w_out
    )
    own_pair = core_swap(own_send)
    far_dz = tie(far_dz, own_send, *hooks["dz"](own_send, parts))
    far_dq, far_dkv, far_send = attn_back(layer, 1, where, far_dz, far_q, kv, marks, far_lse, w_out)
    far_pair = core_swap(tie(far_send, *hooks["send"](far_send)))
    far_dx, own_d, far_d = row_grads(
        small, (own_dq, far_dq), (own_dkv, far_dkv), (own_pair, far_pair), w_qkv
    )
    own_dx, attn_own, attn_pair, qkv_sums = attn_grads(
        tie(where, far_dx, *hooks["dx"](far_dx)),
        (own_d, far_d),
        (own_x, far_x),
        (own_o, far_o),
        (own_dz, far_dz),
        w_qkv,
    )
    far_dx = chip_swap(far_dx)
    sums = (norm1_sums, norm2_sums, own_db, far_db, qkv_sums)
    return (own_dx, far_dx, skip1), grad_in, sums, (attn_own, core_swap(attn_pair))


def body(
    tokens,
    segment_ids,
    pad_mask,
    block_perm,
    qkv_weight,
    qkv_bias,
    out_weight,
    up_weight,
    up_bias,
    down_weight,
    norm_gain,
    shift_bias,
    cotangent,
):
    section = lax.axis_index("pipe")
    place = lax.axis_index("tensor")
    replica = lax.axis_index("dp")
    paired = lax.axis_size("dp") % 2 == 0
    width = tokens.shape[2]
    local = qkv_bias.shape[2]
    here = jnp.stack([section, place % 2, replica % 2, replica, place]).astype(jnp.int32)
    qkv_rows = jnp.transpose(qkv_weight[0], (0, 2, 1))

    def other_half(half, whole):
        if paired:
            return swap(half, "dp", 1)
        even = replica % 2 == 0
        rest = jnp.where(even, whole[..., width // 2 :], whole[..., : width // 2])
        return swap(rest, "pipe", 1)

    (qkv_half,) = halves_of(here, qkv_rows)
    qkv_x = swap(qkv_half, "pipe", 1)
    rows = lax.optimization_barrier(lax.dynamic_index_in_dim(tokens, section, 0, keepdims=False))
    far_rows = chip_swap(rows)
    (own_small,) = call(
        pack_kernel,
        [("v", shape((16, width), F32))],
        [("h", norm_gain), ("h", shift_bias), ("h", up_bias), ("h", qkv_bias), ("s", block_perm)],
        scratch=[
            pltpu.VMEM(item.shape, item.dtype) for item in (norm_gain, shift_bias, up_bias, qkv_bias)
        ],
        copies=4,
    )
    other_small = swap(own_small, "pipe", 1)
    up_half, down_half = halves_of(tie(here, own_small, qkv_half), up_weight, down_weight)
    up_x = swap(up_half, "pipe", 1)
    out_x = swap(tie(out_weight, qkv_x), "pipe", 1)
    (marks,) = call(
        marks_kernel,
        [("v", shape((8, segment_ids.shape[1] // 2), jnp.int32))],
        [("s", tie(here, up_x)), ("v", segment_ids), ("v", pad_mask)],
    )
    *smalls, flags = call(
        params_kernel,
        [("v", shape((16, width), F32))] * 2 + [("h", shape((8, PAIR), F32))],
        [("s", here)]
        + [
            ("v", item)
            for item in (own_small, other_small, core_swap(own_small), core_swap(other_small))
        ],
        scratch=[pltpu.VMEM((8, PAIR), F32)],
        copies=1,
    )
    heads = 2 * block_perm.shape[1]
    where = jnp.concatenate([here, flags[:2, :heads].reshape(-1).astype(jnp.int32)])
    def item(by_core, own, other, after=(), later=()):
        pair_own = core_swap(tie(own, *after) if after else own)
        pair_other = tuple(core_swap(tie(part, *later) if later else part) for part in other)
        return by_core, own, other, pair_own, pair_other

    other_qkv = other_half(tie(qkv_x, up_half, other_small, far_rows), qkv_rows)
    items = dict(qkv=item(True, qkv_rows, (qkv_x, other_qkv)))
    (first_qkv,) = load(0, tie(where, marks, *smalls, far_rows, up_x), [items["qkv"]])

    def first_out(after):
        fetched["down"] = swap(tie(down_half, up_x), "pipe", 1)
        fetched["up"] = other_half(tie(up_x, marks), up_weight)
        items["out"] = item(True, out_weight, (out_x,), (first_qkv,), (first_qkv,))
        return load(0, tie(where, after), [items["out"]])[0]

    fetched = {}

    def first_ffn(early, after):
        down_x = fetched["down"]
        other_down = other_half(tie(down_x, early), down_weight)
        items["up"] = item(False, up_weight, (up_x, fetched["up"]), (early,), (early,))
        items["down"] = item(False, down_weight, (down_x, other_down), (early,), (after,))
        return load_ffn(0, (), tie(where, after))

    def load_ffn(layer, arrays, after):
        return load(layer, after, [items["up"], items["down"]], arrays)

    second = []

    def load_second(after):
        second.extend(load(1, tie(where, after), [items["qkv"], items["out"]]))
        return second

    out_first, first_kept, kept_first = layer_forward(
        0,
        rows,
        far_rows,
        first_qkv,
        smalls[0],
        marks,
        where,
        {"out": first_out, "ffn": first_ffn, "next": load_second},
    )
    def second_ffn(early, after):
        return load_ffn(1, (), tie(where, after))

    upstream = lax.dynamic_index_in_dim(cotangent, section, 0, keepdims=False)
    _, second_kept, kept_second = layer_forward(
        1,
        out_first,
        chip_swap(out_first),
        second[0],
        smalls[1],
        marks,
        where,
        {
            "out": lambda after: second[1],
            "ffn": second_ffn,
            "next": lambda after: (),
        },
        upstream,
    )

    def place_outputs(first, second, got, after):
        return call(
            place_kernel,
            [("h", shape((1, 2) + first.shape))],
            [("s", after), ("h", first), ("h", second), ("v", got)],
            us=1.5,
            scratch=[pltpu.VMEM((2,) + first.shape, BF16)],
            copies=2,
        )[0]

    sums, steps = {}, {}

    def begin(name, *pieces):
        sums[name] = Sum(*pieces)
        steps[name] = sums[name].steps()

    def run(after, *names):
        for name in names:
            if steps[name]:
                after = steps[name].pop(0)(tie(where, after))
        return after

    outputs = []

    def nothing(*_):
        return ()

    def later_df(after):
        (picked,) = call(
            pick_kernel,
            [("v", shape(rows.shape))],
            [("s", tie(where, after)), ("h", first_kept), ("h", second_kept)],
            copies=1,
        )
        outputs.append(swap(picked, "pipe", 1))
        return (picked,)

    def later_dz(after, parts):
        begin("ab1", parts[0:2], parts[2:4])
        return outputs

    grads, _, small_second, attn_second = layer_backward(
        1,
        None,
        kept_second,
        smalls[1],
        marks,
        where,
        {
            "df": later_df,
            "dh": nothing,
            "norm": nothing,
            "dz": later_dz,
            "send": lambda after: sums["ab1"].got[:1],
            "dx": nothing,
        },
    )

    def first_df(after):
        sent, kept = split(tie(where, after), *attn_second)
        begin("c1", (sent, kept))
        return (run(sent, "ab1"),)

    def first_dz(after, parts):
        begin("a0", parts[0:2])
        begin("b0", parts[2:4])
        return (run(after, "ab1", "c1"),)

    def first_send(after):
        return (run(after, "ab1", "c1", "a0"),)

    def first_dx(after):
        return (run(after, "c1", "a0", "b0"),)

    grads, (grad_second,), small_first, attn_first = layer_backward(
        0,
        grads,
        kept_first,
        smalls[0],
        marks,
        where,
        {
            "df": first_df,
            "dh": nothing,
            "norm": lambda after: (run(after, "ab1"),),
            "dz": first_dz,
            "send": first_send,
            "dx": nothing,
        },
    )
    last = [attn_first[0]]

    def now():
        return tie(where, *last)

    def then(*values):
        last[:] = values

    def step(*names):
        then(run(last[-1], *names))

    def small_add(total, got):
        total, shared = call(
            small_add_kernel,
            [("v", shape((16, width), F32))] * 2,
            [("s", now()), ("v", total), ("v", got)],
        )
        then(total)
        return total, shared

    hops = [("pipe", 1)]
    count = lax.axis_size("dp")
    if not count & (count - 1):
        hops += [("dp", 1 << bit) for bit in range(count.bit_length() - 1)]
    total, pair_sums = call(
        pack_sums_kernel,
        [("v", shape((16, width), F32))] * 2,
        [("s", now())] + [("v", value) for value in (*small_first, *small_second)],
    )
    then(total)
    got = core_swap(pair_sums)
    sent, kept = split(now(), *attn_first)
    then(sent)
    begin("c0", (sent, kept))
    step("c1", "a0", "b0", "c0")
    total, shared = small_add(total, got)
    got = chip_swap(shared)
    step("a0", "b0", "c1", "ab1")
    total, _ = small_add(total, got)
    if len(hops) == 1:
        total = lax.psum(total, "dp")
    got = swap(total, *hops[0])
    sent, grad_first = call(
        grad_in_kernel,
        [("v", shape(rows.shape)), ("h", shape(rows.shape))],
        [("s", now())] + [("v", value) for value in grads] + [("h", grad_second)],
        scratch=[pltpu.VMEM(rows.shape, BF16)] * 2,
        copies=2,
    )
    then(sent)
    grad_got = swap(sent, "pipe", 1)
    step("a0", "c0", "b0")
    while steps["c1"]:
        step("c1")
    then(last[-1], grad_got)

    def last_of(*names):
        for name in names:
            while steps[name]:
                step(name)

    def finish(name, later, part):
        sums[name].later = (sums[later], part)
        last_of(name)
        sums[name].finish()

    for at, hop in enumerate(hops[1:]):
        total, _ = small_add(total, got)
        got = swap(total, *hop)
        if at == 0:
            last_of("ab1")
            finish("a0", "ab1", 0)
            step("c0", "b0")
        elif at == 1:
            step("c0")
            finish("b0", "ab1", 1)
    if len(hops) < 2:
        last_of("ab1")
        finish("a0", "ab1", 0)
    if len(hops) < 3:
        finish("b0", "ab1", 1)
    then(last[-1], sums["a0"].other)
    input_grad = place_outputs(grad_first, grad_second, grad_got, now())
    layer_out = place_outputs(first_kept, second_kept, outputs[0], tie(where, input_grad))
    then(layer_out)
    finish("c0", "c1", 0)
    outs = [shape(item.shape, F32) for item in (norm_gain, shift_bias, up_bias, qkv_bias)]
    gains, shifts, upb, qkvb = call(
        small_results_kernel,
        [("h", item) for item in outs],
        [("s", now()), ("v", total), ("v", got)],
        scratch=[pltpu.VMEM(item.shape, F32) for item in outs],
        copies=4,
    )
    then(gains)

    def pieces(later, *names):
        return [
            *(sums[name].total for name in names),
            *(sums[name].other for name in names),
            sums[later].total,
        ]

    upw, downw = results("ffn", now(), pieces("ab1", "a0", "b0"))
    qkvw, outw = results("attn", tie(where, upw), pieces("c1", "c0"))
    qkvw = jnp.transpose(qkvw, (0, 2, 1))
    return (
        layer_out,
        input_grad,
        qkvw[None],
        qkvb,
        outw[None],
        upw[None],
        upb,
        downw[None],
        gains,
        shifts,
    )


def solution(mesh):
    return jax.shard_map(
        body,
        mesh=mesh,
        in_specs=(
            P("dp", "tensor", None),
            P("dp", None),
            P("dp", None),
            P("pipe", "tensor", None),
            P("pipe", None, None, "tensor"),
            P("pipe", None, "tensor"),
            P("pipe", "tensor", None),
            P("pipe", None, "tensor"),
            P("pipe", "tensor"),
            P("pipe", "tensor", None),
            P("pipe", None, None),
            P("pipe", None, None),
            P("dp", "tensor", None),
        ),
        out_specs=(
            P("pipe", "dp", "tensor", None),
            P("pipe", "dp", "tensor", None),
            P("pipe", None, None, "tensor"),
            P("pipe", None, "tensor"),
            P("pipe", "tensor", None),
            P("pipe", None, "tensor"),
            P("pipe", "tensor"),
            P("pipe", "tensor", None),
            P("pipe", None, None),
            P("pipe", None, None),
        ),
        check_vma=False,
    )
```

```python
from functools import partial

import jax
import jax.numpy as jnp
from jax import lax
from jax.experimental import pallas as pl
from jax.experimental.pallas import tpu as pltpu
from jax.sharding import PartitionSpec as P

BF16 = jnp.bfloat16
F32 = jnp.float32
HEAD_DIM = 64
PAIR = 2 * HEAD_DIM
LOG2E = 1.4426950408889634
MASKED = -1e30
VMEM_LIMIT = 16 * 1024 * 1024
COST = 2e10
NORM_EPSILON_TERM = 1e-06

FLAGS = 5

SPACES = {"v": pltpu.VMEM, "s": pltpu.SMEM, "h": pl.ANY}
PLACES = {"v": pltpu.VMEM, "s": pl.ANY, "h": pltpu.HBM}


def shape(dims, dtype=BF16):
    return jax.ShapeDtypeStruct(dims, dtype)


def call(kernel, outs, args, us=0.1, scratch=(), copies=0):
    flops = int(us * COST)
    scratch = list(scratch)
    if copies:
        scratch.append(pltpu.SemaphoreType.DMA((copies,)))
    return pl.pallas_call(
        kernel,
        name=(kernel.func if isinstance(kernel, partial) else kernel).__name__,
        out_shape=[PLACES[space](item.shape, item.dtype) for space, item in outs],
        in_specs=[pl.BlockSpec(memory_space=SPACES[space]) for space, _ in args],
        out_specs=[pl.BlockSpec(memory_space=SPACES[space]) for space, _ in outs],
        scratch_shapes=scratch,
        compiler_params=pltpu.CompilerParams(vmem_limit_bytes=VMEM_LIMIT),
        cost_estimate=pl.CostEstimate(flops=flops, bytes_accessed=0, transcendentals=0),
    )(*[pltpu.with_memory_space_constraint(item, PLACES[space]) for space, item in args])


class Copies:
    def __init__(self, sems):
        self.sems, self.pending = sems, []

    def sem(self):
        at = len(self.pending)
        return self.sems[at] if isinstance(self.sems, list) else self.sems.at[at]

    def start(self, source, target):
        copy = pltpu.make_async_copy(source, target, self.sem())
        copy.start()
        self.pending.append(copy)

    def start_one(self, cases, target):
        sem = self.sem()
        made = []
        for condition, source in cases:
            made.append(pltpu.make_async_copy(source, target, sem))
            pl.when(condition)(made[-1].start)
        self.pending.append(made[0])

    def done(self):
        for copy in self.pending:
            copy.wait()


def loop(count, step):
    lax.fori_loop(0, count, lambda i, _: step(i), None)


def part_of(i, size):
    return pl.ds(pl.multiple_of(i * size, size), size)


def dot(left, right):
    return jnp.dot(left, right, preferred_element_type=F32)


def dot_tn(left, right):
    return lax.dot_general(left, right, (((0,), (0,)), ((), ())), preferred_element_type=F32)


def dot_nt(left, right):
    return lax.dot_general(left, right, (((1,), (1,)), ((), ())), preferred_element_type=F32)


def pack_kernel(gains_in, shifts_in, up_in, qkv_in, perm_ref, out_ref, gains, shifts, up, qkv_b, sems):
    copies = Copies(sems)
    for source, target in ((gains_in, gains), (shifts_in, shifts), (up_in, up), (qkv_in, qkv_b)):
        copies.start(source, target)
    out_ref[...] = jnp.zeros_like(out_ref)
    lane = lax.broadcasted_iota(jnp.int32, (1, out_ref.shape[1]), 1)
    flags = jnp.zeros((1, out_ref.shape[1]), F32)
    for head in range(perm_ref.shape[1]):
        flags = jnp.where(lane == head, perm_ref[0, head, 0].astype(F32), flags)
    out_ref[9:10] = flags
    copies.done()
    out_ref[0:2] = gains[0]
    out_ref[2:6] = shifts[0]
    out_ref[6:7] = up[...].astype(F32)
    out_ref[7:9, 0 : qkv_b.shape[2]] = qkv_b[0].astype(F32)


GAIN1, GAIN2, BIAS_OUT, SHIFT1, BIAS2, SHIFT2, BIAS_UP, BIAS_Q, TURNED = 0, 1, 2, 3, 4, 5, 6, 8, 10


def params_kernel(where_ref, own_ref, other_ref, pair_ref, other_pair_ref, first_out, second_out, flags_copy, flags, sems):
    section, core = where_ref[0], where_ref[1]
    width = own_ref.shape[1]
    local = width // 4
    heads = local // HEAD_DIM
    lane = lax.broadcasted_iota(jnp.int32, (1, width), 1)
    flags[...] = jnp.zeros_like(flags)
    for layer, out_ref in enumerate((first_out, second_out)):
        here = section == layer
        mine = jnp.where(here, own_ref[...], other_ref[...])
        pair = jnp.where(here, pair_ref[...], other_pair_ref[...])
        first = jnp.where(core == 0, mine, pair)
        second = jnp.where(core == 0, pair, mine)
        out_ref[...] = mine
        out_ref[BIAS_UP + 1 : BIAS_UP + 2] = pair[BIAS_UP : BIAS_UP + 1]
        biases = jnp.where(lane < local, first, pltpu.roll(second, local, 1))
        out_ref[BIAS_Q : BIAS_Q + 2] = biases[7:9]
        turned = jnp.where(lane < heads, first, pltpu.roll(second, heads, 1))[9:10]
        lanes = jnp.zeros((1, width), F32)
        for head in range(2 * heads):
            chosen = (lane // HEAD_DIM) % (2 * heads) == head
            lanes = jnp.where(chosen, turned[:, head : head + 1], lanes)
        out_ref[TURNED : TURNED + 1] = lanes
        flags[layer : layer + 1] = turned[:, 0:PAIR]
    copies = Copies(sems)
    copies.start(flags, flags_copy)
    copies.done()


def marks_kernel(where_ref, segments_ref, real_ref, out_ref):
    quarter = out_ref.shape[1] // 2
    out_ref[...] = jnp.zeros_like(out_ref)
    for r in range(4):
        cols = pl.ds(pl.multiple_of((where_ref[4] ^ r) * quarter, PAIR), quarter)
        at = slice((r % 2) * quarter, (r % 2 + 1) * quarter)
        segment = jnp.where(where_ref[0] == 0, segments_ref[0:1, cols], segments_ref[1:2, cols])
        real = jnp.where(where_ref[0] == 0, real_ref[0:1, cols], real_ref[1:2, cols])
        out_ref[1 + r // 2 : 2 + r // 2, at] = jnp.where(real == 1, segment, -1)
        if r % 2 == 0:
            out_ref[0:1, (r // 2) * quarter : (r // 2 + 1) * quarter] = segment


def halve_kernel(where_ref, *refs):
    count = len(refs) // 2
    copies = Copies(refs[-1])
    for source, half in zip(refs[:count], refs[count:-1]):
        columns = half.shape[2]
        copies.start_one(
            [
                (where_ref[2] == side, source.at[:, :, pl.ds(side * columns, columns)])
                for side in range(2)
            ],
            half,
        )
    copies.done()


def halves_of(where, *wholes):
    return call(
        halve_kernel,
        [("v", shape(whole.shape[:2] + (whole.shape[2] // 2,))) for whole in wholes],
        [("s", where)] + [("h", whole) for whole in wholes],
        copies=len(wholes),
    )


def weight_copies(copies, where_ref, layer, k, own, other, target):
    here = where_ref[0] == layer
    if len(other) == 1:
        copies.start_one(
            [(here, own.at[k]), (jnp.logical_not(here), other[0].at[k])], target(slice(None))
        )
        return
    columns = other[0].shape[-1]
    for side in range(2):
        cols = pl.ds(side * columns, columns)
        direct = where_ref[2] == side
        copies.start_one(
            [
                (here, own.at[k, :, cols]),
                (jnp.logical_not(here) & direct, other[0].at[k]),
                (jnp.logical_not(here) & jnp.logical_not(direct), other[1].at[k]),
            ],
            target(cols),
        )


def load_kernel(layer, items, plain, where_ref, *refs):
    sems = refs[-1]
    copies = Copies(sems)
    count = sum(2 * (1 + parts) for _, parts in items)
    sources, plain_in, outs = refs[:count], refs[count : count + plain], refs[count + plain : -1]
    for (by_core, parts), out_ref in zip(items, outs):
        for pair in range(2):
            own, *other = sources[: 1 + parts]
            sources = sources[1 + parts :]
            if by_core:
                rows = out_ref.shape[1] // 2
                slot = (where_ref[1] + pair) % 2
                at = pl.ds(pl.multiple_of(slot * rows, rows), rows)
                for k in range(out_ref.shape[0]):
                    weight_copies(
                        copies, where_ref, layer, k, own, other, lambda cols, k=k: out_ref.at[k, at, cols]
                    )
            else:
                weight_copies(
                    copies, where_ref, layer, 0, own, other, lambda cols: out_ref.at[pair, :, cols]
                )
    for source, target in zip(plain_in, outs[len(items) :]):
        copies.start(source, target)
    copies.done()


def load(layer, where, items, arrays=()):
    outs, sources, kinds, count = [], [], [], len(arrays)
    for by_core, own, other, pair_own, pair_other in items:
        k, rows, columns = own.shape
        outs.append(shape((k, 2 * rows, columns)) if by_core else shape((2, rows, columns)))
        sources += [own, *other, pair_own, *pair_other]
        kinds.append((by_core, len(other)))
        count += 2 * k * len(other)
    outs += [shape(item.shape, item.dtype) for item in arrays]
    return call(
        partial(load_kernel, layer, kinds, len(arrays)),
        [("v", item) for item in outs],
        [("s", where)] + [("h", item) for item in (*sources, *arrays)],
        us=2.4,
        copies=count,
    )


def qkv_kernel(x_ref, w_ref, b_ref, q_ref, kv_ref, x_copy, q_copy, sems):
    copies = Copies(sems)
    copies.start(x_ref, x_copy)
    x = x_ref[...]
    width = q_ref.shape[1]
    q_ref[...] = (dot_nt(x, w_ref[0]) + b_ref[BIAS_Q : BIAS_Q + 1, :width]).astype(BF16)
    copies.start(q_ref, q_copy)
    kv_ref[:, :width] = dot_nt(x, w_ref[1]).astype(BF16)
    kv_ref[:, width:] = (dot_nt(x, w_ref[2]) + b_ref[BIAS_Q + 1 : BIAS_Q + 2, :width]).astype(BF16)
    copies.done()


def qkv(x, w, b):
    rows, width = x.shape[0], w.shape[1]
    return call(
        qkv_kernel,
        [
            ("v", shape((rows, width))),
            ("v", shape((rows, 2 * width))),
            ("h", shape(x.shape)),
            ("h", shape((rows, width))),
        ],
        [("v", x), ("v", w), ("v", b)],
        1.1,
        copies=2,
    )


def lanes_of(rows):
    return lax.broadcasted_iota(jnp.int32, (rows, PAIR), 1)


def fill_bias(bias, side, marks_ref):
    rows = bias.shape[1]
    wanted = jnp.transpose(marks_ref[:, side * rows : (side + 1) * rows])[:, 0:1]
    for j in range(2):
        bias[j] = jnp.where(wanted == marks_ref[1 + j : 2 + j, :], 0.0, MASKED).astype(F32)


def block_of(where_ref, layer, head, turned):
    return where_ref[FLAGS + 6 * layer + head] ^ turned


def attn_rows(layer, where_ref, turned, q_ref, kv_ref, marks_ref, o_ref, lse_ref, bias):
    rows, width = q_ref.shape
    fill_bias(bias, turned, marks_ref)
    lanes = lanes_of(rows)
    low = lanes < HEAD_DIM
    scale = HEAD_DIM**-0.5 * LOG2E
    lse_ref[...] = jnp.zeros_like(lse_ref)

    def step(tile):
        cols, vcols = part_of(tile, PAIR), part_of(tile + width // PAIR, PAIR)
        q = q_ref[:, cols]
        mixed = []
        for side in range(2):
            head = 2 * tile + side
            block = block_of(where_ref, layer, head, turned)
            q_head = jnp.where(low if side == 0 else ~low, q, jnp.zeros_like(q))
            s = dot_nt(q_head, kv_ref[block, :, cols]) * scale + bias[block]
            top = jnp.maximum(jnp.max(s, axis=1, keepdims=True), 0.0)
            e = jnp.exp2(s - top)
            total = jnp.exp2(-top) + jnp.sum(e, axis=1, keepdims=True)
            mixed.append(dot(e.astype(BF16), kv_ref[block, :, vcols]) * (1.0 / total))
            lse_ref[...] = jnp.where(lanes == head, top + jnp.log2(total), lse_ref[...])
        o_ref[:, cols] = jnp.where(low, mixed[0], mixed[1]).astype(BF16)

    loop(width // PAIR, step)


def attn_far_kernel(
    layer, where_ref, q_ref, kv0_ref, kv1_ref, kv2_ref, kv3_ref, marks_ref, w_ref,
    out_ref, kv_ref, kv_copy, o_copy, lse_copy, bias, o_ref, lse_ref, sems,
):
    copies = Copies(sems)
    half = kv0_ref.shape[0]
    for block, pair in enumerate(((kv0_ref, kv1_ref), (kv2_ref, kv3_ref))):
        kv_ref[block, :half] = pair[0][...]
        kv_ref[block, half:] = pair[1][...]
    copies.start(kv_ref, kv_copy)
    attn_rows(layer, where_ref, 1, q_ref, kv_ref, marks_ref, o_ref, lse_ref, bias)
    copies.start(o_ref, o_copy)
    copies.start(lse_ref, lse_copy)
    out_ref[...] = dot(o_ref[...], w_ref[0]).astype(out_ref.dtype)
    copies.done()


def attn_own_kernel(
    layer, where_ref, q_ref, kv_ref, marks_ref, w_ref, out_ref, o_copy, lse_copy, bias, o_ref, lse_ref, sems
):
    copies = Copies(sems)
    attn_rows(layer, where_ref, 0, q_ref, kv_ref, marks_ref, o_ref, lse_ref, bias)
    copies.start(o_ref, o_copy)
    copies.start(lse_ref, lse_copy)
    out_ref[...] = dot(o_ref[...], w_ref[0]).astype(out_ref.dtype)
    copies.done()


def attn(layer, where, q, kv, marks, w):
    rows, width = q.shape
    far = len(kv) > 1
    outs = [("v", shape((rows, w.shape[2]), BF16 if far else F32))]
    if far:
        joined = shape((2, 2 * rows, kv[0].shape[1]))
        outs += [("v", joined), ("h", joined)]
    outs += [("h", shape((rows, width))), ("h", shape((rows, PAIR), F32))]
    args = [("s", where)] + [("v", item) for item in (q, *kv, marks, w)]
    return call(
        partial(attn_far_kernel if far else attn_own_kernel, layer),
        outs,
        args,
        4.6,
        scratch=[
            pltpu.VMEM((2, rows, 2 * rows), F32),
            pltpu.VMEM((rows, width), BF16),
            pltpu.VMEM((rows, PAIR), F32),
        ],
        copies=3 if far else 2,
    )


def normed_rows(resid):
    centred = resid - jnp.mean(resid, axis=1, keepdims=True)
    inverse = lax.rsqrt(jnp.mean(centred * centred, axis=1, keepdims=True) + NORM_EPSILON_TERM)
    return centred * inverse, inverse


def norm1_kernel(x_ref, own_ref, far_ref, norms_ref, low_ref, full_ref, resid_copy, low_copy, resid, sems):
    copies = Copies(sems)
    projected = own_ref[...] + far_ref[...].astype(F32)
    total = x_ref[...].astype(F32) + projected + norms_ref[BIAS_OUT : BIAS_OUT + 1, :]
    resid[...] = total
    copies.start(resid, resid_copy)
    hidden = normed_rows(total)[0] * norms_ref[GAIN1 : GAIN1 + 1, :] + norms_ref[SHIFT1 : SHIFT1 + 1, :]
    full_ref[...] = hidden
    low_ref[...] = hidden.astype(BF16)
    copies.start(low_ref, low_copy)
    copies.done()


def norm1(x, own, far, norms):
    return call(
        norm1_kernel,
        [("v", shape(x.shape)), ("v", shape(x.shape, F32)), ("h", shape(x.shape, F32)), ("h", shape(x.shape))],
        [("v", x), ("v", own), ("v", far), ("v", norms)],
        scratch=[pltpu.VMEM(x.shape, F32)],
        us=1.2,
        copies=2,
    )


def norm2_kernel(h_ref, own_ref, far_ref, norms_ref, low_ref, resid_copy, low_copy, resid, sems):
    copies = Copies(sems)
    branch = own_ref[...] + far_ref[...].astype(F32)
    total = h_ref[...] + branch + norms_ref[BIAS2 : BIAS2 + 1, :]
    resid[...] = total
    copies.start(resid, resid_copy)
    out = normed_rows(total)[0] * norms_ref[GAIN2 : GAIN2 + 1, :] + norms_ref[SHIFT2 : SHIFT2 + 1, :]
    low_ref[...] = out.astype(BF16)
    copies.start(low_ref, low_copy)
    copies.done()


def norm2(h, own, far, norms):
    return call(
        norm2_kernel,
        [("v", shape(h.shape)), ("h", shape(h.shape, F32)), ("h", shape(h.shape))],
        [("v", h), ("v", own), ("v", far), ("v", norms)],
        scratch=[pltpu.VMEM(h.shape, F32)],
        us=1.2,
        copies=2,
    )


TAIL = tuple(
    0.5 * c
    for c in (
        0.05029408002973294, -0.1830316054165625, 0.16930258232763196, -0.005798692821681883,
        0.14152663657068731, 0.16851528425000623, 0.20784663429852349, 0.22566934002005623,
        0.22567586682378352,
    )
)


def gelu_and_slope(u):
    bell = jnp.exp2(u * u * (-0.5 * LOG2E))
    t = 1.0 / (1.0 + jnp.abs(u) * (0.4 * 0.5**0.5))
    poly = TAIL[0]
    for c in TAIL[1:]:
        poly = poly * t + c
    tail = poly * t * bell
    below = jnp.where(u < 0.0, tail, 1.0 - tail)
    return u * below, below + u * bell * 0.3989422804014327


UNITS = 768


def ffn_kernel(far, h_ref, up_ref, down_ref, b_ref, out_ref, act_copy, slope_copy, *rest):
    act_ref, slope_ref, total_ref, sems = rest[-4:]
    steps = up_ref.shape[2] // UNITS
    if far:
        rows_copy = pltpu.make_async_copy(h_ref, rest[0], sems.at[4 * steps])
        rows_copy.start()
    total_ref[...] = jnp.zeros_like(total_ref)

    def copies_of(i):
        half, cols = i // steps, part_of(i % steps, UNITS)
        return [
            pltpu.make_async_copy(kept.at[half, :, cols], copy.at[half, :, cols], sems.at[2 * i + k])
            for k, (kept, copy) in enumerate(((act_ref, act_copy), (slope_ref, slope_copy)))
        ]

    def step(i):
        half, cols = i // steps, part_of(i % steps, UNITS)
        pre = dot(h_ref[...], up_ref[half, :, cols]) + b_ref[pl.ds(BIAS_UP + half, 1), cols]
        act, slope = gelu_and_slope(pre)
        act = act.astype(BF16)
        act_ref[half, :, cols] = act
        slope_ref[half, :, cols] = slope.astype(BF16)
        for copy in copies_of(i):
            copy.start()
        total_ref[...] += dot(act, down_ref[half, cols, :])

    loop(2 * steps, step)
    out_ref[...] = total_ref[...].astype(out_ref.dtype)

    def finish(i):
        for copy in copies_of(i):
            copy.wait()

    loop(2 * steps, finish)
    if far:
        rows_copy.wait()


def ffn(h, up, down, b, far):
    rows, width = h.shape
    units = up.shape[2]
    outs = [
        ("v", shape((rows, width), BF16 if far else F32)),
        ("h", shape((2, rows, units))),
        ("h", shape((2, rows, units))),
    ]
    if far:
        outs.append(("h", shape(h.shape)))
    return call(
        partial(ffn_kernel, far),
        outs,
        [("v", h), ("v", up), ("v", down), ("v", b)],
        0.1,
        scratch=[pltpu.VMEM((2, rows, units), BF16)] * 2 + [pltpu.VMEM((rows, width), F32)],
        copies=4 * (units // UNITS) + 1,
    )


def norm_back(upstream, resid, gain, low_ref, full_ref, sums_ref):
    normed, inverse = normed_rows(resid)
    scaled = upstream * gain
    inner = (
        scaled
        - jnp.mean(scaled, axis=1, keepdims=True)
        - normed * jnp.mean(scaled * normed, axis=1, keepdims=True)
    )
    grad = inverse * inner
    full_ref[...] = grad
    low_ref[...] = grad.astype(BF16)
    sums_ref[...] = jnp.zeros_like(sums_ref)
    sums_ref[0:1] = jnp.sum(upstream * normed, axis=0, keepdims=True)
    sums_ref[1:2] = jnp.sum(upstream, axis=0, keepdims=True)
    sums_ref[2:3] = jnp.sum(grad, axis=0, keepdims=True)


def norm2_back_kernel(inner, *refs):
    if inner:
        own_ref, far_ref, resid1_ref, resid_in, norms_ref, *refs = refs
        low_ref, full_ref, sums_ref, grad_copy, resid, grad_ref, sems = refs
    else:
        up_ref, resid_in, norms_ref, low_ref, full_ref, sums_ref, resid, sems = refs
    copies = Copies(sems)
    copies.start(resid_in, resid)
    if inner:
        grad_in = (own_ref[...] + far_ref[...].astype(F32) + resid1_ref[...]).astype(BF16)
        grad_ref[...] = grad_in
        copies.start(grad_ref, grad_copy)
    else:
        grad_in = up_ref[...]
    copies.done()
    gain = norms_ref[GAIN2 : GAIN2 + 1, :]
    norm_back(grad_in.astype(F32), resid[...], gain, low_ref, full_ref, sums_ref)


def turn_kernel(h_ref, own_ref, far_ref, up_ref, norms_ref, low_ref, full_ref, sums_ref, out_copy, out, sems):
    branch = own_ref[...] + far_ref[...].astype(F32)
    resid = h_ref[...] + branch + norms_ref[BIAS2 : BIAS2 + 1, :]
    gain = norms_ref[GAIN2 : GAIN2 + 1, :]
    out[...] = (normed_rows(resid)[0] * gain + norms_ref[SHIFT2 : SHIFT2 + 1, :]).astype(BF16)
    copies = Copies(sems)
    copies.start(out, out_copy)
    norm_back(up_ref[...].astype(F32), resid, gain, low_ref, full_ref, sums_ref)
    copies.done()


def turn(h, own, far, upstream, norms):
    dims = h.shape
    return call(
        turn_kernel,
        [
            ("v", shape(dims)),
            ("v", shape(dims, F32)),
            ("v", shape((8, dims[1]), F32)),
            ("h", shape(dims)),
        ],
        [("v", item) for item in (h, own, far, upstream, norms)],
        scratch=[pltpu.VMEM(dims, BF16)],
        us=2.5,
        copies=1,
    )


def norm2_back(upstream, resid, norms):
    dims = upstream[0].shape
    inner = len(upstream) > 1
    outs = [("v", shape(dims)), ("v", shape(dims, F32)), ("v", shape((8, dims[1]), F32))]
    scratch = [pltpu.VMEM(dims, F32)]
    if inner:
        outs.append(("h", shape(dims)))
        scratch.append(pltpu.VMEM(dims, BF16))
    return call(
        partial(norm2_back_kernel, inner),
        outs,
        [("v", item) for item in upstream] + [("h", resid), ("v", norms)],
        scratch=scratch,
        us=1.7,
        copies=2,
    )


def norm1_back_kernel(own_ref, far_ref, skip_ref, resid_in, norms_ref, low_ref, full_ref, sums_ref, resid, sems):
    copies = Copies(sems)
    copies.start(resid_in, resid)
    upstream = own_ref[...] + far_ref[...].astype(F32) + skip_ref[...]
    copies.done()
    gain = norms_ref[GAIN1 : GAIN1 + 1, :]
    norm_back(upstream, resid[...], gain, low_ref, full_ref, sums_ref)


def norm1_back(own, far, skip, resid, norms):
    dims = own.shape
    return call(
        norm1_back_kernel,
        [("v", shape(dims)), ("v", shape(dims, F32)), ("v", shape((8, dims[1]), F32))],
        [("v", own), ("v", far), ("v", skip), ("h", resid), ("v", norms)],
        scratch=[pltpu.VMEM(dims, F32)],
        us=1.7,
        copies=1,
    )


def ffn_back_kernel(df_ref, slope_ref, up_ref, down_ref, dh_ref, du_ref, db_ref, total_ref):
    units = up_ref.shape[2]
    steps = units // UNITS
    total_ref[...] = jnp.zeros_like(total_ref)

    def step(i):
        half, cols = i // steps, part_of(i % steps, UNITS)
        du = dot_nt(df_ref[...], down_ref[half, cols, :]) * slope_ref[half, :, cols].astype(F32)
        du = du.astype(BF16)
        du_ref[:, part_of(i, UNITS)] = du
        db_ref[pl.ds(half, 1), cols] = jnp.sum(du.astype(F32), axis=0, keepdims=True)
        total_ref[...] += dot_nt(du, up_ref[half, :, cols])

    loop(2 * steps, step)
    dh_ref[...] = total_ref[...].astype(dh_ref.dtype)


def ffn_back(df, slope, up, down, far):
    rows, width = df.shape
    units = 2 * up.shape[2]
    return call(
        ffn_back_kernel,
        [
            ("v", shape((rows, width), BF16 if far else F32)),
            ("v", shape((rows, units))),
            ("v", shape((2, units // 2), F32)),
        ],
        [("v", df), ("v", slope), ("v", up), ("v", down)],
        1.8,
        scratch=[pltpu.VMEM((rows, width), F32)],
    )


def ffn_grads_of(half, h, act, df, du):
    units = act[0].shape[2]
    cols = slice(half * units, (half + 1) * units)
    up = dot_tn(h[0][...], du[0][:, cols]) + dot_tn(h[1][...], du[1][:, cols])
    down = dot_tn(act[0][half], df[0][...]) + dot_tn(act[1][half], df[1][...])
    return up, down


def ffn_pair_kernel(h0, h1, a0, a1, df0, df1, du0, du1, up_ref, down_ref):
    up, down = ffn_grads_of(1, (h0, h1), (a0, a1), (df0, df1), (du0, du1))
    up_ref[...] = up.astype(BF16)
    down_ref[...] = down.astype(BF16)


def ffn_own_kernel(where_ref, h0, h1, a0, a1, df0, df1, du0, du1, up_got, down_got, *outs):
    up, down = ffn_grads_of(0, (h0, h1), (a0, a1), (df0, df1), (du0, du1))
    up += up_got[...].astype(F32)
    down += down_got[...].astype(F32)
    first = where_ref[0] == 0
    half = outs[0].shape[0]
    for part in range(2):
        rows = slice(part * half, (part + 1) * half)
        outs[2 * part][...] = jnp.where(first, down[rows], up[rows]).astype(BF16)
        outs[2 * part + 1][...] = jnp.where(first, up[rows], down[rows])


def ffn_pair(args):
    rows, width = args[0].shape
    units = args[2].shape[2]
    return call(
        ffn_pair_kernel,
        [("v", shape((width, units)))] * 2,
        [("v", item) for item in args],
        1.4,
    )


def ffn_own(where, args, got):
    rows, width = args[0].shape
    units = args[2].shape[2]
    return call(
        ffn_own_kernel,
        [("v", shape((width // 2, units))), ("v", shape((width // 2, units), F32))] * 2,
        [("s", where)] + [("v", item) for item in (*args, *got)],
        2.2,
    )


def attn_back_kernel(
    layer, turned, where_ref, dz_ref, q_ref, kv_ref, marks_ref, lse_ref, w_ref,
    dq_ref, dkv_ref, dkv_pair_ref, bias, do_ref,
):
    rows, width = q_ref.shape
    fill_bias(bias, turned, marks_ref)
    low = lanes_of(rows) < HEAD_DIM
    scale = HEAD_DIM**-0.5
    do_ref[...] = dot_nt(dz_ref[...], w_ref[0]).astype(BF16)
    lanes = lanes_of(rows)
    tiles = width // PAIR

    def step(tile):
        cols, vcols = part_of(tile, PAIR), part_of(tile + tiles, PAIR)
        q, do = q_ref[:, cols], do_ref[:, cols]
        dq, dk, dv = [], 0.0, 0.0
        for side in range(2):
            head = 2 * tile + side
            block = block_of(where_ref, layer, head, turned)
            part = low if side == 0 else ~low
            q_head = jnp.where(part, q, jnp.zeros_like(q))
            do_head = jnp.where(part, do, jnp.zeros_like(do))
            k = kv_ref[block, :, cols]
            s = dot_nt(q_head, k) * (scale * LOG2E) + bias[block]
            log_total = jnp.sum(jnp.where(lanes == head, lse_ref[...], 0.0), axis=1, keepdims=True)
            p = jnp.exp2(s - log_total)
            dp = dot_nt(do_head, kv_ref[block, :, vcols])
            centre = jnp.sum(p * dp, axis=1, keepdims=True)
            ds = (p * (dp - centre)).astype(BF16)
            dq.append(dot(ds, k))
            dv += dot_tn(p.astype(BF16), do_head)
            dk += dot_tn(ds, q_head)
        dq_ref[:, cols] = (jnp.where(low, dq[0], dq[1]) * scale).astype(BF16)
        dkv_ref[:, cols] = dk[:rows] * scale
        dkv_ref[:, vcols] = dv[:rows]
        dkv_pair_ref[:, cols] = (dk[rows:] * scale).astype(BF16)
        dkv_pair_ref[:, vcols] = dv[rows:].astype(BF16)

    loop(tiles, step)


def attn_back(layer, turned, where, dz, q, kv, marks, lse, w):
    rows, width = q.shape
    return call(
        partial(attn_back_kernel, layer, turned),
        [("v", shape((rows, width))), ("v", shape((rows, 2 * width), F32)), ("v", shape((rows, 2 * width)))],
        [("s", where)] + [("v", item) for item in (dz, q, kv, marks, lse, w)],
        4.4,
        scratch=[pltpu.VMEM((2, rows, 2 * rows), F32), pltpu.VMEM((rows, width), BF16)],
    )


def row_grads_kernel(
    small_ref, dq0_ref, dq1_ref, kv0_ref, kv1_ref, pair0_ref, pair1_ref, w_ref, dx_ref, d0_ref, d1_ref
):
    width = dq0_ref.shape[1]
    turned = small_ref[TURNED : TURNED + 1, :] == 1.0
    near = kv0_ref[...] + pair0_ref[...].astype(F32)
    far = kv1_ref[...] + pair1_ref[...].astype(F32)
    d0_ref[:, :width] = dq0_ref[...]
    d1_ref[:, :width] = dq1_ref[...]
    d0_ref[:, width:] = jnp.where(turned, far, near).astype(BF16)
    d1_ref[:, width:] = jnp.where(turned, near, far).astype(BF16)
    total = None
    for k in range(3):
        part = dot(d1_ref[:, k * width : (k + 1) * width], w_ref[k])
        total = part if total is None else total + part
    dx_ref[...] = total.astype(BF16)


def row_grads(small, dq, kv, pair, w):
    rows, width = dq[0].shape
    return call(
        row_grads_kernel,
        [("v", shape((rows, w.shape[2])))] + [("v", shape((rows, 3 * width)))] * 2,
        [("v", item) for item in (small, *dq, *kv, *pair, w)],
        0.9,
    )


def attn_grads_kernel(
    where_ref, d0_ref, d1_ref, x0_ref, x1_ref, o0_ref, o1_ref, dz0_ref, dz1_ref, w_ref,
    dx_ref, own_ref, pair_ref, db_ref,
):
    width = o0_ref.shape[1]
    first_core = where_ref[1] == 0
    share = width // 2
    db_ref[...] = jnp.zeros_like(db_ref)
    for k in range(4):
        cols = slice(k * width, (k + 1) * width)
        if k < 3:
            left, right = (d0_ref[:, cols], d1_ref[:, cols]), (x0_ref[...], x1_ref[...])
        else:
            left, right = (o0_ref[...], o1_ref[...]), (dz0_ref[...], dz1_ref[...])
        if k in (0, 2):
            sums = jnp.sum(left[0].astype(F32), axis=0, keepdims=True)
            sums += jnp.sum(left[1].astype(F32), axis=0, keepdims=True)
            db_ref[0:1, k // 2 * width : (k // 2 + 1) * width] = sums
        both = dot_tn(left[0], right[0]) + dot_tn(left[1], right[1])
        rows = slice(k * share, (k + 1) * share)
        own_ref[rows] = jnp.where(first_core, both[:share], both[share:])
        pair_ref[rows] = jnp.where(first_core, both[share:], both[:share]).astype(BF16)
    total = None
    for k in range(3):
        part = dot(d0_ref[:, k * width : (k + 1) * width], w_ref[k])
        total = part if total is None else total + part
    dx_ref[...] = total


def attn_grads(where, d, x, o, dz, w):
    rows, width = o[0].shape
    columns = x[0].shape[1]
    return call(
        attn_grads_kernel,
        [
            ("v", shape((rows, columns), F32)),
            ("v", shape((2 * width, columns), F32)),
            ("v", shape((2 * width, columns))),
            ("v", shape((8, 2 * width), F32)),
        ],
        [("s", where)] + [("v", item) for item in (*d, *x, *o, *dz, w)],
        2.7,
    )


def split_kernel(where_ref, own_ref, got_ref, sent_ref, kept_ref):
    half = kept_ref.shape[0]
    first = where_ref[0] == 0
    top = own_ref[:half] + got_ref[:half].astype(F32)
    bottom = own_ref[half:] + got_ref[half:].astype(F32)
    kept_ref[...] = jnp.where(first, top, bottom)
    sent_ref[...] = jnp.where(first, bottom, top).astype(BF16)


def split(where, own, got):
    rows, columns = own.shape
    return call(
        split_kernel,
        [("v", shape((rows // 2, columns))), ("v", shape((rows // 2, columns), F32))],
        [("s", where), ("v", own), ("v", got)],
    )


def add_kernel(where_ref, *refs):
    parts, out_ref = len(refs) // 2, refs[-1]
    rows = refs[0].shape[0]
    for part in range(parts):
        total = refs[part][...] + refs[parts + part][...].astype(F32)
        out_ref[part * rows : (part + 1) * rows] = total.astype(BF16)


def halve_sum_kernel(bit, parts, where_ref, *refs):
    kept, got, (sent_ref, own_ref) = refs[:parts], refs[parts : 2 * parts], refs[2 * parts :]
    mine = (where_ref[3] >> bit) & 1
    if parts == 2:
        for half in range(2):

            @pl.when(mine == half)
            def _():
                own_ref[...] = kept[half][...] + got[half][...].astype(F32)
                sent_ref[...] = (kept[1 - half][...] + got[1 - half][...].astype(F32)).astype(BF16)

        return
    rows = own_ref.shape[0]
    at = pl.ds(pl.multiple_of(mine * rows, 16), rows)
    own_ref[...] = kept[0][at] + got[0][at].astype(F32)
    at = pl.ds(pl.multiple_of((1 - mine) * rows, 16), rows)
    sent_ref[...] = (kept[0][at] + got[0][at].astype(F32)).astype(BF16)


def join_kernel(bit, where_ref, own_ref, got_ref, out_ref):
    rows = own_ref.shape[0]
    mine = (where_ref[3] >> bit) & 1
    out_ref[pl.ds(pl.multiple_of(mine * rows, 16), rows)] = own_ref[...]
    out_ref[pl.ds(pl.multiple_of((1 - mine) * rows, 16), rows)] = got_ref[...]


def last_join_kernel(part, where_ref, own_ref, got_ref, later_ref, out_ref, sent_ref):
    join_kernel(0, where_ref, own_ref, got_ref, out_ref)
    rows = out_ref.shape[0]
    later = later_ref[part * rows : (part + 1) * rows]
    sent_ref[...] = jnp.where(where_ref[0] == 0, later, out_ref[...])


def results_kernel(kind, where_ref, *refs):
    *pieces, first_ref, second_ref, buffer, sems = refs
    copies = Copies(sems)
    first = where_ref[0] == 0
    rows = buffer.shape[1]
    half = rows // 2
    count = len(pieces) // 2
    size = rows // count

    def piece(refs, part):
        at = part * half
        return refs[at // size][at % size : at % size + half]

    for side in range(2):
        for part in range(2):
            at = slice(part * half, (part + 1) * half)
            ours, got = piece(pieces[:count], part), piece(pieces[count : 2 * count], part)
            values = jnp.where(first, ours, got) if side == 0 else jnp.where(first, got, pieces[-1][at])
            buffer[side, at] = values.astype(F32)
            if kind == "ffn":
                target = (first_ref, second_ref)[side].at[pl.ds(part * half, half)]
            else:
                k = 2 * side + part
                target = first_ref.at[k] if k < 3 else second_ref
            copies.start(buffer.at[side, pl.ds(part * half, half)], target)
    copies.done()


def results(kind, where, pieces):
    rows, columns = pieces[-1].shape
    if kind == "attn":
        outs = [shape((3, rows // 2, columns), F32), shape((rows // 2, columns), F32)]
    else:
        outs = [shape((rows, columns), F32)] * 2
    return call(
        partial(results_kernel, kind),
        [("h", item) for item in outs],
        [("s", where)] + [("v", item) for item in pieces],
        us=2.5,
        scratch=[pltpu.VMEM((2, rows, columns), F32)],
        copies=4,
    )


def pick_kernel(where_ref, first_in, second_in, out_ref, sems):
    copies = Copies(sems)
    first = where_ref[0] == 0
    copies.start_one([(first, second_in), (jnp.logical_not(first), first_in)], out_ref)
    copies.done()


def place_kernel(where_ref, first_in, second_in, got_ref, out_ref, buffer, sems):
    section = where_ref[0]
    copies = Copies(sems)
    copies.start_one([(section == 0, first_in), (section == 1, second_in)], buffer.at[section])
    buffer[1 - section] = got_ref[...]
    copies.done()
    out = Copies([sems.at[1]])
    out.start(buffer, out_ref.at[0])
    out.done()


def grad_in_kernel(where_ref, own_ref, far_ref, skip_ref, later_in, sent_ref, out_copy, later, out, sems):
    copies = Copies(sems)
    copies.start(later_in, later)
    grad = (own_ref[...] + far_ref[...].astype(F32) + skip_ref[...]).astype(BF16)
    out[...] = grad
    copies.start(out, out_copy)
    copies.done()
    sent_ref[...] = jnp.where(where_ref[0] == 0, later[...], grad)


def pack_sums_kernel(where_ref, *refs):
    own_ref, pair_ref = refs[-2:]
    for layer in range(2):
        norm1_ref, norm2_ref, up0_ref, up1_ref, qkv_ref = refs[5 * layer : 5 * layer + 5]
        at = 8 * layer
        for row, source in (
            (GAIN1, norm1_ref[0:1]),
            (GAIN2, norm2_ref[0:1]),
            (BIAS_OUT, norm1_ref[2:3]),
            (SHIFT1, norm1_ref[1:2]),
            (BIAS2, norm2_ref[2:3]),
            (SHIFT2, norm2_ref[1:2]),
            (7, qkv_ref[0:1]),
        ):
            own_ref[at + row : at + row + 1] = source
            pair_ref[at + row : at + row + 1] = source
        own_ref[at + 6 : at + 7] = up0_ref[0:1] + up1_ref[0:1]
        pair_ref[at + 6 : at + 7] = up0_ref[1:2] + up1_ref[1:2]


def small_add_kernel(where_ref, own_ref, got_ref, total_ref, shared_ref):
    total = own_ref[...] + got_ref[...]
    total_ref[...] = total
    row = lax.broadcasted_iota(jnp.int32, total.shape, 0)
    shared_ref[...] = jnp.where(row % 8 < BIAS_UP, total, 0.0)


def small_results_kernel(where_ref, own_ref, got_ref, *refs):
    outs, (gains, shifts, up, qkv_b), sems = refs[:4], refs[4:8], refs[8]
    total = own_ref[...] + got_ref[...]
    total = jnp.where(where_ref[0] == 0, total[:8], total[8:])
    gains[0] = total[0:2]
    shifts[0] = total[2:6]
    up[...] = total[6:7]
    local = qkv_b.shape[2]
    for k in range(2):
        both = total[7:8, 2 * k * local : 2 * (k + 1) * local]
        qkv_b[0, k : k + 1] = jnp.where(where_ref[1] == 0, both[:, :local], both[:, local:])
    copies = Copies(sems)
    for source, target in zip((gains, shifts, up, qkv_b), outs):
        copies.start(source, target)
    copies.done()


def swap(value, axis, bit):
    count = lax.axis_size(axis)
    return lax.ppermute(value, axis, [(source, source ^ bit) for source in range(count)])


def core_swap(value):
    return swap(value, "tensor", 1)


def chip_swap(value):
    return swap(value, "tensor", 2)


def tie(value, *after):
    return lax.optimization_barrier((value, *after))[0]


class Sum:
    def __init__(self, *pieces):
        self.sent, self.later = None, None
        self.kept = [kept for _, kept in pieces]
        self.got = [swap(sent, "pipe", 1) for sent, _ in pieces]
        count = lax.axis_size("dp")
        self.bits = count.bit_length() - 1
        self.halving = count == 1 << self.bits and self.kept[0].shape[0] % (16 * count) == 0

    def add(self, where):
        rows, columns = self.kept[0].shape
        (self.total,) = call(
            add_kernel,
            [("v", shape((rows * len(self.kept), columns)))],
            [("s", where)] + [("v", item) for item in (*self.kept, *self.got)],
        )
        return self.total

    def whole(self, where, *after):
        total = self.add(where)
        self.total = lax.psum(tie(total, *after), "dp")
        return total

    def halve(self, bit, where):
        parts = len(self.kept)
        rows, columns = self.kept[0].shape
        dims = (rows * parts // 2, columns)
        sent, kept = call(
            partial(halve_sum_kernel, bit, parts),
            [("v", shape(dims)), ("v", shape(dims, F32))],
            [("s", where)] + [("v", item) for item in (*self.kept, *self.got)],
        )
        self.kept, self.got = [kept], [swap(sent, "dp", 1 << bit)]
        return sent

    def join(self, bit, where):
        rows, columns = self.total.shape
        got = swap(self.total, "dp", 1 << bit)
        if bit or self.later is None:
            (self.total,) = call(
                partial(join_kernel, bit),
                [("v", shape((2 * rows, columns)))],
                [("s", where), ("v", self.total), ("v", got)],
            )
            return self.total
        later, part = self.later
        self.total, self.sent = call(
            partial(last_join_kernel, part),
            [("v", shape((2 * rows, columns)))] * 2,
            [("s", where), ("v", self.total), ("v", got), ("v", later.total)],
        )
        return self.total

    def steps(self):
        if not self.halving:
            return [self.whole]
        bits = range(self.bits)
        return (
            [partial(self.halve, bit) for bit in bits]
            + [self.add]
            + [partial(self.join, bit) for bit in reversed(bits)]
        )

    def finish(self):
        if self.sent is None:
            later, part = self.later
            rows = self.total.shape[0]
            piece = later.total[part * rows : (part + 1) * rows]
            self.sent = jnp.where(lax.axis_index("pipe") == 0, piece, self.total)
        self.other = swap(self.sent, "pipe", 1)


def layer_forward(layer, own_in, far_in, w_qkv, small, marks, where, hooks, upstream=None):
    own_q, own_kv, own_x_kept, own_q_kept = qkv(own_in, w_qkv, small)
    own_pair = core_swap(own_kv)
    far_q, far_kv, far_x_kept, far_q_kept = qkv(far_in, w_qkv, small)
    far_pair = core_swap(far_kv)
    w_out = hooks["out"](far_q)
    far_out, kv, kv_kept, far_o, far_lse = attn(
        layer, where, far_q, (own_kv, own_pair, far_kv, far_pair), marks, w_out
    )
    far_sent = far_out
    far_out = chip_swap(far_out)
    own_out, own_o, own_lse = attn(layer, where, own_q, (kv,), marks, w_out)
    own_h, hidden, resid1, own_h_kept = norm1(own_in, own_out, far_out, small)
    far_h = chip_swap(own_h)
    w_up, w_down = hooks["ffn"](far_sent, own_h)
    own_branch, own_act, own_slope = ffn(own_h, w_up, w_down, small, False)
    far_h = tie(far_h, own_branch)
    far_branch, far_act, far_slope, far_h_kept = ffn(far_h, w_up, w_down, small, True)
    own_branch = tie(own_branch, *hooks["next"](far_branch))
    branch = (hidden, own_branch, chip_swap(far_branch))
    turned = None
    if upstream is None:
        output, resid2, output_kept = norm2(*branch, small)
    else:
        *turned, output_kept = turn(*branch, upstream, small)
        output, resid2 = None, None
    kept = dict(
        x=(own_x_kept, far_x_kept),
        q=(own_q_kept, far_q_kept),
        kv=kv_kept,
        lse=(own_lse, far_lse),
        o=(own_o, far_o),
        resid=(resid1, resid2),
        turned=turned,
        weights=(w_qkv, w_out, w_up, w_down),
        h=(own_h_kept, far_h_kept),
        act=(own_act, far_act),
        slope=(own_slope, far_slope),
    )
    return output, output_kept, kept


def layer_backward(layer, upstream, kept, small, marks, where, hooks):
    if kept["turned"] is None:
        own_df, skip2, norm2_sums, *grad_in = norm2_back(upstream, kept["resid"][1], small)
    else:
        (own_df, skip2, norm2_sums), grad_in = kept["turned"], []
    far_df = chip_swap(own_df)
    w_qkv, w_out, w_up, w_down = kept["weights"]
    own_slope, far_slope = load(layer, tie(where, own_df), [], kept["slope"])
    own_dh, own_du, own_db = ffn_back(own_df, own_slope, w_up, w_down, False)
    far_df = tie(far_df, own_dh, *hooks["df"](own_dh))
    far_dh, far_du, far_db = ffn_back(far_df, far_slope, w_up, w_down, True)
    names = ("act", "h", "q", "lse", "x", "o")
    kv, *rows = load(
        layer,
        tie(where, far_dh, *hooks["dh"](far_dh)),
        [],
        [kept["kv"]] + [item for name in names for item in kept[name]],
    )
    own_act, far_act, own_h, far_h, own_q, far_q, own_lse, far_lse, own_x, far_x, own_o, far_o = rows
    grads = (own_h, far_h, own_act, far_act, own_df, far_df, own_du, far_du)
    pair = ffn_pair(grads)
    got = [core_swap(item) for item in pair]
    own_dh = tie(own_dh, pair[0], *hooks["norm"](pair[0]))
    own_dz, skip1, norm1_sums = norm1_back(own_dh, chip_swap(far_dh), skip2, kept["resid"][0], small)
    far_dz = chip_swap(own_dz)
    parts = ffn_own(tie(where, own_dz), grads, got)
    own_dq, own_dkv, own_send = attn_back(
        layer, 0, tie(where, parts[0]), own_dz, own_q, kv, marks, own_lse, w_out
    )
    own_pair = core_swap(own_send)
    far_dz = tie(far_dz, own_send, *hooks["dz"](own_send, parts))
    far_dq, far_dkv, far_send = attn_back(layer, 1, where, far_dz, far_q, kv, marks, far_lse, w_out)
    far_pair = core_swap(tie(far_send, *hooks["send"](far_send)))
    far_dx, own_d, far_d = row_grads(
        small, (own_dq, far_dq), (own_dkv, far_dkv), (own_pair, far_pair), w_qkv
    )
    own_dx, attn_own, attn_pair, qkv_sums = attn_grads(
        tie(where, far_dx, *hooks["dx"](far_dx)),
        (own_d, far_d),
        (own_x, far_x),
        (own_o, far_o),
        (own_dz, far_dz),
        w_qkv,
    )
    far_dx = chip_swap(far_dx)
    sums = (norm1_sums, norm2_sums, own_db, far_db, qkv_sums)
    return (own_dx, far_dx, skip1), grad_in, sums, (attn_own, core_swap(attn_pair))


def body(
    tokens,
    segment_ids,
    pad_mask,
    block_perm,
    qkv_weight,
    qkv_bias,
    out_weight,
    up_weight,
    up_bias,
    down_weight,
    norm_gain,
    shift_bias,
    cotangent,
):
    section = lax.axis_index("pipe")
    place = lax.axis_index("tensor")
    replica = lax.axis_index("dp")
    paired = lax.axis_size("dp") % 2 == 0
    width = tokens.shape[2]
    local = qkv_bias.shape[2]
    here = jnp.stack([section, place % 2, replica % 2, replica, place]).astype(jnp.int32)
    qkv_rows = jnp.transpose(qkv_weight[0], (0, 2, 1))

    def other_half(half, whole):
        if paired:
            return swap(half, "dp", 1)
        even = replica % 2 == 0
        rest = jnp.where(even, whole[..., width // 2 :], whole[..., : width // 2])
        return swap(rest, "pipe", 1)

    (qkv_half,) = halves_of(here, qkv_rows)
    qkv_x = swap(qkv_half, "pipe", 1)
    rows = lax.optimization_barrier(lax.dynamic_index_in_dim(tokens, section, 0, keepdims=False))
    far_rows = chip_swap(rows)
    (own_small,) = call(
        pack_kernel,
        [("v", shape((16, width), F32))],
        [("h", norm_gain), ("h", shift_bias), ("h", up_bias), ("h", qkv_bias), ("s", block_perm)],
        scratch=[
            pltpu.VMEM(item.shape, item.dtype) for item in (norm_gain, shift_bias, up_bias, qkv_bias)
        ],
        copies=4,
    )
    other_small = swap(own_small, "pipe", 1)
    up_half, down_half = halves_of(tie(here, own_small, qkv_half), up_weight, down_weight)
    up_x = swap(up_half, "pipe", 1)
    out_x = swap(tie(out_weight, qkv_x), "pipe", 1)
    (marks,) = call(
        marks_kernel,
        [("v", shape((8, segment_ids.shape[1] // 2), jnp.int32))],
        [("s", tie(here, up_x)), ("v", segment_ids), ("v", pad_mask)],
    )
    *smalls, flags = call(
        params_kernel,
        [("v", shape((16, width), F32))] * 2 + [("h", shape((8, PAIR), F32))],
        [("s", here)]
        + [
            ("v", item)
            for item in (own_small, other_small, core_swap(own_small), core_swap(other_small))
        ],
        scratch=[pltpu.VMEM((8, PAIR), F32)],
        copies=1,
    )
    heads = 2 * block_perm.shape[1]
    where = jnp.concatenate([here, flags[:2, :heads].reshape(-1).astype(jnp.int32)])
    def item(by_core, own, other, after=(), later=()):
        pair_own = core_swap(tie(own, *after) if after else own)
        pair_other = tuple(core_swap(tie(part, *later) if later else part) for part in other)
        return by_core, own, other, pair_own, pair_other

    other_qkv = other_half(tie(qkv_x, up_half, other_small, far_rows), qkv_rows)
    items = dict(qkv=item(True, qkv_rows, (qkv_x, other_qkv)))
    (first_qkv,) = load(0, tie(where, marks, *smalls, far_rows, up_x), [items["qkv"]])

    def first_out(after):
        fetched["down"] = swap(tie(down_half, up_x), "pipe", 1)
        fetched["up"] = other_half(tie(up_x, marks), up_weight)
        items["out"] = item(True, out_weight, (out_x,), (first_qkv,), (first_qkv,))
        return load(0, tie(where, after), [items["out"]])[0]

    fetched = {}

    def first_ffn(early, after):
        down_x = fetched["down"]
        other_down = other_half(tie(down_x, early), down_weight)
        items["up"] = item(False, up_weight, (up_x, fetched["up"]), (early,), (early,))
        items["down"] = item(False, down_weight, (down_x, other_down), (early,), (after,))
        return load_ffn(0, (), tie(where, after))

    def load_ffn(layer, arrays, after):
        return load(layer, after, [items["up"], items["down"]], arrays)

    second = []

    def load_second(after):
        second.extend(load(1, tie(where, after), [items["qkv"], items["out"]]))
        return second

    out_first, first_kept, kept_first = layer_forward(
        0,
        rows,
        far_rows,
        first_qkv,
        smalls[0],
        marks,
        where,
        {"out": first_out, "ffn": first_ffn, "next": load_second},
    )
    def second_ffn(early, after):
        return load_ffn(1, (), tie(where, after))

    upstream = lax.dynamic_index_in_dim(cotangent, section, 0, keepdims=False)
    _, second_kept, kept_second = layer_forward(
        1,
        out_first,
        chip_swap(out_first),
        second[0],
        smalls[1],
        marks,
        where,
        {
            "out": lambda after: second[1],
            "ffn": second_ffn,
            "next": lambda after: (),
        },
        upstream,
    )

    def place_outputs(first, second, got, after):
        return call(
            place_kernel,
            [("h", shape((1, 2) + first.shape))],
            [("s", after), ("h", first), ("h", second), ("v", got)],
            us=1.5,
            scratch=[pltpu.VMEM((2,) + first.shape, BF16)],
            copies=2,
        )[0]

    sums, steps = {}, {}

    def begin(name, *pieces):
        sums[name] = Sum(*pieces)
        steps[name] = sums[name].steps()

    def run(after, *names):
        for name in names:
            if steps[name]:
                after = steps[name].pop(0)(tie(where, after))
        return after

    outputs = []

    def nothing(*_):
        return ()

    def later_df(after):
        (picked,) = call(
            pick_kernel,
            [("v", shape(rows.shape))],
            [("s", tie(where, after)), ("h", first_kept), ("h", second_kept)],
            copies=1,
        )
        outputs.append(swap(picked, "pipe", 1))
        return (picked,)

    def later_dz(after, parts):
        begin("ab1", parts[0:2], parts[2:4])
        return outputs

    grads, _, small_second, attn_second = layer_backward(
        1,
        None,
        kept_second,
        smalls[1],
        marks,
        where,
        {
            "df": later_df,
            "dh": nothing,
            "norm": nothing,
            "dz": later_dz,
            "send": lambda after: sums["ab1"].got[:1],
            "dx": nothing,
        },
    )

    def first_df(after):
        sent, kept = split(tie(where, after), *attn_second)
        begin("c1", (sent, kept))
        return (run(sent, "ab1"),)

    def first_dz(after, parts):
        begin("a0", parts[0:2])
        begin("b0", parts[2:4])
        return (run(after, "ab1", "c1"),)

    def first_send(after):
        return (run(after, "ab1", "c1", "a0"),)

    def first_dx(after):
        return (run(after, "c1", "a0", "b0"),)

    grads, (grad_second,), small_first, attn_first = layer_backward(
        0,
        grads,
        kept_first,
        smalls[0],
        marks,
        where,
        {
            "df": first_df,
            "dh": nothing,
            "norm": lambda after: (run(after, "ab1"),),
            "dz": first_dz,
            "send": first_send,
            "dx": nothing,
        },
    )
    last = [attn_first[0]]

    def now():
        return tie(where, *last)

    def then(*values):
        last[:] = values

    def step(*names):
        then(run(last[-1], *names))

    def small_add(total, got):
        total, shared = call(
            small_add_kernel,
            [("v", shape((16, width), F32))] * 2,
            [("s", now()), ("v", total), ("v", got)],
        )
        then(total)
        return total, shared

    hops = [("pipe", 1)]
    count = lax.axis_size("dp")
    if not count & (count - 1):
        hops += [("dp", 1 << bit) for bit in range(count.bit_length() - 1)]
    total, pair_sums = call(
        pack_sums_kernel,
        [("v", shape((16, width), F32))] * 2,
        [("s", now())] + [("v", value) for value in (*small_first, *small_second)],
    )
    then(total)
    got = core_swap(pair_sums)
    sent, kept = split(now(), *attn_first)
    then(sent)
    begin("c0", (sent, kept))
    step("c1", "a0", "b0", "c0")
    total, shared = small_add(total, got)
    got = chip_swap(shared)
    step("a0", "b0", "c1", "ab1")
    total, _ = small_add(total, got)
    if len(hops) == 1:
        total = lax.psum(total, "dp")
    got = swap(total, *hops[0])
    sent, grad_first = call(
        grad_in_kernel,
        [("v", shape(rows.shape)), ("h", shape(rows.shape))],
        [("s", now())] + [("v", value) for value in grads] + [("h", grad_second)],
        scratch=[pltpu.VMEM(rows.shape, BF16)] * 2,
        copies=2,
    )
    then(sent)
    grad_got = swap(sent, "pipe", 1)
    step("a0", "c0", "b0")
    while steps["c1"]:
        step("c1")
    then(last[-1], grad_got)

    def last_of(*names):
        for name in names:
            while steps[name]:
                step(name)

    def finish(name, later, part):
        sums[name].later = (sums[later], part)
        last_of(name)
        sums[name].finish()

    for at, hop in enumerate(hops[1:]):
        total, _ = small_add(total, got)
        got = swap(total, *hop)
        if at == 0:
            last_of("ab1")
            finish("a0", "ab1", 0)
            step("c0", "b0")
        elif at == 1:
            step("c0")
            finish("b0", "ab1", 1)
    if len(hops) < 2:
        last_of("ab1")
        finish("a0", "ab1", 0)
    if len(hops) < 3:
        finish("b0", "ab1", 1)
    then(last[-1], sums["a0"].other)
    input_grad = place_outputs(grad_first, grad_second, grad_got, now())
    layer_out = place_outputs(first_kept, second_kept, outputs[0], tie(where, input_grad))
    then(layer_out)
    outs = [shape(item.shape, F32) for item in (norm_gain, shift_bias, up_bias, qkv_bias)]
    gains, shifts, upb, qkvb = call(
        small_results_kernel,
        [("h", item) for item in outs],
        [("s", now()), ("v", total), ("v", got)],
        scratch=[pltpu.VMEM(item.shape, F32) for item in outs],
        copies=4,
    )
    then(gains)
    finish("c0", "c1", 0)

    def pieces(later, *names):
        return [
            *(sums[name].total for name in names),
            *(sums[name].other for name in names),
            sums[later].total,
        ]

    upw, downw = results("ffn", now(), pieces("ab1", "a0", "b0"))
    qkvw, outw = results("attn", tie(where, upw), pieces("c1", "c0"))
    qkvw = jnp.transpose(qkvw, (0, 2, 1))
    return (
        layer_out,
        input_grad,
        qkvw[None],
        qkvb,
        outw[None],
        upw[None],
        upb,
        downw[None],
        gains,
        shifts,
    )


def solution(mesh):
    return jax.shard_map(
        body,
        mesh=mesh,
        in_specs=(
            P("dp", "tensor", None),
            P("dp", None),
            P("dp", None),
            P("pipe", "tensor", None),
            P("pipe", None, None, "tensor"),
            P("pipe", None, "tensor"),
            P("pipe", "tensor", None),
            P("pipe", None, "tensor"),
            P("pipe", "tensor"),
            P("pipe", "tensor", None),
            P("pipe", None, None),
            P("pipe", None, None),
            P("dp", "tensor", None),
        ),
        out_specs=(
            P("pipe", "dp", "tensor", None),
            P("pipe", "dp", "tensor", None),
            P("pipe", None, None, "tensor"),
            P("pipe", None, "tensor"),
            P("pipe", "tensor", None),
            P("pipe", None, "tensor"),
            P("pipe", "tensor"),
            P("pipe", "tensor", None),
            P("pipe", None, None),
            P("pipe", None, None),
        ),
        check_vma=False,
    )
```
